128 devices in a mesh: tx: 8 (over y, core), ty: 16 (over z, x).
Axes of the slice: x: 4, y: 4, z: 4, core: 2. Of those that a mesh axis runs over, the one named last changes fastest.
Arguments:
- right_side: float32 [16, 256, 2048], P(None, 'tx', 'ty'), may hold values from -4 to 4
- screening: float32 [16, 256, 2048], P(None, 'tx', 'ty'), may hold values from 0.001 to 0.3
- owners: int32 [8, 16], P('tx'), may hold values from 0 to 15, as said below
Outputs:
- solution_field: float32 [16, 256, 2048], P(None, 'tx', 'ty')
- residual: float32 [16, 256, 2048], P(None, 'tx', 'ty')
The draws below stay inside these ranges and needn't reach their ends.
Inputs may be any that keep to these rules, and one draw needn't show every extreme that they name: In each tile row the tile columns fall into runs of consecutive columns, each of 1 to 4 columns, the first run of every row holding exactly 4. All tiles of a run have the same entry of owners, and different runs of one row have different entries.
All inputs are finite; a program needn't handle non-finite values.
Results may differ from the reference program's by a relative error of at most 0.0003.
Values sent between devices are 32-bit elements; how exact they have to be, the bound alone decides.
A program may use at most 128 MiB of HBM per device.

```python
import math
import jax
import jax.numpy as jnp

CX = 32
CY = 128
NZ = 16
ITERS = 2
LEVELS = 4
NU = 3
CS = 8
MOST = 4
NX = 256
NY = 2048
N_TX = 8
N_TY = 16


def draw_right_side(key, part):
    key = jax.random.fold_in(key, 5)
    return jnp.clip(jax.random.normal(key, (NZ, NX, NY), jnp.float32), -4.0, 4.0)


def draw_owners(key, part):
    key = jax.random.fold_in(key, 9)
    length_key, shift_key = jax.random.split(key)
    run_lengths = jax.random.randint(length_key, (N_TX, N_TY), 1, MOST + 1)
    leading = jnp.arange(N_TY)[None, :] == 0
    run_lengths = jnp.where(leading, MOST, run_lengths)
    starts = jnp.cumsum(run_lengths, axis=1) - run_lengths
    places = jnp.arange(N_TY)
    covered = starts[:, None, :] <= places[None, :, None]
    begins = jnp.max(jnp.where(covered, starts[:, None, :], 0), axis=2)
    shifts = jax.random.randint(shift_key, (N_TX,), 0, N_TY)
    rows = jnp.arange(N_TX)
    shifts = jnp.where(rows == 0, N_TY // 2, jnp.where(rows == 1, 1, jnp.where(rows == 2, 0, shifts)))
    return ((begins + shifts[:, None]) % N_TY).astype(jnp.int32)


def block_scale(rng, extent, cuts, low, high):
    loudness, own = 1.0, jax.random.fold_in(rng, 6)
    for position, parts in cuts:
        steps = jnp.exp(jax.random.uniform(jax.random.fold_in(own, position), (parts,), jnp.float32, low / len(cuts), high / len(cuts)))
        loudness = loudness * jnp.repeat(steps, extent[position] // parts).reshape([-1 if axis == position else 1 for axis in range(len(extent))])
    return loudness


def setup_inputs(seed: int = 0) -> dict:
    seeds = jax.random.split(jax.random.key(seed), 4)
    right_side = draw_right_side(jax.random.fold_in(seeds[3], 71), 0)
    screening = jnp.clip(jnp.exp(math.log(0.3) - 5.7037825 * jax.random.uniform(seeds[1], (NZ, NX, NY), jnp.float32) ** block_scale(seeds[1], (NZ, NX, NY), ((1, 8), (2, 16)), -0.2, 0.2)), 0.001, 0.3)
    owners = draw_owners(jax.random.fold_in(seeds[3], 71), 0)
    return dict(right_side=right_side, screening=screening, owners=owners)


OMEGA = 0.8


def restrict(values):
    depth, row_count, columns = values.shape
    blocks = values.reshape(depth // 2, 2, row_count // 2, 2, columns // 2, 2)
    return jnp.sum(blocks, axis=(1, 3, 5)) * 0.125


def prolong(values):
    return jnp.repeat(jnp.repeat(jnp.repeat(values, 2, axis=0), 2, axis=1), 2, axis=2)


def neighbours(values):
    padded = jnp.pad(values, 1)
    summed = padded[2:, 1:-1, 1:-1] + padded[:-2, 1:-1, 1:-1]
    summed = summed + padded[1:-1, 2:, 1:-1] + padded[1:-1, :-2, 1:-1]
    return summed + padded[1:-1, 1:-1, 2:] + padded[1:-1, 1:-1, :-2]


def linked_neighbours(values, row_links, column_links):
    depth_padded = jnp.pad(values, ((1, 1), (0, 0), (0, 0)))
    summed = depth_padded[2:] + depth_padded[:-2]
    forward = values[:, 1:, :] * row_links[None, :, None]
    backward = values[:, :-1, :] * row_links[None, :, None]
    summed = summed + jnp.pad(forward, ((0, 0), (0, 1), (0, 0))) + jnp.pad(backward, ((0, 0), (1, 0), (0, 0)))
    forward = values[:, :, 1:] * column_links[None]
    backward = values[:, :, :-1] * column_links[None]
    return summed + jnp.pad(forward, ((0, 0), (0, 0), (0, 1))) + jnp.pad(backward, ((0, 0), (0, 0), (1, 0)))


def vcycle(source, screens, row_links, column_links, depth_level, coupling):
    screen = screens[depth_level]
    diagonal = screen + 6.0 * coupling
    if depth_level == LEVELS - 1:
        values = jnp.zeros_like(source)
        for counter in range(CS):
            nearby = linked_neighbours(values, row_links, column_links)
            values = values + OMEGA * (source - (diagonal * values - coupling * nearby)) / diagonal
        return values
    values = OMEGA * source / diagonal
    for counter in range(NU - 1):
        values = values + OMEGA * (source - (diagonal * values - coupling * neighbours(values))) / diagonal
    defect = source - (diagonal * values - coupling * neighbours(values))
    values = values + prolong(vcycle(restrict(defect), screens, row_links, column_links, depth_level + 1, 0.5 * coupling))
    for counter in range(NU):
        values = values + OMEGA * (source - (diagonal * values - coupling * neighbours(values))) / diagonal
    return values


def reference(right_side, screening, owners):
    screens = [screening]
    for counter in range(LEVELS - 1):
        screens.append(restrict(screens[-1]))
    shrink = 2 ** (LEVELS - 1)
    coarse_rows = CX // shrink
    coarse_cols = CY // shrink
    total_rows = coarse_rows * N_TX
    total_cols = coarse_cols * N_TY
    row_links = ((jnp.arange(total_rows - 1) + 1) % coarse_rows != 0).astype(jnp.float32)
    tile_row = (jnp.arange(total_rows) // coarse_rows).astype(jnp.int32)
    tile_col = (jnp.arange(total_cols) // coarse_cols).astype(jnp.int32)
    run_ids = owners[tile_row][:, tile_col]
    column_links = (run_ids[:, 1:] == run_ids[:, :-1]).astype(jnp.float32)

    solution_field = jnp.zeros_like(right_side)
    residual = right_side
    precond = vcycle(residual, screens, row_links, column_links, 0, 1.0)
    direction = precond
    inner_now = jnp.sum(residual * precond)
    for counter in range(ITERS):
        applied = (screening + 6.0) * direction - neighbours(direction)
        step_size = inner_now / jnp.sum(direction * applied)
        solution_field = solution_field + step_size * direction
        residual = residual - step_size * applied
        if counter + 1 < ITERS:
            precond = vcycle(residual, screens, row_links, column_links, 0, 1.0)
            inner_next = jnp.sum(residual * precond)
            direction = precond + (inner_next / inner_now) * direction
            inner_now = inner_next
    return solution_field, residual
```

```python
import functools

import jax
import jax.numpy as jnp
from jax import lax
from jax.experimental import pallas as pl
from jax.experimental.pallas import tpu as pltpu
from jax.sharding import PartitionSpec as P

MESH = pl.DeviceIdType.MESH
F32 = jnp.float32
BF16 = jnp.bfloat16

NTX, NTY = 8, 16
HALO = 11
ROWS = 56
TOP = 12
PLANE = ROWS * 16
PITCH = 24
R1 = 32
DIRS8 = [(a, b) for a in (-1, 0, 1) for b in (-1, 0, 1) if (a, b) != (0, 0)]
DIRS14 = [(a, b) for a in (-2, -1, 0, 1, 2) for b in (-1, 0, 1) if (a, b) != (0, 0)]


def iota(shape, axis):
    return lax.broadcasted_iota(jnp.int32, shape, axis)


def dot_split(x, table):
    high = x.astype(BF16)
    low = (x - high.astype(F32)).astype(BF16)
    return jnp.dot(high, table, preferred_element_type=F32) + jnp.dot(
        low, table, preferred_element_type=F32
    )


def kernel(
    rhs_ref, scr_ref, own_ref, sol_ref, res_ref,
    bs1, b2, gain, va, vb, vc, q1, pk1, pk2, rp1, rp2, ebuf, xbuf,
    l1s, l1g, l1b, l1x, l1v, l1w, l1e,
    m1ud, m1lr, m2ud, m2lr, rt1, rt2,
    l2b, l2s, l2g, l2v, l2w, l2e, l2x,
    t01, p10, t12, u2, t23, p32, p21,
    arbuf, arr1, arr2,
    s_r1, r_r1, s_r2, r_r2, s_ar, r_ar,
):
    tx = lax.axis_index("tx")
    ty = lax.axis_index("ty")
    zero = lax.div(tx, 64)
    barrier = pltpu.get_barrier_semaphore()

    def inside(dx, dy):
        a, b = tx + dx, ty + dy
        return (a >= 0) & (a < NTX) & (b >= 0) & (b < NTY)

    def at(dx, dy):
        return {"tx": tx + dx, "ty": ty + dy}

    def ring(dx, dy):
        return {"tx": lax.rem(tx + dx, NTX), "ty": lax.rem(ty + dy, NTY)}

    ring_dirs = [(k, 0) for k in range(1, NTX)] + [(0, k) for k in range(1, NTY)]
    extra = [d for d in DIRS14 if d[0] != 0 and d[1] != 0]
    expected = jnp.int32(len(ring_dirs))
    for d in ring_dirs:
        pl.semaphore_signal(barrier, inc=1, device_id=ring(*d), device_id_type=MESH)
    for d in extra:
        ok = inside(*d)
        expected = expected + ok.astype(jnp.int32)

        @pl.when(ok)
        def _():
            pl.semaphore_signal(barrier, inc=1, device_id=at(*d), device_id_type=MESH)

    lane16 = iota((16, 128), 1)
    lane8 = iota((8, 128), 1)
    sub8 = iota((8, 128), 0)
    grp16 = lane16 >> 4
    grp8 = lane8 >> 4
    first16, last16 = lane16 == 0, lane16 == 127
    edge16 = (lane16 < 16) | (lane16 >= 112)
    side8 = ((lane8 >= 16) & (lane8 < 32)) | ((lane8 >= 96) & (lane8 < 112))
    z16 = jnp.zeros((16, 128), F32)
    z8 = jnp.zeros((8, 128), F32)

    def vrow(t, r):
        return pl.multiple_of(8 + (t * ROWS + r) * PITCH, 8)

    def brow(t, r):
        return pl.multiple_of((t * ROWS + r) * 16, 16)

    for z in range(16):
        for k in range(4):
            start = (TOP + 8 * k) * 16 + z
            bs1[0, pl.ds(start, 8, stride=16), :] = rhs_ref[z, 8 * k : 8 * k + 8, :]
            bs1[1, pl.ds(start, 8, stride=16), :] = scr_ref[z, 8 * k : 8 * k + 8, :]

    def pack0(src, count, pk):
        def body(j, c):
            for a in range(count):
                left, right = z16, z16
                for g in range(8):
                    x = src[a, pl.ds(brow(0, TOP + j * 8 + g), 16), :]
                    x = pltpu.roll(x, (16 * (g + 1)) % 128, 1)
                    right = jnp.where(grp16 == g, x, right)
                    left = jnp.where(grp16 == (g + 1) % 8, x, left)
                dst = pl.ds(pl.multiple_of(j * 16, 16), 16)
                pk[0, a, dst, :] = left
                pk[1, a, dst, :] = right
            return c

        lax.fori_loop(0, 4, body, 0)

    def unpack0(dst, count, rp, mask):
        def rows(dxi, j, groups):
            for a in range(count):
                span = pl.ds(pl.multiple_of(j * 16, 16), 16)
                fl = rp[dxi, 0, a, span, :]
                fr = rp[dxi, 1, a, span, :]
                for g in groups:
                    x = jnp.where(grp16 == g, fl, fr)
                    x = pltpu.roll(x, (128 - 16 * (g + 1)) % 128, 1)
                    if mask:
                        x = jnp.where(edge16, x, 0.0)
                    r = TOP + (dxi - 1) * 32 + j * 8 + g
                    dst[a, pl.ds(brow(1, r), 16), :] = x

        def body(j, c):
            rows(1, j, range(8))
            return c

        lax.fori_loop(0, 4, body, 0)
        rows(0, 2, range(5, 8))
        rows(0, 3, range(8))
        rows(2, 0, range(8))
        rows(2, 1, range(3))

    def r1_copy(i, d, src, pk, rp, cyc):
        dx, dy = d
        if dy == 0:
            if dx == -1:
                a, b = TOP, TOP + 32
            else:
                a, b = TOP + 32 - HALO, TOP - HALO
            s = src.at[:, pl.ds(a * 16, HALO * 16)]
            t = src.at[:, pl.ds(b * 16, HALO * 16)]
        else:
            side = 0 if dy == -1 else 1
            if dx == 0:
                s, t = pk.at[side], rp.at[1, 1 - side]
            elif dx == -1:
                s, t = pk.at[side, :, pl.ds(0, 32)], rp.at[2, 1 - side, :, pl.ds(0, 32)]
            else:
                s, t = pk.at[side, :, pl.ds(32, 32)], rp.at[0, 1 - side, :, pl.ds(32, 32)]
        return pltpu.make_async_remote_copy(
            src_ref=s, dst_ref=t, send_sem=s_r1.at[cyc, i], recv_sem=r_r1.at[cyc, i],
            device_id=at(*d), device_id_type=MESH,
        )

    def start_r1(src, pk, rp, cyc):
        for i, d in enumerate(DIRS8):
            @pl.when(inside(*d))
            def _():
                r1_copy(i, d, src, pk, rp, cyc).start()

    def wait_r1(src, pk, rp, cyc):
        for i, d in enumerate(DIRS8):
            @pl.when(inside(-d[0], -d[1]))
            def _():
                r1_copy(i, d, src, pk, rp, cyc).wait_recv()

    def sent_r1(src, pk, rp, cyc):
        for i, d in enumerate(DIRS8):
            @pl.when(inside(*d))
            def _():
                r1_copy(i, d, src, pk, rp, cyc).wait_send()

    def clear_r1(src, count, rp):
        for a in range(count):
            for t in (0, 1):
                for r in (0, ROWS - 1):
                    src[a, pl.ds(brow(t, r), 16), :] = z16
        for dx, r in ((-1, TOP - HALO), (1, TOP + 32)):
            @pl.when(jnp.logical_not(inside(dx, 0)))
            def _():
                for a in range(count):
                    src[a, pl.ds(r * 16, HALO * 16), :] = jnp.zeros((HALO * 16, 128), F32)
        for dxi in range(3):
            for sidei, dy in ((0, -1), (1, 1)):
                @pl.when(jnp.logical_not(inside(dxi - 1, dy)))
                def _():
                    rp[dxi, sidei] = jnp.zeros((count, 64, 128), F32)

    def r2_copy(i, d, mud, mlr, rt, cyc):
        dx, dy = d
        ns = 2 - cyc
        if dy == 0:
            n = (6 + ns - cyc) if abs(dx) == 1 else ns
            s = mud.at[0 if dx < 0 else 1, pl.ds(0, n)]
        else:
            n = (2 + ns) if abs(dx) <= 1 else ns
            s = mlr.at[0 if dy < 0 else 1, pl.ds(0, n)]
        return pltpu.make_async_remote_copy(
            src_ref=s, dst_ref=rt.at[2 - dx, 1 - dy, pl.ds(0, n)],
            send_sem=s_r2.at[cyc, i], recv_sem=r_r2.at[cyc, i],
            device_id=at(*d), device_id_type=MESH,
        )

    def each_r2(op, mud, mlr, rt, cyc):
        for i, d in enumerate(DIRS14):
            @pl.when(inside(-d[0], -d[1]) if op == "wait_recv" else inside(*d))
            def _():
                getattr(r2_copy(i, d, mud, mlr, rt, cyc), op)()

    def clear_r2(rt):
        for dx, dy in DIRS14:
            @pl.when(jnp.logical_not(inside(dx, dy)))
            def _():
                rt[2 + dx, 1 + dy] = jnp.zeros((8, 8, 128), F32)

    def ar_copy(cyc, i):
        if i < 7:
            d, s, t = ring(i + 1, 0), arbuf.at[cyc, 0], arr1.at[cyc, i]
        else:
            d, s, t = ring(0, i - 6), arbuf.at[cyc, 1], arr2.at[cyc, i - 7]
        return pltpu.make_async_remote_copy(
            src_ref=s, dst_ref=t, send_sem=s_ar.at[cyc, i], recv_sem=r_ar.at[cyc, i],
            device_id=d, device_id_type=MESH,
        )

    def ar_begin(cyc, rows):
        out = z8
        for k, acc in enumerate(rows):
            out = jnp.where(sub8 == k, jnp.sum(acc, axis=0, keepdims=True), out)
        arbuf[cyc, 0] = out
        for i in range(7):
            ar_copy(cyc, i).start()

    def ar_middle(cyc):
        total = arbuf[cyc, 0]
        for i in range(7):
            ar_copy(cyc, i).wait_recv()
        for i in range(7):
            total = total + arr1[cyc, i]
        arbuf[cyc, 1] = total
        for i in range(7, 22):
            ar_copy(cyc, i).start()

    def ar_end(cyc, count):
        total = arbuf[cyc, 1]
        for i in range(7, 22):
            ar_copy(cyc, i).wait_recv()
        for i in range(15):
            total = total + arr2[cyc, i]
        sums = jnp.broadcast_to(jnp.sum(total, axis=1, keepdims=True), (8, 128))
        return [jnp.broadcast_to(sums[k : k + 1], (8, 128)) for k in range(count)]

    def stencil0(src, r, count, tiles, with_centre):
        rows = [
            [src[pl.ds(vrow(t, r + k - 1), 16), :] for k in range(count + 2)] for t in (0, 1)
        ]
        for k in range(count):
            c = [rows[0][k + 1], rows[1][k + 1]]
            left = [pltpu.roll(x, 1, 1) for x in c]
            right = [pltpu.roll(x, 127, 1) for x in c]
            for t in tiles:
                at_row = vrow(t, r + k)
                n = rows[t][k] + rows[t][k + 2]
                n = n + (src[pl.ds(at_row - 1, 16), :] + src[pl.ds(at_row + 1, 16), :])
                n = n + jnp.where(first16, left[1 - t], left[t])
                n = n + jnp.where(last16, right[1 - t], right[t])
                with_centre(k, t, c[t], n)

    def sweep0(src, dst, bref, r0, steps):
        def body(i, carry):
            r = r0 + 4 * i

            def put(k, t, c, n):
                row = pl.ds(brow(t, r + k), 16)
                dst[pl.ds(vrow(t, r + k), 16), :] = 0.2 * c + gain[row, :] * (bref[0, row, :] + n)

            stencil0(src, r, 4, (0, 1), put)
            return carry

        lax.fori_loop(0, steps, body, 0)

    def restrict0(out):
        for i in range(3):
            parts = []
            for t in (0, 1):
                parts.append(
                    ebuf[t, pl.ds(i * 128, 64, stride=2), :]
                    + ebuf[t, pl.ds(i * 128 + 1, 64, stride=2), :]
                )
            x = jnp.concatenate(parts, axis=1)
            out[pl.ds(32 + i * 64, 64), :] = dot_split(x, t01[...])

    def wrow(r):
        return pl.multiple_of(8 + r * 16, 8)

    def stencil1(src, r, count, put):
        rows = [src[pl.ds(wrow(r + k - 1), 8), :] for k in range(count + 2)]
        for k in range(count):
            c = rows[k + 1]
            n = rows[k] + rows[k + 2]
            n = n + (src[pl.ds(wrow(r + k) - 1, 8), :] + src[pl.ds(wrow(r + k) + 1, 8), :])
            n = n + (pltpu.roll(c, 1, 1) + pltpu.roll(c, 127, 1))
            put(k, c, n)

    def sweep1(src, dst):
        def body(i, carry):
            r = 4 + 8 * i

            def put(k, c, n):
                row = pl.ds(pl.multiple_of((r + k) * 8, 8), 8)
                dst[pl.ds(wrow(r + k), 8), :] = 0.2 * c + l1g[row, :] * (l1b[row, :] + 0.5 * n)

            stencil1(src, r, 8, put)
            return carry

        lax.fori_loop(0, 3, body, 0)

    def restrict1():
        parts = []
        for z in range(4):
            x = l1e[pl.ds(2 * z, 8, stride=16), :] + l1e[pl.ds(2 * z + 1, 8, stride=16), :]
            x = x + l1e[pl.ds(2 * z + 8, 8, stride=16), :] + l1e[pl.ds(2 * z + 9, 8, stride=16), :]
            parts.append(x)
        return dot_split(jnp.concatenate(parts, axis=1), t12[...])

    def base2(z, k):
        return z * 56 + 8 + 8 * k + zero

    def stencil2(src, z, k):
        c = src[pl.ds(base2(z, k), 8), :]
        n = src[pl.ds(base2(z, k) - 1, 8), :] + src[pl.ds(base2(z, k) + 1, 8), :]
        if z > 0:
            n = n + src[pl.ds(base2(z - 1, k), 8), :]
        if z < 3:
            n = n + src[pl.ds(base2(z + 1, k), 8), :]
        return c, n + (pltpu.roll(c, 1, 1) + pltpu.roll(c, 127, 1))

    def sweep2(src, dst, tiles):
        for z in range(4):
            for k in tiles:
                c, n = stencil2(src, z, k)
                row = pl.ds(z * 40 + 8 * k, 8)
                dst[pl.ds(base2(z, k), 8), :] = 0.2 * c + l2g[row, :] * (l2b[row, :] + 0.25 * n)

    def table(ref, rows, cols, f):
        ref[...] = jnp.where(f(iota((rows, cols), 0), iota((rows, cols), 1)), ref_scale[0], 0.0).astype(BF16)

    ref_scale = [0.125]

    def col0(k):
        return jnp.where(k < 128, k, jnp.where(k < 192, k, k - 256))

    table(t01, 256, 128, lambda i, o: (col0(i) >> 1) == o - 32)
    table(t12, 512, 128, lambda i, o: (((i & 127) - 32) >> 1 == (o & 31)) & ((i >> 7) == (o >> 5)))
    table(t23, 128, 128, lambda i, o: ((i - 48) >> 1) == o - 56)
    ref_scale[0] = 1.0
    table(p10, 128, 256, lambda i, o: (col0(o) >> 1) == i - 32)
    table(u2, 384, 512, lambda i, o: (((i & 127) >> 5) == (o >> 7)) & ((o & 127) - 48 == ((i >> 7) - 1) * 32 + (i & 31)))
    table(p32, 128, 128, lambda i, o: ((o - 48) >> 1) == i - 56)
    table(p21, 128, 128, lambda i, o: ((o - 32) >> 1) == i - 48)

    def clear_pads(i, c):
        for ref in (va, vb, vc):
            ref[pl.ds(pl.multiple_of(i * PITCH, 8), 8), :] = z8
        return c

    lax.fori_loop(0, 2 * ROWS + 1, clear_pads, 0)
    for ref in (vb, vc):
        for t in (0, 1):
            for r in (0, 1, ROWS - 2, ROWS - 1):
                ref[pl.ds(vrow(t, r), 16), :] = z16
    for ref in (l1v, l1w):
        ref[...] = jnp.zeros(ref.shape, F32)
    for ref in (l1s, l1g, l1b):
        ref[...] = jnp.zeros(ref.shape, F32)
    for ref in (l2v, l2w):
        ref[...] = jnp.zeros(ref.shape, F32)
    clear_r1(bs1, 2, rp1)
    clear_r1(b2, 1, rp2)
    clear_r2(rt1)
    clear_r2(rt2)

    here = own_ref[0, ty]
    link_l = jnp.where(own_ref[0, jnp.maximum(ty - 1, 0)] == here, 1.0, 0.0)
    link_r = jnp.where(own_ref[0, jnp.minimum(ty + 1, NTY - 1)] == here, 1.0, 0.0)
    link = jnp.where(lane8 == 56, link_l, jnp.where(lane8 == 72, link_r, 1.0))

    pack0(bs1, 2, pk1)
    pl.semaphore_wait(barrier, expected)
    start_r1(bs1, pk1, rp1, 0)

    level3 = {}

    def vcycle(cyc, src, pk, rp, mud, mlr, rt, x, y):
        ns = 2 - cyc
        wait_r1(src, pk, rp, cyc)
        unpack0(src, ns, rp, cyc == 0)

        def start0(i, c):
            for k in range(4):
                for t in (0, 1):
                    row = pl.ds(brow(t, 4 * i + k), 16)
                    if cyc == 0:
                        s = bs1[1, row, :]
                        g = jnp.where(s > 0.0, 0.8 / (s + 6.0), 0.0)
                        gain[row, :] = g
                    else:
                        g = gain[row, :]
                    x[pl.ds(vrow(t, 4 * i + k), 16), :] = g * src[0, row, :]
            return c

        lax.fori_loop(0, ROWS // 4, start0, 0)
        if cyc == 0:
            def sum_rows(i, c):
                for t in (0, 1):
                    ebuf[t, pl.ds(pl.multiple_of(i * 16, 16), 16), :] = (
                        bs1[1, pl.ds(brow(t, 4 + 2 * i), 16), :]
                        + bs1[1, pl.ds(brow(t, 5 + 2 * i), 16), :]
                    )
                return c

            lax.fori_loop(0, 24, sum_rows, 0, unroll=4)
            restrict0(l1s)
            s = l1s[...]
            l1g[...] = jnp.where(s > 0.0, 0.8 / (s + 3.0), 0.0)
            l1e[...] = l1s[pl.ds(64, 128), :]
            s2_own = restrict1()

        sweep0(x, y, src, 2, 13)
        sweep0(y, x, src, 2, 13)

        def defect0(i, c):
            r = 4 + 4 * i
            held = {}

            def put(k, t, centre, n):
                row = pl.ds(brow(t, r + k), 16)
                held[k, t] = src[0, row, :] - (bs1[1, row, :] + 6.0) * centre + n
                if k % 2 == 1:
                    ebuf[t, pl.ds(pl.multiple_of((2 * i + k // 2) * 16, 16), 16), :] = (
                        held[k - 1, t] + held[k, t]
                    )

            stencil0(x, r, 4, (0, 1), put)
            return c

        lax.fori_loop(0, 12, defect0, 0)
        restrict0(l1b)

        for r in range(4, 28):
            row = pl.ds(r * 8, 8)
            l1v[pl.ds(wrow(r), 8), :] = l1g[row, :] * l1b[row, :]
        sweep1(l1v, l1w)
        sweep1(l1w, l1v)

        def defect1(i, c):
            r = 8 + 8 * i

            def put(k, centre, n):
                row = pl.ds(pl.multiple_of((r + k) * 8, 8), 8)
                l1e[pl.ds(pl.multiple_of((8 * i + k) * 8, 8), 8), :] = (
                    l1b[row, :] - (l1s[row, :] + 3.0) * centre + 0.5 * n
                )

            stencil1(l1v, r, 8, put)
            return c

        lax.fori_loop(0, 2, defect1, 0)
        b2_own = restrict1()

        for m in (0, 1):
            mud[m, 0] = b2_own
            mlr[m, 0] = b2_own
            if cyc == 0:
                mud[m, 1] = s2_own
                mlr[m, 1] = s2_own
                mud[m, 7] = link
            for k in range(5):
                mud[m, ns + k] = l1v[pl.ds(wrow(8 + k + 11 * m), 8), :]
        for j in (0, 1):
            left, right = z8, z8
            for g in range(8):
                v = pltpu.roll(l1v[pl.ds(wrow(8 + 8 * j + g), 8), :], (16 * g - 80) % 128, 1)
                right = jnp.where(grp8 == g, v, right)
                left = jnp.where(grp8 == (g + 5) % 8, v, left)
            mlr[0, ns + j] = left
            mlr[1, ns + j] = right
        each_r2("start", mud, mlr, rt, cyc)
        rt[2, 1, 0] = b2_own
        if cyc == 0:
            rt[2, 1, 1] = s2_own
        each_r2("wait_recv", mud, mlr, rt, cyc)

        blocks = []
        for a in range(ns):
            blocks.append(
                jnp.concatenate(
                    [
                        jnp.concatenate([rt[dxi, dyi, a] for dxi in range(5)], axis=0)
                        for dyi in range(3)
                    ],
                    axis=1,
                )
            )
        for a in range(ns):
            spread = dot_split(blocks[a], u2[...])
            for z in range(4):
                part = spread[:, 128 * z : 128 * z + 128]
                if a == 0:
                    l2b[pl.ds(z * 40, 40), :] = part
                else:
                    l2s[pl.ds(z * 40, 40), :] = part
        if cyc == 0:
            s = l2s[...]
            l2g[...] = jnp.where(s > 0.0, 0.8 / (s + 1.5), 0.0)
            for z in range(2):
                l2e[pl.ds(z * 40, 40), :] = (
                    l2s[pl.ds(2 * z * 40, 40), :] + l2s[pl.ds((2 * z + 1) * 40, 40), :]
                )
            level3["s"] = restrict2()
            s = level3["s"]
            level3["g"] = jnp.where(s > 0.0, 0.8 / (s + 0.75), 0.0)
            up, down = rt[1, 1, 7], rt[3, 1, 7]
            ml = [jnp.where(sub8 < 4, up, link), down]
            level3["ml"] = [0.125 * m for m in ml]
            level3["mr"] = [pltpu.roll(0.125 * m, 127, 1) for m in ml]
        for z in range(4):
            for k in range(5):
                row = pl.ds(z * 40 + 8 * k, 8)
                l2v[pl.ds(base2(z, k), 8), :] = l2g[row, :] * l2b[row, :]
        sweep2(l2v, l2w, range(5))
        sweep2(l2w, l2v, range(5))
        for k in range(5):
            d = []
            for z in range(4):
                c, n = stencil2(l2v, z, k)
                row = pl.ds(z * 40 + 8 * k, 8)
                d.append(l2b[row, :] - (l2s[row, :] + 1.5) * c + 0.25 * n)
            l2e[pl.ds(8 * k, 8), :] = d[0] + d[1]
            l2e[pl.ds(40 + 8 * k, 8), :] = d[2] + d[3]
        b3 = restrict2()
        solve3(b3)

        for z in range(4):
            for k in (1, 2, 3):
                row = pl.ds(base2(z, k), 8)
                l2v[row, :] = l2v[row, :] + l2x[pl.ds((z // 2) * 32 + 8 * (k - 1), 8), :]
        sweep2(l2v, l2w, (1, 2, 3))
        sweep2(l2w, l2v, (1, 2, 3))
        sweep2(l2v, l2w, (1, 2, 3))
        e2 = jnp.concatenate([l2w[pl.ds(z * 56 + 20 + zero, 16), :] for z in range(4)], axis=0)
        e2 = dot_split(e2, p21[...])
        for z in range(4):
            for a in (0, 8):
                for b in (0, 1):
                    l1x[pl.ds(a + 2 * z + b, 16, stride=16), :] = e2[16 * z : 16 * z + 16]

        for r in range(3, 29):
            tile, inner = (r - 8) // 16, (r - 8) % 16
            j, g = inner // 8, inner % 8
            v = jnp.where(grp8 == g, rt[2 + tile, 0, ns + j], rt[2 + tile, 2, ns + j])
            v = pltpu.roll(v, (16 - 16 * g) % 128, 1)
            if tile == 0:
                base = l1v[pl.ds(wrow(r), 8), :]
            elif tile < 0:
                base = rt[1, 1, ns + inner - 11]
            else:
                base = rt[3, 1, ns + inner]
            l1v[pl.ds(wrow(r), 8), :] = jnp.where(side8, v, base) + l1x[pl.ds(r * 8, 8), :]
        sweep1(l1v, l1w)
        sweep1(l1w, l1v)
        sweep1(l1v, l1w)
        for i in range(2):
            e1 = jnp.concatenate([l1w[pl.ds(wrow(6 + 10 * i + k), 8), :] for k in range(10)], axis=0)
            e1 = dot_split(e1, p10[...])
            for t in (0, 1):
                for b in (0, 1):
                    xbuf[t, pl.ds(160 * i + b, 80, stride=2), :] = e1[:, 128 * t : 128 * t + 128]

        def correct0(i, c):
            for t in (0, 1):
                e = xbuf[t, pl.ds(pl.multiple_of(i * 16, 16), 16), :]
                for k in (0, 1):
                    row = pl.ds(vrow(t, 8 + 2 * i + k), 16)
                    x[row, :] = x[row, :] + e
            return c

        lax.fori_loop(0, 20, correct0, 0, unroll=2)
        sweep0(x, y, src, 8, 10)
        sweep0(y, x, src, 10, 9)
        sweep0(x, y, src, 10, 9)

    def restrict2():
        parts = [
            l2e[pl.ds(z * 40 + 8, 16, stride=2), :] + l2e[pl.ds(z * 40 + 9, 16, stride=2), :]
            for z in range(2)
        ]
        return dot_split(jnp.concatenate(parts, axis=0), t23[...])

    def solve3(b3):
        up_ok = jnp.where((sub8 & 3) != 0, 0.125, 0.0)
        down_ok = jnp.where((sub8 & 3) != 3, 0.125, 0.0)
        g = [[level3["g"][16 * z + 8 * k : 16 * z + 8 * k + 8] for k in (0, 1)] for z in (0, 1)]
        b = [[b3[16 * z + 8 * k : 16 * z + 8 * k + 8] for k in (0, 1)] for z in (0, 1)]
        v = [[g[z][k] * b[z][k] for k in (0, 1)] for z in (0, 1)]
        for counter in range(7):
            new = [[None, None], [None, None]]
            for z in (0, 1):
                for k in (0, 1):
                    c = v[z][k]
                    n = 0.125 * v[1 - z][k]
                    n = n + pltpu.roll(c, 1, 0) * up_ok + pltpu.roll(c, 7, 0) * down_ok
                    n = n + pltpu.roll(c, 1, 1) * level3["ml"][k] + pltpu.roll(c, 127, 1) * level3["mr"][k]
                    new[z][k] = 0.2 * c + g[z][k] * (b[z][k] + n)
            v = new
        e3 = jnp.concatenate([v[0][0], v[0][1], v[1][0], v[1][1]], axis=0)
        e3 = dot_split(e3, p32[...])
        for z in (0, 1):
            for a in (0, 1):
                l2x[pl.ds(z * 32 + a, 16, stride=2), :] = e3[16 * z : 16 * z + 16]

    vcycle(0, bs1, pk1, rp1, m1ud, m1lr, rt1, va, vb)

    def halves(a):
        return a[0:8] + a[8:16]

    def apply_first(i, acc):
        r = TOP + 4 * i
        rz, zq = acc
        held = []

        def put(k, t, c, n):
            row = pl.ds(brow(0, r + k), 16)
            q = (bs1[1, row, :] + 6.0) * c - n
            b2[0, row, :] = q
            held.append((bs1[0, row, :] * c, c * q))

        stencil0(vb, r, 4, (0,), put)
        for a, b in held:
            rz = rz + halves(a)
            zq = zq + halves(b)
        return rz, zq

    sums = lax.fori_loop(0, 8, apply_first, (z8, z8))
    pack0(b2, 1, pk2)
    start_r1(b2, pk2, rp2, 1)
    ar_begin(0, sums)
    ar_middle(0)

    vcycle(1, b2, pk2, rp2, m2ud, m2lr, rt2, va, vc)
    rho0, curv0 = ar_end(0, 2)
    step0 = rho0 / curv0
    step0_16 = jnp.concatenate([step0, step0], axis=0)

    def next_z(i, c):
        for k in (0, 1):
            for t in (0, 1):
                row = pl.ds(vrow(t, TOP - 2 + 2 * i + k), 16)
                vc[row, :] = vb[row, :] - step0_16 * vc[row, :]
        return c

    lax.fori_loop(0, 18, next_z, 0, unroll=2)

    def apply_second(i, acc):
        r = TOP + 4 * i
        rz, zz, cross = acc
        held = []

        def put(k, t, c, n):
            row = pl.ds(brow(0, r + k), 16)
            q = (bs1[1, row, :] + 6.0) * c - n
            q1[row, :] = q
            q0 = b2[0, row, :]
            z0 = vb[pl.ds(vrow(0, r + k), 16), :]
            held.append(((bs1[0, row, :] - step0_16 * q0) * c, c * q, c * q0 + z0 * q))

        stencil0(vc, r, 4, (0,), put)
        for a, b, d in held:
            rz, zz, cross = rz + halves(a), zz + halves(b), cross + halves(d)
        return rz, zz, cross

    sums = lax.fori_loop(0, 8, apply_second, (z8, z8, z8))
    ar_begin(1, sums)
    ar_middle(1)
    rho1, zz, cross = ar_end(1, 3)
    beta = rho1 / rho0
    curv1 = zz + beta * (cross + beta * curv0)
    step1 = rho1 / curv1
    mixed = step0 + step1 * beta

    for z in range(16):
        for k in range(4):
            r = TOP + 8 * k
            z0 = vb[pl.ds(8 + r * PITCH + z, 8, stride=PITCH), :]
            z1 = vc[pl.ds(8 + r * PITCH + z, 8, stride=PITCH), :]
            q0 = b2[0, pl.ds(r * 16 + z, 8, stride=16), :]
            qn = q1[pl.ds(r * 16 + z, 8, stride=16), :]
            sol_ref[z, 8 * k : 8 * k + 8, :] = mixed * z0 + step1 * z1
            res_ref[z, 8 * k : 8 * k + 8, :] = rhs_ref[z, 8 * k : 8 * k + 8, :] - mixed * q0 - step1 * qn

    sent_r1(bs1, pk1, rp1, 0)
    sent_r1(b2, pk2, rp2, 1)
    each_r2("wait_send", m1ud, m1lr, rt1, 0)
    each_r2("wait_send", m2ud, m2lr, rt2, 1)
    for cyc in (0, 1):
        for i in range(22):
            ar_copy(cyc, i).wait_send()


def on_device(right_side, screening, owners):
    vm = lambda *s: pltpu.VMEM(s, F32)
    bm = lambda *s: pltpu.VMEM(s, BF16)
    padded = 8 + 2 * ROWS * PITCH + 8
    scratch = [
        vm(2, 2 * PLANE, 128), vm(1, 2 * PLANE, 128), vm(2 * PLANE, 128),
        vm(padded, 128), vm(padded, 128), vm(padded, 128), vm(PLANE, 128),
        vm(2, 2, 64, 128), vm(2, 1, 64, 128), vm(3, 2, 2, 64, 128), vm(3, 2, 1, 64, 128),
        vm(2, 24 * 16, 128), vm(2, 20 * 16, 128),
        vm(R1 * 8, 128), vm(R1 * 8, 128), vm(R1 * 8, 128), vm(R1 * 8, 128),
        vm(R1 * 16 + 16, 128), vm(R1 * 16 + 16, 128), vm(128, 128),
        vm(2, 8, 8, 128), vm(2, 4, 8, 128), vm(2, 8, 8, 128), vm(2, 4, 8, 128),
        vm(5, 3, 8, 8, 128), vm(5, 3, 8, 8, 128),
        vm(160, 128), vm(160, 128), vm(160, 128), vm(4 * 56, 128), vm(4 * 56, 128),
        vm(80, 128), vm(64, 128),
        bm(256, 128), bm(128, 256), bm(512, 128), bm(384, 512), bm(128, 128), bm(128, 128), bm(128, 128),
        vm(2, 2, 8, 128), vm(2, 7, 8, 128), vm(2, 15, 8, 128),
        pltpu.SemaphoreType.DMA((2, 8)), pltpu.SemaphoreType.DMA((2, 8)),
        pltpu.SemaphoreType.DMA((2, 14)), pltpu.SemaphoreType.DMA((2, 14)),
        pltpu.SemaphoreType.DMA((2, 22)), pltpu.SemaphoreType.DMA((2, 22)),
    ]
    block = jax.ShapeDtypeStruct(right_side.shape, F32)
    vmem = pl.BlockSpec(memory_space=pltpu.VMEM)
    return tuple(
        pl.pallas_call(
            kernel,
            out_shape=(block, block),
            in_specs=[vmem, vmem, pl.BlockSpec(memory_space=pltpu.SMEM)],
            out_specs=(vmem, vmem),
            scratch_shapes=scratch,
            compiler_params=pltpu.CompilerParams(
                collective_id=0, has_side_effects=True, vmem_limit_bytes=40 * 2**20
            ),
        )(right_side, screening, owners)
    )


def solution(mesh):
    spec = P(None, "tx", "ty")
    return jax.shard_map(
        on_device, mesh=mesh, in_specs=(spec, spec, P("tx", None)), out_specs=(spec, spec),
        check_vma=False,
    )
```

```python
import functools

import jax
import jax.numpy as jnp
from jax import lax
from jax.experimental import pallas as pl
from jax.experimental.pallas import tpu as pltpu
from jax.sharding import PartitionSpec as P

MESH = pl.DeviceIdType.MESH
F32 = jnp.float32
BF16 = jnp.bfloat16

NTX, NTY = 8, 16
HALO = 11
ROWS = 56
TOP = 12
PLANE = ROWS * 16
PITCH = 24
R1 = 32
DIRS8 = [(-1, -1), (1, -1), (-1, 1), (1, 1), (0, -1), (0, 1), (-1, 0), (1, 0)]
DIRS14 = [(-2, -1), (2, -1), (-2, 1), (2, 1)] + DIRS8[:6] + [(-2, 0), (2, 0), (-1, 0), (1, 0)]


def iota(shape, axis):
    return lax.broadcasted_iota(jnp.int32, shape, axis)


def dot_split(x, table):
    high = x.astype(BF16)
    low = (x - high.astype(F32)).astype(BF16)
    return jnp.dot(high, table, preferred_element_type=F32) + jnp.dot(
        low, table, preferred_element_type=F32
    )


def dot_exact(x, table):
    high = x.astype(BF16)
    rest = x - high.astype(F32)
    middle = rest.astype(BF16)
    low = (rest - middle.astype(F32)).astype(BF16)
    dot = functools.partial(jnp.dot, preferred_element_type=F32)
    return dot(high, table) + (dot(middle, table) + dot(low, table))


def kernel(
    rhs_hbm, scr_hbm, own_hbm, sol_ref, res_ref,
    rhs_ref, scr_ref, own_ref, s_in,
    bs1, b2, gain, va, vb, vc, q1, pk1, pk2, rp1, rp2, sl1, sl2, rs1, rs2, ebuf, xbuf, natural,
    l1s, l1g, l1b, l1x, l1v, l1w, l1e,
    m1ud, m1lr, m2ud, m2lr, rt1, rt2,
    l2b, l2s, l2g, l2v, l2w, l2e, l2x, l3g, l3m,
    split, merge, t12, u2, t23, p32, p21,
    arbuf, arr1, arr2,
    s_r1, r_r1, s_r2, r_r2, s_ar, r_ar,
):
    tx = lax.axis_index("tx")
    ty = lax.axis_index("ty")
    zero = lax.div(tx, 64)
    barrier = pltpu.get_barrier_semaphore()
    loads = [
        pltpu.make_async_copy(rhs_hbm, rhs_ref, s_in.at[0]),
        pltpu.make_async_copy(scr_hbm, scr_ref, s_in.at[1]),
        pltpu.make_async_copy(own_hbm, own_ref, s_in.at[2]),
    ]
    for load in loads:
        load.start()

    def inside(dx, dy):
        a, b = tx + dx, ty + dy
        return (a >= 0) & (a < NTX) & (b >= 0) & (b < NTY)

    def at(dx, dy):
        return {"tx": tx + dx, "ty": ty + dy}

    def ring(dx, dy):
        return {"tx": lax.rem(tx + dx, NTX), "ty": lax.rem(ty + dy, NTY)}

    ring_dirs = [(k, 0) for k in range(1, NTX)] + [(0, k) for k in range(1, NTY)]
    extra = [d for d in DIRS14 if d[0] != 0 and d[1] != 0]
    expected = jnp.int32(len(ring_dirs))
    for d in ring_dirs:
        pl.semaphore_signal(barrier, inc=1, device_id=ring(*d), device_id_type=MESH)
    for d in extra:
        ok = inside(*d)
        expected = expected + ok.astype(jnp.int32)

        @pl.when(ok)
        def _():
            pl.semaphore_signal(barrier, inc=1, device_id=at(*d), device_id_type=MESH)

    lane16 = iota((16, 128), 1)
    lane8 = iota((8, 128), 1)
    sub8 = iota((8, 128), 0)
    grp8 = lane8 >> 4
    half16 = lane16 >> 3
    own16 = (lane16 >= 32) & (lane16 < 96)
    own8 = (lane8 >= 32) & (lane8 < 96)
    side16 = ((lane16 >= 24) & (lane16 < 32)) | ((lane16 >= 96) & (lane16 < 104))
    side8 = ((lane8 >= 16) & (lane8 < 32)) | ((lane8 >= 96) & (lane8 < 112))
    z16 = jnp.zeros((16, 128), F32)
    z8 = jnp.zeros((8, 128), F32)

    def vrow(t, r):
        return pl.multiple_of(8 + (t * ROWS + r) * PITCH, 8)

    def brow(t, r):
        return pl.multiple_of((t * ROWS + r) * 16, 16)

    def stage(name, fn):
        fn()

    def take_inputs():
        for a, ref in enumerate((rhs_ref, scr_ref)):
            for i in range(2):
                x = [ref[pl.ds(16 * i + k, 16, stride=32), :] for k in range(16)]
                x = dot_exact(jnp.concatenate(x, axis=0), split[...])
                for t in (0, 1):
                    at_row = (t * ROWS + TOP + 16 * i) * 16
                    bs1[a, pl.ds(at_row, 256), :] = x[:, 128 * t : 128 * t + 128]

    def pack0(src, count, pk, sl):
        def body(j, c):
            span = pl.ds(pl.multiple_of(j * 16, 16), 16)
            for a in range(count):
                left, right = z16, z16
                for g in range(8):
                    even = src[a, pl.ds(brow(0, TOP + j * 8 + g), 16), :]
                    odd = src[a, pl.ds(brow(1, TOP + j * 8 + g), 16), :]
                    even = pltpu.roll(even, (16 * g - 88) % 128, 1)
                    odd = pltpu.roll(odd, (16 * g - 80) % 128, 1)
                    right = jnp.where(half16 == 2 * g, even, jnp.where(half16 == 2 * g + 1, odd, right))
                    left = jnp.where(
                        half16 == (2 * g - 7) % 16, even,
                        jnp.where(half16 == (2 * g - 6) % 16, odd, left),
                    )
                pk[0, a, span, :] = left
                pk[1, a, span, :] = right
            return c

        lax.fori_loop(0, 4, body, 0)
        for a in range(count):
            for m, first in ((0, TOP), (1, TOP + 32 - HALO)):
                for k in range(HALO):
                    even = src[a, pl.ds(brow(0, first + k), 16), :]
                    odd = src[a, pl.ds(brow(1, first + k), 16), :]
                    sl[m, a, pl.ds(16 * k, 16), :] = jnp.where(own16, even, pltpu.roll(odd, 64, 1))

    def unpack0(dst, count, rp, rs, x):
        def row(dxi, j, g):
            r = TOP + (dxi - 1) * 32 + j * 8 + g
            span = pl.ds(pl.multiple_of(j * 16, 16), 16)
            out = []
            for a in range(count):
                fl, fr = rp[dxi, 0, a, span, :], rp[dxi, 1, a, span, :]
                if dxi == 1:
                    even, odd = dst[a, pl.ds(brow(0, r), 16), :], dst[a, pl.ds(brow(1, r), 16), :]
                else:
                    k = j * 8 + g - (32 - HALO if dxi == 0 else 0)
                    both = rs[dxi // 2, a, pl.ds(16 * k, 16), :]
                    even, odd = jnp.where(own16, both, 0.0), jnp.where(own16, pltpu.roll(both, 64, 1), 0.0)
                ve = pltpu.roll(jnp.where(half16 == 2 * g, fl, fr), (24 - 16 * g) % 128, 1)
                vo = pltpu.roll(jnp.where(half16 == 2 * g + 1, fl, fr), (16 - 16 * g) % 128, 1)
                even, odd = jnp.where(side16, ve, even), jnp.where(side16, vo, odd)
                dst[a, pl.ds(brow(0, r), 16), :] = even
                dst[a, pl.ds(brow(1, r), 16), :] = odd
                out.append((even, odd))
            for t in (0, 1):
                at_row = pl.ds(brow(t, r), 16)
                if count == 2:
                    s = out[1][t]
                    gv = jnp.where(s > 0.0, 0.8 / (s + 6.0), 0.0)
                    gain[at_row, :] = gv
                else:
                    gv = gain[at_row, :]
                x[pl.ds(vrow(t, r), 16), :] = gv * out[0][t]

        def body(j, c):
            for g in range(8):
                row(1, j, g)
            return c

        lax.fori_loop(0, 4, body, 0)
        for j, groups in ((2, range(5, 8)), (3, range(8))):
            for g in groups:
                row(0, j, g)
        for j, groups in ((0, range(8)), (1, range(3))):
            for g in groups:
                row(2, j, g)

    def r1_copy(i, d, pk, rp, sl, rs, cyc):
        dx, dy = d
        if dy == 0:
            s, t = sl.at[0 if dx == -1 else 1], rs.at[1 if dx == -1 else 0]
        else:
            side = 0 if dy == -1 else 1
            if dx == 0:
                s, t = pk.at[side], rp.at[1, 1 - side]
            elif dx == -1:
                s, t = pk.at[side, :, pl.ds(0, 32)], rp.at[2, 1 - side, :, pl.ds(0, 32)]
            else:
                s, t = pk.at[side, :, pl.ds(32, 32)], rp.at[0, 1 - side, :, pl.ds(32, 32)]
        return pltpu.make_async_remote_copy(
            src_ref=s, dst_ref=t, send_sem=s_r1.at[cyc, i], recv_sem=r_r1.at[cyc, i],
            device_id=at(*d), device_id_type=MESH,
        )

    def start_r1(pk, rp, sl, rs, cyc):
        for i, d in enumerate(DIRS8):
            @pl.when(inside(*d))
            def _():
                r1_copy(i, d, pk, rp, sl, rs, cyc).start()

    def wait_r1(pk, rp, sl, rs, cyc):
        for i, d in enumerate(DIRS8):
            @pl.when(inside(-d[0], -d[1]))
            def _():
                r1_copy(i, d, pk, rp, sl, rs, cyc).wait_recv()

    def sent_r1(pk, rp, sl, rs, cyc):
        for i, d in enumerate(DIRS8):
            @pl.when(inside(*d))
            def _():
                r1_copy(i, d, pk, rp, sl, rs, cyc).wait_send()

    def clear_r1(src, count, rp, rs):
        for a in range(count):
            for t in (0, 1):
                for r in (0, ROWS - 1):
                    src[a, pl.ds(brow(t, r), 16), :] = z16
        for i, dx in ((0, -1), (1, 1)):
            @pl.when(jnp.logical_not(inside(dx, 0)))
            def _():
                rs[i] = jnp.zeros((count, HALO * 16, 128), F32)
        for dxi in range(3):
            for sidei, dy in ((0, -1), (1, 1)):
                @pl.when(jnp.logical_not(inside(dxi - 1, dy)))
                def _():
                    rp[dxi, sidei] = jnp.zeros((count, 64, 128), F32)

    def r2_copy(i, d, mud, mlr, rt, cyc):
        dx, dy = d
        ns = 2 - cyc
        if dy == 0:
            n = (6 + ns - cyc) if abs(dx) == 1 else ns
            s = mud.at[0 if dx < 0 else 1, pl.ds(0, n)]
        else:
            n = (2 + ns) if abs(dx) <= 1 else ns
            s = mlr.at[0 if dy < 0 else 1, pl.ds(0, n)]
        return pltpu.make_async_remote_copy(
            src_ref=s, dst_ref=rt.at[2 - dx, 1 - dy, pl.ds(0, n)],
            send_sem=s_r2.at[cyc, i], recv_sem=r_r2.at[cyc, i],
            device_id=at(*d), device_id_type=MESH,
        )

    def each_r2(op, mud, mlr, rt, cyc):
        for i, d in enumerate(DIRS14):
            @pl.when(inside(-d[0], -d[1]) if op == "wait_recv" else inside(*d))
            def _():
                getattr(r2_copy(i, d, mud, mlr, rt, cyc), op)()

    def clear_r2(rt):
        for dx, dy in DIRS14:
            @pl.when(jnp.logical_not(inside(dx, dy)))
            def _():
                rt[2 + dx, 1 + dy] = jnp.zeros((8, 8, 128), F32)

    def ar_copy(cyc, i):
        if i < 7:
            d, s, t = ring(i + 1, 0), arbuf.at[cyc, 0], arr1.at[cyc, i]
        else:
            d, s, t = ring(0, i - 6), arbuf.at[cyc, 1], arr2.at[cyc, i - 7]
        return pltpu.make_async_remote_copy(
            src_ref=s, dst_ref=t, send_sem=s_ar.at[cyc, i], recv_sem=r_ar.at[cyc, i],
            device_id=d, device_id_type=MESH,
        )

    def ar_begin(cyc, rows):
        out = jnp.zeros((1, 128), F32)
        for k, acc in enumerate(rows):
            acc = jnp.sum(jnp.where(own8, acc, 0.0), axis=0, keepdims=True)
            out = jnp.where(lane8[:1] == k, jnp.sum(acc, axis=1, keepdims=True), out)
        arbuf[cyc, 0] = out
        for i in range(7):
            ar_copy(cyc, i).start()

    def ar_middle(cyc):
        total = arbuf[cyc, 0]
        for i in range(7):
            ar_copy(cyc, i).wait_recv()
        for i in range(7):
            total = total + arr1[cyc, i]
        arbuf[cyc, 1] = total
        for i in range(7, 22):
            ar_copy(cyc, i).start()

    def ar_end(cyc, count):
        total = arbuf[cyc, 1]
        for i in range(7, 22):
            ar_copy(cyc, i).wait_recv()
        for i in range(15):
            total = total + arr2[cyc, i]
        return [jnp.broadcast_to(total[:, k : k + 1], (8, 128)) for k in range(count)]

    def stencil0(src, r, count, put):
        rows = [
            [src[pl.ds(vrow(t, r + k - 1), 16), :] for k in range(count + 2)] for t in (0, 1)
        ]
        for k in range(count):
            even, odd = rows[0][k + 1], rows[1][k + 1]
            beside = (odd + pltpu.roll(odd, 1, 1), even + pltpu.roll(even, 127, 1))
            for t in (0, 1):
                at_row = vrow(t, r + k)
                n = rows[t][k] + rows[t][k + 2]
                n = n + (src[pl.ds(at_row - 1, 16), :] + src[pl.ds(at_row + 1, 16), :])
                put(k, t, rows[t][k + 1], n + beside[t])

    def sweep0(src, dst, bref, r0, count, per):
        def body(i, carry):
            r = r0 + per * i

            def put(k, t, c, n):
                row = pl.ds(brow(t, r + k), 16)
                dst[pl.ds(vrow(t, r + k), 16), :] = 0.2 * c + gain[row, :] * (bref[0, row, :] + n)

            stencil0(src, r, per, put)
            return carry

        lax.fori_loop(0, count // per, body, 0)

    def restrict0(out):
        x = ebuf[pl.ds(0, 192, stride=2), :] + ebuf[pl.ds(1, 192, stride=2), :]
        out[pl.ds(32, 192), :] = 0.125 * x

    def wrow(r):
        return pl.multiple_of(8 + r * 16, 8)

    def stencil1(src, r, count, put):
        rows = [src[pl.ds(wrow(r + k - 1), 8), :] for k in range(count + 2)]
        for k in range(count):
            c = rows[k + 1]
            n = rows[k] + rows[k + 2]
            n = n + (src[pl.ds(wrow(r + k) - 1, 8), :] + src[pl.ds(wrow(r + k) + 1, 8), :])
            n = n + (pltpu.roll(c, 1, 1) + pltpu.roll(c, 127, 1))
            put(k, c, n)

    def sweep1(src, dst):
        def put(k, c, n):
            row = pl.ds((4 + k) * 8, 8)
            dst[pl.ds(wrow(4 + k + zero), 8), :] = 0.2 * c + l1g[row, :] * (l1b[row, :] + 0.5 * n)

        stencil1(src, 4 + zero, 24, put)

    def restrict1():
        parts = []
        for z in range(4):
            x = l1e[pl.ds(2 * z, 8, stride=16), :] + l1e[pl.ds(2 * z + 1, 8, stride=16), :]
            x = x + l1e[pl.ds(2 * z + 8, 8, stride=16), :] + l1e[pl.ds(2 * z + 9, 8, stride=16), :]
            parts.append(x)
        return dot_split(jnp.concatenate(parts, axis=1), t12[...])

    def base2(z, k):
        return z * 56 + 8 + 8 * k + zero

    def stencil2(src, z, k):
        c = src[pl.ds(base2(z, k), 8), :]
        n = src[pl.ds(base2(z, k) - 1, 8), :] + src[pl.ds(base2(z, k) + 1, 8), :]
        if z > 0:
            n = n + src[pl.ds(base2(z - 1, k), 8), :]
        if z < 3:
            n = n + src[pl.ds(base2(z + 1, k), 8), :]
        return c, n + (pltpu.roll(c, 1, 1) + pltpu.roll(c, 127, 1))

    def sweep2(src, dst, tiles):
        for z in range(4):
            for k in tiles:
                c, n = stencil2(src, z, k)
                row = pl.ds(z * 40 + 8 * k, 8)
                dst[pl.ds(base2(z, k), 8), :] = 0.2 * c + l2g[row, :] * (l2b[row, :] + 0.25 * n)

    def table(ref, rows, cols, value, f):
        ref[...] = jnp.where(f(iota((rows, cols), 0), iota((rows, cols), 1)), value, 0.0).astype(BF16)

    def prepare():
        tables()
        zeros()

    def tables():
        table(merge, 256, 128, 1.0, lambda i, o: ((i & 127) - 32 == o >> 1) & ((i >> 7) == (o & 1)))
        table(t12, 512, 128, 0.125, lambda i, o: (((i & 127) - 32) >> 1 == (o & 31)) & ((i >> 7) == (o >> 5)))
        table(t23, 128, 128, 0.125, lambda i, o: ((i - 48) >> 1) == o - 56)
        table(u2, 384, 512, 1.0, lambda i, o: (((i & 127) >> 5) == (o >> 7)) & ((o & 127) - 48 == ((i >> 7) - 1) * 32 + (i & 31)))
        table(p32, 128, 128, 1.0, lambda i, o: ((o - 48) >> 1) == i - 56)
        table(p21, 128, 128, 1.0, lambda i, o: ((o - 32) >> 1) == i - 48)

    def zeros():
        def clear_pads(i, c):
            for ref in (va, vb, vc):
                ref[pl.ds(pl.multiple_of(i * PITCH, 8), 8), :] = z8
            return c

        lax.fori_loop(0, 2 * ROWS + 1, clear_pads, 0)
        for ref in (vb, vc):
            for t in (0, 1):
                for r in (0, 1, ROWS - 2, ROWS - 1):
                    ref[pl.ds(vrow(t, r), 16), :] = z16
        for ref in (l1v, l1w):
            ref[...] = jnp.zeros(ref.shape, F32)
        for ref in (l1s, l1g, l1b):
            ref[...] = jnp.zeros(ref.shape, F32)
        for ref in (l2v, l2w):
            ref[...] = jnp.zeros(ref.shape, F32)
        clear_r1(bs1, 2, rp1, rs1)
        clear_r1(b2, 1, rp2, rs2)
        clear_r2(rt1)
        clear_r2(rt2)

    table(split, 128, 256, 1.0, lambda i, o: ((o & 127) - 32 == i >> 1) & ((o >> 7) == (i & 1)))
    for load in loads:
        load.wait()
    stage("take_inputs", take_inputs)
    here = own_ref[0, ty]
    link_l = jnp.where(own_ref[0, jnp.maximum(ty - 1, 0)] == here, 1.0, 0.0)
    link_r = jnp.where(own_ref[0, jnp.minimum(ty + 1, NTY - 1)] == here, 1.0, 0.0)
    link = jnp.where(lane8 == 56, link_l, jnp.where(lane8 == 72, link_r, 1.0))

    def screen_sums(first, count):
        for i in range(first, first + count):
            even = bs1[1, pl.ds(brow(0, 4 + 2 * i), 32), :]
            odd = bs1[1, pl.ds(brow(1, 4 + 2 * i), 32), :]
            x = even + odd
            ebuf[pl.ds(i * 16, 16), :] = x[:16] + x[16:]

    def own_screens():
        screen_sums(4, 16)
        x = ebuf[pl.ds(64, 128, stride=2), :] + ebuf[pl.ds(65, 128, stride=2), :]
        l1e[...] = 0.125 * x
        s2_own = restrict1()
        for m in (0, 1):
            m1ud[m, 1] = s2_own
            m1lr[m, 1] = s2_own
            m1ud[m, 7] = link
        rt1[2, 1, 1] = s2_own

    def vcycle(cyc, src, pk, rp, sl, rs, mud, mlr, rt, x, y):
        ns = 2 - cyc

        def screens1():
            screen_sums(0, 24)
            restrict0(l1s)
            s = l1s[...]
            l1g[...] = jnp.where(s > 0.0, 0.8 / (s + 3.0), 0.0)

        def defect0():
            per = 24

            def body(i, c):
                r = 4 + per * i
                held = []

                def put(k, t, centre, n):
                    row = pl.ds(brow(t, r + k), 16)
                    held.append(src[0, row, :] - (bs1[1, row, :] + 6.0) * centre + n)
                    if len(held) == 4:
                        at_row = pl.multiple_of((i * (per // 2) + k // 2) * 16, 16)
                        ebuf[pl.ds(at_row, 16), :] = (held[0] + held[1]) + (held[2] + held[3])
                        held.clear()

                stencil0(x, r, per, put)
                return c

            lax.fori_loop(0, 48 // per, body, 0)

        def start1():
            for r in range(4, 28):
                row = pl.ds(r * 8, 8)
                l1v[pl.ds(wrow(r), 8), :] = l1g[row, :] * l1b[row, :]

        def defect1():
            def put(k, centre, n):
                row = pl.ds((8 + k) * 8, 8)
                l1e[pl.ds(k * 8, 8), :] = l1b[row, :] - (l1s[row, :] + 3.0) * centre + 0.5 * n

            stencil1(l1v, 8 + zero, 16, put)

        def pack1():
            for m in (0, 1):
                for k in range(5):
                    mud[m, ns + k] = l1v[pl.ds(wrow(8 + k + 11 * m), 8), :]
            for j in (0, 1):
                left, right = z8, z8
                for g in range(8):
                    v = pltpu.roll(l1v[pl.ds(wrow(8 + 8 * j + g), 8), :], (16 * g - 80) % 128, 1)
                    right = jnp.where(grp8 == g, v, right)
                    left = jnp.where(grp8 == (g + 5) % 8, v, left)
                mlr[0, ns + j] = left
                mlr[1, ns + j] = right

        def down1():
            b2_own = restrict1()
            for m in (0, 1):
                mud[m, 0] = b2_own
                mlr[m, 0] = b2_own
            rt[2, 1, 0] = b2_own

        def unpack2():
            for a in range(ns):
                block = jnp.concatenate(
                    [
                        jnp.concatenate([rt[dxi, dyi, a] for dxi in range(5)], axis=0)
                        for dyi in range(3)
                    ],
                    axis=1,
                )
                spread = dot_split(block, u2[...])
                for z in range(4):
                    part = spread[:, 128 * z : 128 * z + 128]
                    if a == 0:
                        l2b[pl.ds(z * 40, 40), :] = part
                    else:
                        l2s[pl.ds(z * 40, 40), :] = part

        def screens3():
            s = l2s[...]
            l2g[...] = jnp.where(s > 0.0, 0.8 / (s + 1.5), 0.0)
            for z in range(2):
                l2e[pl.ds(z * 40, 40), :] = (
                    l2s[pl.ds(2 * z * 40, 40), :] + l2s[pl.ds((2 * z + 1) * 40, 40), :]
                )
            s = restrict2()
            l3g[...] = jnp.where(s > 0.0, 0.8 / (s + 0.75), 0.0)
            up, down = rt[1, 1, 7], rt[3, 1, 7]
            for k, m in enumerate((jnp.where(sub8 < 4, up, link), down)):
                l3m[0, k] = 0.125 * m
                l3m[1, k] = pltpu.roll(0.125 * m, 127, 1)

        def down2():
            for z in range(4):
                for k in range(5):
                    row = pl.ds(z * 40 + 8 * k, 8)
                    l2v[pl.ds(base2(z, k), 8), :] = l2g[row, :] * l2b[row, :]
            sweep2(l2v, l2w, range(5))
            sweep2(l2w, l2v, range(5))
            for k in range(5):
                d = []
                for z in range(4):
                    c, n = stencil2(l2v, z, k)
                    row = pl.ds(z * 40 + 8 * k, 8)
                    d.append(l2b[row, :] - (l2s[row, :] + 1.5) * c + 0.25 * n)
                l2e[pl.ds(8 * k, 8), :] = d[0] + d[1]
                l2e[pl.ds(40 + 8 * k, 8), :] = d[2] + d[3]

        def up2():
            for z in range(4):
                for k in (1, 2, 3):
                    row = pl.ds(base2(z, k), 8)
                    l2v[row, :] = l2v[row, :] + l2x[pl.ds((z // 2) * 32 + 8 * (k - 1), 8), :]
            sweep2(l2v, l2w, (1, 2, 3))
            sweep2(l2w, l2v, (1, 2, 3))
            sweep2(l2v, l2w, (1, 2, 3))
            e2 = jnp.concatenate([l2w[pl.ds(z * 56 + 20 + zero, 16), :] for z in range(4)], axis=0)
            e2 = dot_split(e2, p21[...])
            for z in range(4):
                for a in (0, 8):
                    for b in (0, 1):
                        l1x[pl.ds(a + 2 * z + b, 16, stride=16), :] = e2[16 * z : 16 * z + 16]

        def correct1():
            for r in range(3, 29):
                tile, inner = (r - 8) // 16, (r - 8) % 16
                j, g = inner // 8, inner % 8
                v = jnp.where(grp8 == g, rt[2 + tile, 0, ns + j], rt[2 + tile, 2, ns + j])
                v = pltpu.roll(v, (16 - 16 * g) % 128, 1)
                if tile == 0:
                    base = l1v[pl.ds(wrow(r), 8), :]
                elif tile < 0:
                    base = rt[1, 1, ns + inner - 11]
                else:
                    base = rt[3, 1, ns + inner]
                l1v[pl.ds(wrow(r), 8), :] = jnp.where(side8, v, base) + l1x[pl.ds(r * 8, 8), :]

        def up1():
            e1 = jnp.concatenate([l1w[pl.ds(wrow(6 + k), 8), :] for k in range(20)], axis=0)
            for b in (0, 1):
                xbuf[pl.ds(b, 160, stride=2), :] = e1

        def correct0():
            def body(i, c):
                e = xbuf[pl.ds(pl.multiple_of(i * 16, 16), 16), :]
                for t in (0, 1):
                    for k in (0, 1):
                        row = pl.ds(vrow(t, 8 + 2 * i + k), 16)
                        x[row, :] = x[row, :] + e
                return c

            lax.fori_loop(0, 20, body, 0, unroll=10)

        wait_r1(pk, rp, sl, rs, cyc)
        stage("unpack0", lambda: unpack0(src, ns, rp, rs, x))
        if cyc == 0:
            stage("screens1", screens1)
        stage("sweep0pre", lambda: sweep0(x, y, src, 2, 52, 26))
        sweep0(y, x, src, 2, 52, 26)
        stage("defect0", defect0)
        stage("restrict0", lambda: restrict0(l1b))
        stage("start1", start1)
        stage("sweep1", lambda: sweep1(l1v, l1w))
        sweep1(l1w, l1v)
        stage("pack1", pack1)
        stage("defect1", defect1)
        stage("down1", down1)
        each_r2("start", mud, mlr, rt, cyc)
        each_r2("wait_recv", mud, mlr, rt, cyc)
        stage("unpack2", unpack2)
        if cyc == 0:
            stage("screens3", screens3)
        stage("down2", down2)
        stage("solve3", lambda: solve3(restrict2()))
        stage("up2", up2)
        stage("correct1", correct1)
        sweep1(l1v, l1w)
        sweep1(l1w, l1v)
        sweep1(l1v, l1w)
        stage("up1", up1)
        stage("correct0", correct0)
        stage("sweep0post", lambda: sweep0(x, y, src, 8, 40, 20))
        sweep0(y, x, src, 10, 36, 18)
        sweep0(x, y, src, 10, 36, 18)

    def restrict2():
        parts = [
            l2e[pl.ds(z * 40 + 8, 16, stride=2), :] + l2e[pl.ds(z * 40 + 9, 16, stride=2), :]
            for z in range(2)
        ]
        return dot_split(jnp.concatenate(parts, axis=0), t23[...])

    def solve3(b3):
        up_ok = jnp.where((sub8 & 3) != 0, 0.125, 0.0)
        down_ok = jnp.where((sub8 & 3) != 3, 0.125, 0.0)
        g = [[l3g[pl.ds(16 * z + 8 * k, 8), :] for k in (0, 1)] for z in (0, 1)]
        b = [[b3[16 * z + 8 * k : 16 * z + 8 * k + 8] for k in (0, 1)] for z in (0, 1)]
        ml, mr = [l3m[0, 0], l3m[0, 1]], [l3m[1, 0], l3m[1, 1]]
        v = [[g[z][k] * b[z][k] for k in (0, 1)] for z in (0, 1)]
        for counter in range(7):
            new = [[None, None], [None, None]]
            for z in (0, 1):
                for k in (0, 1):
                    c = v[z][k]
                    n = 0.125 * v[1 - z][k]
                    n = n + pltpu.roll(c, 1, 0) * up_ok + pltpu.roll(c, 7, 0) * down_ok
                    n = n + pltpu.roll(c, 1, 1) * ml[k] + pltpu.roll(c, 127, 1) * mr[k]
                    new[z][k] = 0.2 * c + g[z][k] * (b[z][k] + n)
            v = new
        e3 = jnp.concatenate([v[0][0], v[0][1], v[1][0], v[1][1]], axis=0)
        e3 = dot_split(e3, p32[...])
        for z in (0, 1):
            for a in (0, 1):
                l2x[pl.ds(z * 32 + a, 16, stride=2), :] = e3[16 * z : 16 * z + 16]

    stage("pack0x2", lambda: pack0(bs1, 2, pk1, sl1))
    pl.semaphore_wait(barrier, expected)
    start_r1(pk1, rp1, sl1, rs1, 0)
    stage("prepare", prepare)
    stage("own_screens", own_screens)

    vcycle(0, bs1, pk1, rp1, sl1, rs1, m1ud, m1lr, rt1, va, vb)

    def halves(a):
        return a[0:8] + a[8:16]

    def apply_first(i, acc):
        r = TOP + 16 * i
        acc = list(acc)

        def put(k, t, c, n):
            row = pl.ds(brow(t, r + k), 16)
            q = (bs1[1, row, :] + 6.0) * c - n
            b2[0, row, :] = q
            acc[0] = acc[0] + halves(bs1[0, row, :] * c)
            acc[1] = acc[1] + halves(c * q)

        stencil0(vb, r, 16, put)
        return tuple(acc)

    sums = lax.fori_loop(0, 2, apply_first, (z8, z8))
    stage("pack0x1", lambda: pack0(b2, 1, pk2, sl2))
    start_r1(pk2, rp2, sl2, rs2, 1)
    ar_begin(0, sums)
    ar_middle(0)

    vcycle(1, b2, pk2, rp2, sl2, rs2, m2ud, m2lr, rt2, va, vc)
    rho0, curv0 = ar_end(0, 2)
    step0 = rho0 / curv0
    step0_16 = jnp.concatenate([step0, step0], axis=0)

    def next_z(i, c):
        for k in (0, 1):
            for t in (0, 1):
                row = pl.ds(vrow(t, TOP - 2 + 2 * i + k), 16)
                vc[row, :] = vb[row, :] - step0_16 * vc[row, :]
        return c

    lax.fori_loop(0, 18, next_z, 0, unroll=9)

    def apply_second(i, acc):
        r = TOP + 16 * i
        acc = list(acc)

        def put(k, t, c, n):
            row = pl.ds(brow(t, r + k), 16)
            q = (bs1[1, row, :] + 6.0) * c - n
            q1[row, :] = q
            q0 = b2[0, row, :]
            z0 = vb[pl.ds(vrow(t, r + k), 16), :]
            acc[0] = acc[0] + halves((bs1[0, row, :] - step0_16 * q0) * c)
            acc[1] = acc[1] + halves(c * q)
            acc[2] = acc[2] + halves(c * q0 + z0 * q)

        stencil0(vc, r, 16, put)
        return tuple(acc)

    sums = lax.fori_loop(0, 2, apply_second, (z8, z8, z8))
    ar_begin(1, sums)
    ar_middle(1)
    rho1, zz, cross = ar_end(1, 3)
    beta = rho1 / rho0
    curv1 = zz + beta * (cross + beta * curv0)
    step1 = rho1 / curv1
    mixed = step0 + step1 * beta

    def finish():
        mixed_16 = jnp.concatenate([mixed, mixed], axis=0)
        step1_16 = jnp.concatenate([step1, step1], axis=0)

        def body(i, c):
            sol, app = [], []
            for k in range(8):
                r = TOP + 8 * i + k
                z, q = [], []
                for t in (0, 1):
                    v, b = pl.ds(vrow(t, r), 16), pl.ds(brow(t, r), 16)
                    z.append(mixed_16 * vb[v, :] + step1_16 * vc[v, :])
                    q.append(mixed_16 * b2[0, b, :] + step1_16 * q1[b, :])
                sol.append(jnp.concatenate(z, axis=1))
                app.append(jnp.concatenate(q, axis=1))
            for a, rows in ((0, sol), (1, app)):
                natural[a] = dot_exact(jnp.concatenate(rows, axis=0), merge[...])
            at_rows = pl.ds(pl.multiple_of(8 * i, 8), 8)
            for z in range(16):
                sol_ref[z, at_rows, :] = natural[0, pl.ds(z, 8, stride=16), :]
                res_ref[z, at_rows, :] = (
                    rhs_ref[pl.ds(pl.multiple_of(z * 32 + 8 * i, 8), 8), :]
                    - natural[1, pl.ds(z, 8, stride=16), :]
                )
            return c

        lax.fori_loop(0, 4, body, 0)

    stage("finish", finish)

    sent_r1(pk1, rp1, sl1, rs1, 0)
    sent_r1(pk2, rp2, sl2, rs2, 1)
    each_r2("wait_send", m1ud, m1lr, rt1, 0)
    each_r2("wait_send", m2ud, m2lr, rt2, 1)
    for cyc in (0, 1):
        for i in range(22):
            ar_copy(cyc, i).wait_send()


def on_device(right_side, screening, owners):
    vm = lambda *s: pltpu.VMEM(s, F32)
    bm = lambda *s: pltpu.VMEM(s, BF16)
    padded = 8 + 2 * ROWS * PITCH + 8
    scratch = [
        vm(512, 128), vm(512, 128), pltpu.SMEM(owners.shape, jnp.int32),
        pltpu.SemaphoreType.DMA((3,)),
        vm(2, 2 * PLANE, 128), vm(1, 2 * PLANE, 128), vm(2 * PLANE, 128),
        vm(padded, 128), vm(padded, 128), vm(padded, 128), vm(2 * PLANE, 128),
        vm(2, 2, 64, 128), vm(2, 1, 64, 128), vm(3, 2, 2, 64, 128), vm(3, 2, 1, 64, 128),
        vm(2, 2, HALO * 16, 128), vm(2, 1, HALO * 16, 128), vm(2, 2, HALO * 16, 128), vm(2, 1, HALO * 16, 128),
        vm(24 * 16, 128), vm(20 * 16, 128), vm(2, 128, 128),
        vm(R1 * 8, 128), vm(R1 * 8, 128), vm(R1 * 8, 128), vm(R1 * 8, 128),
        vm(R1 * 16 + 16, 128), vm(R1 * 16 + 16, 128), vm(128, 128),
        vm(2, 8, 8, 128), vm(2, 4, 8, 128), vm(2, 8, 8, 128), vm(2, 4, 8, 128),
        vm(5, 3, 8, 8, 128), vm(5, 3, 8, 8, 128),
        vm(160, 128), vm(160, 128), vm(160, 128), vm(4 * 56, 128), vm(4 * 56, 128),
        vm(80, 128), vm(64, 128), vm(32, 128), vm(2, 2, 8, 128),
        bm(128, 256), bm(256, 128), bm(512, 128), bm(384, 512), bm(128, 128), bm(128, 128), bm(128, 128),
        vm(2, 2, 1, 128), vm(2, 7, 1, 128), vm(2, 15, 1, 128),
        pltpu.SemaphoreType.DMA((2, 8)), pltpu.SemaphoreType.DMA((2, 8)),
        pltpu.SemaphoreType.DMA((2, 14)), pltpu.SemaphoreType.DMA((2, 14)),
        pltpu.SemaphoreType.DMA((2, 22)), pltpu.SemaphoreType.DMA((2, 22)),
    ]
    block = jax.ShapeDtypeStruct(right_side.shape, F32)
    vmem = pl.BlockSpec(memory_space=pltpu.VMEM)
    return tuple(
        pl.pallas_call(
            kernel,
            out_shape=(block, block),
            in_specs=[pl.BlockSpec(memory_space=pl.ANY)] * 3,
            out_specs=(vmem, vmem),
            scratch_shapes=scratch,
            compiler_params=pltpu.CompilerParams(
                collective_id=0, has_side_effects=True, vmem_limit_bytes=60 * 2**20
            ),
        )(right_side.reshape(512, 128), screening.reshape(512, 128), owners)
    )


def solution(mesh):
    spec = P(None, "tx", "ty")
    return jax.shard_map(
        on_device, mesh=mesh, in_specs=(spec, spec, P("tx", None)), out_specs=(spec, spec),
        check_vma=False,
    )
```

```python
import functools

import jax
import jax.numpy as jnp
from jax import lax
from jax.experimental import pallas as pl
from jax.experimental.pallas import tpu as pltpu
from jax.sharding import PartitionSpec as P

MESH = pl.DeviceIdType.MESH
F32 = jnp.float32
BF16 = jnp.bfloat16

NTX, NTY = 8, 16
HALO = 11
ROWS = 56
TOP = 12
PLANE = ROWS * 16
PITCH = 24
R1 = 32
DIRS8 = [(-1, -1), (1, -1), (-1, 1), (1, 1), (0, -1), (0, 1), (-1, 0), (1, 0)]
DIRS14 = [(-2, -1), (2, -1), (-2, 1), (2, 1)] + DIRS8[:6] + [(-2, 0), (2, 0), (-1, 0), (1, 0)]


def iota(shape, axis):
    return lax.broadcasted_iota(jnp.int32, shape, axis)


def dot_split(x, table):
    high = x.astype(BF16).astype(F32)
    parts = jnp.concatenate([high, x - high], axis=0).astype(BF16)
    out = jnp.dot(parts, table, preferred_element_type=F32)
    return out[: x.shape[0]] + out[x.shape[0] :]


def dot_exact(x, table):
    high = x.astype(BF16).astype(F32)
    middle = (x - high).astype(BF16).astype(F32)
    parts = jnp.concatenate([high, middle, x - high - middle], axis=0).astype(BF16)
    out = jnp.dot(parts, table, preferred_element_type=F32)
    n = x.shape[0]
    return out[:n] + (out[n : 2 * n] + out[2 * n :])


def kernel(
    rhs_hbm, scr_hbm, own_hbm, sol_ref, res_ref,
    rhs_ref, scr_ref, own_ref, s_in,
    bs1, b2, gain, va, vb, vc, q1, pk1, pk2, rp1, rp2, sl1, sl2, rs1, rs2, ebuf, xbuf, natural,
    l1s, l1g, l1b, l1x, l1v, l1w, l1e,
    tb1, tb2, sd1, sd2, st1, st2, rt1, rt2, rd1, rd2, rx1, rx2,
    l2b, l2s, l2g, l2v, l2w, l2e, l2x, l3g, l3m,
    split, merge, t12, t23, p32, p21,
    arbuf, arr1, arr2,
    s_r1, r_r1, s_r2, r_r2, s_ar, r_ar,
):
    tx = lax.axis_index("tx")
    ty = lax.axis_index("ty")
    zero = lax.div(tx, 64)
    barrier = pltpu.get_barrier_semaphore()
    loads = [
        pltpu.make_async_copy(rhs_hbm, rhs_ref, s_in.at[0]),
        pltpu.make_async_copy(scr_hbm, scr_ref, s_in.at[1]),
        pltpu.make_async_copy(own_hbm, own_ref, s_in.at[2]),
    ]
    for load in loads:
        load.start()

    def inside(dx, dy):
        a, b = tx + dx, ty + dy
        return (a >= 0) & (a < NTX) & (b >= 0) & (b < NTY)

    def at(dx, dy):
        return {"tx": tx + dx, "ty": ty + dy}

    def ring(dx, dy):
        return {"tx": lax.rem(tx + dx, NTX), "ty": lax.rem(ty + dy, NTY)}

    ring_dirs = [(k, 0) for k in range(1, NTX)] + [(0, k) for k in range(1, NTY)]
    extra = [d for d in DIRS14 if d[0] != 0 and d[1] != 0]
    expected = jnp.int32(len(ring_dirs))
    for d in ring_dirs:
        pl.semaphore_signal(barrier, inc=1, device_id=ring(*d), device_id_type=MESH)
    for d in extra:
        ok = inside(*d)
        expected = expected + ok.astype(jnp.int32)

        @pl.when(ok)
        def _():
            pl.semaphore_signal(barrier, inc=1, device_id=at(*d), device_id_type=MESH)

    lane16 = iota((16, 128), 1)
    lane8 = iota((8, 128), 1)
    sub8 = iota((8, 128), 0)
    grp8 = lane8 >> 4
    quarter = lane8 >> 5
    half16 = lane16 >> 3
    own16 = (lane16 >= 32) & (lane16 < 96)
    own8 = (lane8 >= 32) & (lane8 < 96)
    side16 = ((lane16 >= 24) & (lane16 < 32)) | ((lane16 >= 96) & (lane16 < 104))
    side8 = ((lane8 >= 16) & (lane8 < 32)) | ((lane8 >= 96) & (lane8 < 112))
    z16 = jnp.zeros((16, 128), F32)
    z8 = jnp.zeros((8, 128), F32)

    def vrow(t, r):
        return pl.multiple_of(8 + (t * ROWS + r) * PITCH, 8)

    def brow(t, r):
        return pl.multiple_of((t * ROWS + r) * 16, 16)

    def stage(name, fn):
        fn()

    def take_inputs():
        for a, ref in enumerate((rhs_ref, scr_ref)):
            for i in range(2):
                x = [ref[pl.ds(16 * i + k, 16, stride=32), :] for k in range(16)]
                x = dot_exact(jnp.concatenate(x, axis=0), split[...])
                for t in (0, 1):
                    at_row = (t * ROWS + TOP + 16 * i) * 16
                    bs1[a, pl.ds(at_row, 256), :] = x[:, 128 * t : 128 * t + 128]

    def pack0(src, count, pk, sl):
        for j in range(4):
            span = pl.ds(pl.multiple_of(j * 16, 16), 16)
            for a in range(count):
                left, right = z16, z16
                for g in range(8):
                    even = src[a, pl.ds(brow(0, TOP + j * 8 + g), 16), :]
                    odd = src[a, pl.ds(brow(1, TOP + j * 8 + g), 16), :]
                    even = pltpu.roll(even, (16 * g - 88) % 128, 1)
                    odd = pltpu.roll(odd, (16 * g - 80) % 128, 1)
                    right = jnp.where(half16 == 2 * g, even, jnp.where(half16 == 2 * g + 1, odd, right))
                    left = jnp.where(
                        half16 == (2 * g - 7) % 16, even,
                        jnp.where(half16 == (2 * g - 6) % 16, odd, left),
                    )
                pk[0, a, span, :] = left
                pk[1, a, span, :] = right
        for a in range(count):
            for m, first in ((0, TOP), (1, TOP + 32 - HALO)):
                for k in range(HALO):
                    even = src[a, pl.ds(brow(0, first + k), 16), :]
                    odd = src[a, pl.ds(brow(1, first + k), 16), :]
                    sl[m, a, pl.ds(16 * k, 16), :] = jnp.where(own16, even, pltpu.roll(odd, 64, 1))

    def unpack0(dst, count, rp, rs, x):
        def row(dxi, j, g):
            r = TOP + (dxi - 1) * 32 + j * 8 + g
            span = pl.ds(pl.multiple_of(j * 16, 16), 16)
            out = []
            for a in range(count):
                fl, fr = rp[dxi, 0, a, span, :], rp[dxi, 1, a, span, :]
                if dxi == 1:
                    even, odd = dst[a, pl.ds(brow(0, r), 16), :], dst[a, pl.ds(brow(1, r), 16), :]
                else:
                    k = j * 8 + g - (32 - HALO if dxi == 0 else 0)
                    both = rs[dxi // 2, a, pl.ds(16 * k, 16), :]
                    even, odd = jnp.where(own16, both, 0.0), jnp.where(own16, pltpu.roll(both, 64, 1), 0.0)
                ve = pltpu.roll(jnp.where(half16 == 2 * g, fl, fr), (24 - 16 * g) % 128, 1)
                vo = pltpu.roll(jnp.where(half16 == 2 * g + 1, fl, fr), (16 - 16 * g) % 128, 1)
                even, odd = jnp.where(side16, ve, even), jnp.where(side16, vo, odd)
                dst[a, pl.ds(brow(0, r), 16), :] = even
                dst[a, pl.ds(brow(1, r), 16), :] = odd
                out.append((even, odd))
            for t in (0, 1):
                at_row = pl.ds(brow(t, r), 16)
                if count == 2:
                    s = out[1][t]
                    gv = jnp.where(s > 0.0, 0.8 / (s + 6.0), 0.0)
                    gain[at_row, :] = gv
                else:
                    gv = gain[at_row, :]
                x[pl.ds(vrow(t, r), 16), :] = gv * out[0][t]

        for j in range(4):
            for g in range(8):
                row(1, j, g)
        for j, groups in ((2, range(5, 8)), (3, range(8))):
            for g in groups:
                row(0, j, g)
        for j, groups in ((0, range(8)), (1, range(3))):
            for g in groups:
                row(2, j, g)

    def r1_copy(i, d, pk, rp, sl, rs, cyc):
        dx, dy = d
        if dy == 0:
            s, t = sl.at[0 if dx == -1 else 1], rs.at[1 if dx == -1 else 0]
        else:
            side = 0 if dy == -1 else 1
            if dx == 0:
                s, t = pk.at[side], rp.at[1, 1 - side]
            elif dx == -1:
                s, t = pk.at[side, :, pl.ds(0, 32)], rp.at[2, 1 - side, :, pl.ds(0, 32)]
            else:
                s, t = pk.at[side, :, pl.ds(32, 32)], rp.at[0, 1 - side, :, pl.ds(32, 32)]
        return pltpu.make_async_remote_copy(
            src_ref=s, dst_ref=t, send_sem=s_r1.at[cyc, i], recv_sem=r_r1.at[cyc, i],
            device_id=at(*d), device_id_type=MESH,
        )

    def start_r1(pk, rp, sl, rs, cyc):
        for i, d in enumerate(DIRS8):
            @pl.when(inside(*d))
            def _():
                r1_copy(i, d, pk, rp, sl, rs, cyc).start()

    def wait_r1(pk, rp, sl, rs, cyc):
        for i, d in enumerate(DIRS8):
            @pl.when(inside(-d[0], -d[1]))
            def _():
                r1_copy(i, d, pk, rp, sl, rs, cyc).wait_recv()

    def sent_r1(pk, rp, sl, rs, cyc):
        for i, d in enumerate(DIRS8):
            @pl.when(inside(*d))
            def _():
                r1_copy(i, d, pk, rp, sl, rs, cyc).wait_send()

    def clear_r1(src, count, rp, rs):
        for a in range(count):
            for t in (0, 1):
                for r in (0, ROWS - 1):
                    src[a, pl.ds(brow(t, r), 16), :] = z16
        for i, dx in ((0, -1), (1, 1)):
            @pl.when(jnp.logical_not(inside(dx, 0)))
            def _():
                rs[i] = jnp.zeros((count, HALO * 16, 128), F32)
        for dxi in range(3):
            for sidei, dy in ((0, -1), (1, 1)):
                @pl.when(jnp.logical_not(inside(dxi - 1, dy)))
                def _():
                    rp[dxi, sidei] = jnp.zeros((count, 64, 128), F32)

    def r2_copy(i, d, bufs, cyc):
        tb, sd, st, rt, rd, rx = bufs
        dx, dy = d
        if i < 14:
            s, t = tb.at[1 + dy], rt.at[2 - dx, 1 - dy]
        elif dy == 0:
            s, t = sd.at[0 if dx < 0 else 1], rd.at[1 if dx < 0 else 0]
        else:
            side = 0 if dy < 0 else 1
            s, t = st.at[side], rx.at[1 - dx, 1 - side]
        return pltpu.make_async_remote_copy(
            src_ref=s, dst_ref=t, send_sem=s_r2.at[cyc, i], recv_sem=r_r2.at[cyc, i],
            device_id=at(*d), device_id_type=MESH,
        )

    def each_r2(op, part, bufs, cyc):
        for i, d in enumerate(DIRS14) if part == 0 else enumerate(DIRS8, 14):
            @pl.when(inside(-d[0], -d[1]) if op == "wait_recv" else inside(*d))
            def _():
                getattr(r2_copy(i, d, bufs, cyc), op)()

    def clear_r2(rt, rd, rx):
        for dx, dy in DIRS14:
            @pl.when(jnp.logical_not(inside(dx, dy)))
            def _():
                rt[2 + dx, 1 + dy] = jnp.zeros(rt.shape[2:], F32)
                if abs(dx) <= 1:
                    if dy == 0:
                        rd[(dx + 1) // 2] = jnp.zeros(rd.shape[1:], F32)
                    else:
                        rx[1 + dx, (dy + 1) // 2] = jnp.zeros(rx.shape[2:], F32)

    def ar_copy(cyc, i):
        if i < 7:
            d, s, t = ring(i + 1, 0), arbuf.at[cyc, 0], arr1.at[cyc, i]
        else:
            d, s, t = ring(0, i - 6), arbuf.at[cyc, 1], arr2.at[cyc, i - 7]
        return pltpu.make_async_remote_copy(
            src_ref=s, dst_ref=t, send_sem=s_ar.at[cyc, i], recv_sem=r_ar.at[cyc, i],
            device_id=d, device_id_type=MESH,
        )

    def ar_begin(cyc, rows):
        out = jnp.zeros((1, 128), F32)
        for k, acc in enumerate(rows):
            acc = jnp.sum(jnp.where(own8, acc, 0.0), axis=0, keepdims=True)
            out = jnp.where(lane8[:1] == k, jnp.sum(acc, axis=1, keepdims=True), out)
        arbuf[cyc, 0] = out
        for i in range(7):
            ar_copy(cyc, i).start()

    def ar_middle(cyc):
        total = arbuf[cyc, 0]
        for i in range(7):
            ar_copy(cyc, i).wait_recv()
        for i in range(7):
            total = total + arr1[cyc, i]
        arbuf[cyc, 1] = total
        for i in range(7, 22):
            ar_copy(cyc, i).start()
        if cyc == 1:
            for i in range(7):
                ar_copy(cyc, i).wait_send()

    def ar_end(cyc, count):
        total = arbuf[cyc, 1]
        for i in range(7, 22):
            ar_copy(cyc, i).wait_recv()
        for i in range(15):
            total = total + arr2[cyc, i]
        return [jnp.broadcast_to(total[:, k : k + 1], (8, 128)) for k in range(count)]

    def stencil0(src, r, count, put):
        rows = [
            [src[pl.ds(vrow(t, r + k - 1), 16), :] for k in range(count + 2)] for t in (0, 1)
        ]
        for k in range(count):
            even, odd = rows[0][k + 1], rows[1][k + 1]
            beside = (odd + pltpu.roll(odd, 1, 1), even + pltpu.roll(even, 127, 1))
            for t in (0, 1):
                at_row = vrow(t, r + k)
                n = rows[t][k] + rows[t][k + 2]
                n = n + (src[pl.ds(at_row - 1, 16), :] + src[pl.ds(at_row + 1, 16), :])
                put(k, t, rows[t][k + 1], n + beside[t])

    def sweep0(src, dst, bref, r0, count, per):
        def body(i, carry):
            r = r0 + per * i

            def put(k, t, c, n):
                row = pl.ds(brow(t, r + k), 16)
                dst[pl.ds(vrow(t, r + k), 16), :] = 0.2 * c + gain[row, :] * (bref[0, row, :] + n)

            stencil0(src, r, per, put)
            return carry

        lax.fori_loop(0, count // per, body, 0)

    def restrict0(out):
        x = ebuf[pl.ds(0, 192, stride=2), :] + ebuf[pl.ds(1, 192, stride=2), :]
        out[pl.ds(32, 192), :] = 0.125 * x

    def wrow(r):
        return pl.multiple_of(8 + r * 16, 8)

    def stencil1(src, r, count, put):
        rows = [src[pl.ds(wrow(r + k - 1), 8), :] for k in range(count + 2)]
        for k in range(count):
            c = rows[k + 1]
            n = rows[k] + rows[k + 2]
            n = n + (src[pl.ds(wrow(r + k) - 1, 8), :] + src[pl.ds(wrow(r + k) + 1, 8), :])
            n = n + (pltpu.roll(c, 1, 1) + pltpu.roll(c, 127, 1))
            put(k, c, n)

    def sweep1(src, dst):
        def put(k, c, n):
            row = pl.ds((4 + k) * 8, 8)
            dst[pl.ds(wrow(4 + k + zero), 8), :] = 0.2 * c + l1g[row, :] * (l1b[row, :] + 0.5 * n)

        stencil1(src, 4 + zero, 24, put)

    def restrict1():
        parts = []
        for z in range(4):
            x = l1e[pl.ds(2 * z, 8, stride=16), :] + l1e[pl.ds(2 * z + 1, 8, stride=16), :]
            x = x + l1e[pl.ds(2 * z + 8, 8, stride=16), :] + l1e[pl.ds(2 * z + 9, 8, stride=16), :]
            parts.append(x)
        return dot_split(jnp.concatenate(parts, axis=1), t12[...])

    def base2(z, k):
        return z * 56 + 8 + 8 * k + zero

    def stencil2(src, z, k):
        c = src[pl.ds(base2(z, k), 8), :]
        n = src[pl.ds(base2(z, k) - 1, 8), :] + src[pl.ds(base2(z, k) + 1, 8), :]
        if z > 0:
            n = n + src[pl.ds(base2(z - 1, k), 8), :]
        if z < 3:
            n = n + src[pl.ds(base2(z + 1, k), 8), :]
        return c, n + (pltpu.roll(c, 1, 1) + pltpu.roll(c, 127, 1))

    def sweep2(src, dst, tiles):
        for z in range(4):
            for k in tiles:
                c, n = stencil2(src, z, k)
                row = pl.ds(z * 40 + 8 * k, 8)
                dst[pl.ds(base2(z, k), 8), :] = 0.2 * c + l2g[row, :] * (l2b[row, :] + 0.25 * n)

    def table(ref, rows, cols, value, f):
        ref[...] = jnp.where(f(iota((rows, cols), 0), iota((rows, cols), 1)), value, 0.0).astype(BF16)

    def prepare():
        tables()
        zeros()

    def tables():
        table(merge, 256, 128, 1.0, lambda i, o: ((i & 127) - 32 == o >> 1) & ((i >> 7) == (o & 1)))
        table(t12, 512, 128, 0.125, lambda i, o: (((i & 127) - 32) >> 1 == (o & 31)) & ((i >> 7) == (o >> 5)))
        table(t23, 128, 128, 0.125, lambda i, o: ((i - 48) >> 1) == o - 56)
        table(p32, 128, 128, 1.0, lambda i, o: ((o - 48) >> 1) == i - 56)
        table(p21, 128, 128, 1.0, lambda i, o: ((o - 32) >> 1) == i - 48)

    def zeros():
        def clear_pads(i, c):
            for ref in (va, vb, vc):
                ref[pl.ds(pl.multiple_of(i * PITCH, 8), 8), :] = z8
            return c

        lax.fori_loop(0, 2 * ROWS + 1, clear_pads, 0)
        for ref in (vb, vc):
            for t in (0, 1):
                for r in (0, 1, ROWS - 2, ROWS - 1):
                    ref[pl.ds(vrow(t, r), 16), :] = z16
        for ref in (l1v, l1w):
            ref[...] = jnp.zeros(ref.shape, F32)
        for ref in (l1s, l1g, l1b):
            ref[...] = jnp.zeros(ref.shape, F32)
        for ref in (l2v, l2w):
            ref[...] = jnp.zeros(ref.shape, F32)
        clear_r1(bs1, 2, rp1, rs1)
        clear_r1(b2, 1, rp2, rs2)
        clear_r2(rt1, rd1, rx1)
        clear_r2(rt2, rd2, rx2)

    table(split, 128, 256, 1.0, lambda i, o: ((o & 127) - 32 == i >> 1) & ((o >> 7) == (i & 1)))
    for load in loads:
        load.wait()
    stage("take_inputs", take_inputs)
    here = own_ref[0, ty]
    link_l = jnp.where(own_ref[0, jnp.maximum(ty - 1, 0)] == here, 1.0, 0.0)
    link_r = jnp.where(own_ref[0, jnp.minimum(ty + 1, NTY - 1)] == here, 1.0, 0.0)
    link = jnp.where(lane8 == 56, link_l, jnp.where(lane8 == 72, link_r, 1.0))

    bufs1 = (tb1, sd1, st1, rt1, rd1, rx1)
    bufs2 = (tb2, sd2, st2, rt2, rd2, rx2)

    def screen_sums(first, count):
        for i in range(first, first + count):
            even = bs1[1, pl.ds(brow(0, 4 + 2 * i), 32), :]
            odd = bs1[1, pl.ds(brow(1, 4 + 2 * i), 32), :]
            x = even + odd
            ebuf[pl.ds(i * 16, 16), :] = x[:16] + x[16:]

    def put_tile(tb, a, x):
        tb[0, a] = pltpu.roll(x, 32, 1)
        tb[1, a] = x
        tb[2, a] = pltpu.roll(x, 96, 1)

    def own_screens():
        screen_sums(4, 16)
        x = ebuf[pl.ds(64, 128, stride=2), :] + ebuf[pl.ds(65, 128, stride=2), :]
        l1e[...] = 0.125 * x
        s2_own = restrict1()
        put_tile(tb1, 1, s2_own)
        for m in range(3):
            tb1[m, 2] = link
        rt1[2, 1, 1] = s2_own

    def vcycle(cyc, src, pk, rp, sl, rs, bufs, x, y):
        ns = 2 - cyc
        tb, sd, st, rt, rd, rx = bufs

        def screens1():
            screen_sums(0, 24)
            restrict0(l1s)
            s = l1s[...]
            l1g[...] = jnp.where(s > 0.0, 0.8 / (s + 3.0), 0.0)

        def defect0():
            per = 48

            def body(i, c):
                r = 4 + per * i
                held = []

                def put(k, t, centre, n):
                    row = pl.ds(brow(t, r + k), 16)
                    held.append(src[0, row, :] - (bs1[1, row, :] + 6.0) * centre + n)
                    if len(held) == 4:
                        at_row = pl.multiple_of((i * (per // 2) + k // 2) * 16, 16)
                        ebuf[pl.ds(at_row, 16), :] = (held[0] + held[1]) + (held[2] + held[3])
                        held.clear()

                stencil0(x, r, per, put)
                return c

            lax.fori_loop(0, 48 // per, body, 0)

        def start1():
            for r in range(4, 28):
                row = pl.ds(r * 8, 8)
                l1v[pl.ds(wrow(r), 8), :] = l1g[row, :] * l1b[row, :]

        def defect1():
            def put(k, centre, n):
                row = pl.ds((8 + k) * 8, 8)
                l1e[pl.ds(k * 8, 8), :] = l1b[row, :] - (l1s[row, :] + 3.0) * centre + 0.5 * n

            stencil1(l1v, 8 + zero, 16, put)

        def pack1():
            for m in (0, 1):
                for k in range(5):
                    sd[m, k] = l1v[pl.ds(wrow(8 + k + 11 * m), 8), :]
            for j in (0, 1):
                left, right = z8, z8
                for g in range(8):
                    v = pltpu.roll(l1v[pl.ds(wrow(8 + 8 * j + g), 8), :], (16 * g - 80) % 128, 1)
                    right = jnp.where(grp8 == g, v, right)
                    left = jnp.where(grp8 == (g + 5) % 8, v, left)
                st[0, j] = left
                st[1, j] = right

        def down1():
            b2_own = restrict1()
            put_tile(tb, 0, b2_own)
            rt[2, 1, 0] = b2_own

        def unpack2():
            for a in range(ns):
                for z in range(4):
                    for k in range(5):
                        x = jnp.where(quarter == (z + 3) % 4, rt[k, 0, a], rt[k, 1, a])
                        x = jnp.where(quarter == (z + 1) % 4, rt[k, 2, a], x)
                        x = pltpu.roll(x, (48 - 32 * z) % 128, 1)
                        row = pl.ds(z * 40 + 8 * k, 8)
                        if a == 0:
                            l2b[row, :] = x
                        else:
                            l2s[row, :] = jnp.where((lane8 >= 16) & (lane8 < 112), x, 0.0)

        def screens3():
            s = l2s[...]
            l2g[...] = jnp.where(s > 0.0, 0.8 / (s + 1.5), 0.0)
            for z in range(2):
                l2e[pl.ds(z * 40, 40), :] = (
                    l2s[pl.ds(2 * z * 40, 40), :] + l2s[pl.ds((2 * z + 1) * 40, 40), :]
                )
            s = restrict2()
            l3g[...] = jnp.where(s > 0.0, 0.8 / (s + 0.75), 0.0)
            up, down = rt[1, 1, 2], rt[3, 1, 2]
            for k, m in enumerate((jnp.where(sub8 < 4, up, link), down)):
                l3m[0, k] = 0.125 * m
                l3m[1, k] = pltpu.roll(0.125 * m, 127, 1)

        def down2():
            for z in range(4):
                for k in range(5):
                    row = pl.ds(z * 40 + 8 * k, 8)
                    l2v[pl.ds(base2(z, k), 8), :] = l2g[row, :] * l2b[row, :]
            sweep2(l2v, l2w, range(5))
            sweep2(l2w, l2v, range(5))
            for k in range(5):
                d = []
                for z in range(4):
                    c, n = stencil2(l2v, z, k)
                    row = pl.ds(z * 40 + 8 * k, 8)
                    d.append(l2b[row, :] - (l2s[row, :] + 1.5) * c + 0.25 * n)
                l2e[pl.ds(8 * k, 8), :] = d[0] + d[1]
                l2e[pl.ds(40 + 8 * k, 8), :] = d[2] + d[3]

        def up2():
            for z in range(4):
                for k in (1, 2, 3):
                    row = pl.ds(base2(z, k), 8)
                    l2v[row, :] = l2v[row, :] + l2x[pl.ds((z // 2) * 32 + 8 * (k - 1), 8), :]
            sweep2(l2v, l2w, (1, 2, 3))
            sweep2(l2w, l2v, (1, 2, 3))
            sweep2(l2v, l2w, (1, 2, 3))
            e2 = jnp.concatenate([l2w[pl.ds(z * 56 + 20 + zero, 16), :] for z in range(4)], axis=0)
            e2 = dot_split(e2, p21[...])
            for z in range(4):
                for a in (0, 8):
                    for b in (0, 1):
                        l1x[pl.ds(a + 2 * z + b, 16, stride=16), :] = e2[16 * z : 16 * z + 16]

        def correct1():
            for r in range(3, 29):
                tile, inner = (r - 8) // 16, (r - 8) % 16
                j, g = inner // 8, inner % 8
                v = jnp.where(grp8 == g, rx[1 + tile, 0, j], rx[1 + tile, 1, j])
                v = pltpu.roll(v, (16 - 16 * g) % 128, 1)
                if tile == 0:
                    base = l1v[pl.ds(wrow(r), 8), :]
                elif tile < 0:
                    base = rd[0, inner - 11]
                else:
                    base = rd[1, inner]
                l1v[pl.ds(wrow(r), 8), :] = jnp.where(side8, v, base) + l1x[pl.ds(r * 8, 8), :]

        def up1():
            e1 = jnp.concatenate([l1w[pl.ds(wrow(6 + k), 8), :] for k in range(20)], axis=0)
            for b in (0, 1):
                xbuf[pl.ds(b, 160, stride=2), :] = e1

        def correct0():
            def body(i, c):
                e = xbuf[pl.ds(pl.multiple_of(i * 16, 16), 16), :]
                for t in (0, 1):
                    for k in (0, 1):
                        row = pl.ds(vrow(t, 8 + 2 * i + k), 16)
                        x[row, :] = x[row, :] + e
                return c

            lax.fori_loop(0, 20, body, 0, unroll=20)

        wait_r1(pk, rp, sl, rs, cyc)
        stage("unpack0", lambda: unpack0(src, ns, rp, rs, x))
        if cyc == 0:
            stage("screens1", screens1)
        stage("sweep0pre", lambda: sweep0(x, y, src, 2, 52, 52))
        sweep0(y, x, src, 2, 52, 52)
        stage("defect0", defect0)
        stage("restrict0", lambda: restrict0(l1b))
        stage("start1", start1)
        stage("sweep1", lambda: sweep1(l1v, l1w))
        sweep1(l1w, l1v)
        stage("defect1", defect1)
        stage("down1", down1)
        each_r2("start", 0, bufs, cyc)
        stage("pack1", pack1)
        each_r2("start", 1, bufs, cyc)
        sent_r1(pk, rp, sl, rs, cyc)
        if cyc == 1:
            for part in (0, 1):
                each_r2("wait_send", part, bufs1, 0)
            for i in range(22):
                ar_copy(0, i).wait_send()
        each_r2("wait_recv", 0, bufs, cyc)
        stage("unpack2", unpack2)
        if cyc == 0:
            stage("screens3", screens3)
        stage("down2", down2)
        stage("solve3", lambda: solve3(restrict2()))
        stage("up2", up2)
        each_r2("wait_recv", 1, bufs, cyc)
        stage("correct1", correct1)
        sweep1(l1v, l1w)
        sweep1(l1w, l1v)
        sweep1(l1v, l1w)
        stage("up1", up1)
        stage("correct0", correct0)
        stage("sweep0post", lambda: sweep0(x, y, src, 8, 40, 40))
        sweep0(y, x, src, 10, 36, 36)
        sweep0(x, y, src, 10, 36, 36)

    def restrict2():
        parts = [
            l2e[pl.ds(z * 40 + 8, 16, stride=2), :] + l2e[pl.ds(z * 40 + 9, 16, stride=2), :]
            for z in range(2)
        ]
        return dot_split(jnp.concatenate(parts, axis=0), t23[...])

    def solve3(b3):
        up_ok = jnp.where((sub8 & 3) != 0, 0.125, 0.0)
        down_ok = jnp.where((sub8 & 3) != 3, 0.125, 0.0)
        g = [[l3g[pl.ds(16 * z + 8 * k, 8), :] for k in (0, 1)] for z in (0, 1)]
        b = [[b3[16 * z + 8 * k : 16 * z + 8 * k + 8] for k in (0, 1)] for z in (0, 1)]
        ml, mr = [l3m[0, 0], l3m[0, 1]], [l3m[1, 0], l3m[1, 1]]
        v = [[g[z][k] * b[z][k] for k in (0, 1)] for z in (0, 1)]
        for counter in range(7):
            new = [[None, None], [None, None]]
            for z in (0, 1):
                for k in (0, 1):
                    c = v[z][k]
                    n = 0.125 * v[1 - z][k]
                    n = n + pltpu.roll(c, 1, 0) * up_ok + pltpu.roll(c, 7, 0) * down_ok
                    n = n + pltpu.roll(c, 1, 1) * ml[k] + pltpu.roll(c, 127, 1) * mr[k]
                    new[z][k] = 0.2 * c + g[z][k] * (b[z][k] + n)
            v = new
        e3 = jnp.concatenate([v[0][0], v[0][1], v[1][0], v[1][1]], axis=0)
        e3 = dot_split(e3, p32[...])
        for z in (0, 1):
            for a in (0, 1):
                l2x[pl.ds(z * 32 + a, 16, stride=2), :] = e3[16 * z : 16 * z + 16]

    stage("pack0x2", lambda: pack0(bs1, 2, pk1, sl1))
    pl.semaphore_wait(barrier, expected)
    start_r1(pk1, rp1, sl1, rs1, 0)
    stage("prepare", prepare)
    stage("own_screens", own_screens)

    def merged(i, planes, start):
        def body(j, c):
            rows = []
            for k in range(16):
                r = TOP + 16 * j + k
                rows.append(jnp.concatenate([planes[pl.ds(start(t, r), 16), :] for t in (0, 1)], axis=1))
            x = dot_exact(jnp.concatenate(rows, axis=0), merge[...])
            for k in range(16):
                natural[i, pl.ds(16 * j + k, 16, stride=32), :] = x[16 * k : 16 * k + 16]
            return c

        lax.fori_loop(0, 2, body, 0)

    vcycle(0, bs1, pk1, rp1, sl1, rs1, bufs1, va, vb)

    def halves(a):
        return a[0:8] + a[8:16]

    def apply_first(i, acc):
        r = TOP + 32 * i
        acc = list(acc)

        def put(k, t, c, n):
            row = pl.ds(brow(t, r + k), 16)
            q = (bs1[1, row, :] + 6.0) * c - n
            b2[0, row, :] = q
            acc[0] = acc[0] + halves(bs1[0, row, :] * c)
            acc[1] = acc[1] + halves(c * q)

        stencil0(vb, r, 32, put)
        return tuple(acc)

    sums = lax.fori_loop(0, 1, apply_first, (z8, z8))
    stage("pack0x1", lambda: pack0(b2, 1, pk2, sl2))
    start_r1(pk2, rp2, sl2, rs2, 1)
    ar_begin(0, sums)
    stage("merged", lambda: merged(0, vb, vrow))
    merged(1, b2.at[0], brow)
    ar_middle(0)

    vcycle(1, b2, pk2, rp2, sl2, rs2, bufs2, va, vc)
    rho0, curv0 = ar_end(0, 2)
    step0 = rho0 / curv0
    step0_16 = jnp.concatenate([step0, step0], axis=0)

    def next_z(i, c):
        for k in (0, 1):
            for t in (0, 1):
                row = pl.ds(vrow(t, TOP - 2 + 2 * i + k), 16)
                vc[row, :] = vb[row, :] - step0_16 * vc[row, :]
        return c

    lax.fori_loop(0, 18, next_z, 0, unroll=18)

    def apply_second(i, acc):
        r = TOP + 32 * i
        acc = list(acc)

        def put(k, t, c, n):
            row = pl.ds(brow(t, r + k), 16)
            q = (bs1[1, row, :] + 6.0) * c - n
            q1[row, :] = q
            q0 = b2[0, row, :]
            z0 = vb[pl.ds(vrow(t, r + k), 16), :]
            acc[0] = acc[0] + halves((bs1[0, row, :] - step0_16 * q0) * c)
            acc[1] = acc[1] + halves(c * q)
            acc[2] = acc[2] + halves(c * q0 + z0 * q)

        stencil0(vc, r, 32, put)
        return tuple(acc)

    sums = lax.fori_loop(0, 1, apply_second, (z8, z8, z8))
    ar_begin(1, sums)
    merged(2, vc, vrow)
    merged(3, q1, brow)
    ar_middle(1)
    rho1, zz, cross = ar_end(1, 3)
    beta = rho1 / rho0
    curv1 = zz + beta * (cross + beta * curv0)
    step1 = rho1 / curv1
    mixed = step0 + step1 * beta

    for k in range(0, 512, 8):
        row = pl.ds(k, 8)
        sol_ref[row, :] = mixed * natural[0, row, :] + step1 * natural[2, row, :]
        res_ref[row, :] = rhs_ref[row, :] - mixed * natural[1, row, :] - step1 * natural[3, row, :]

    for part in (0, 1):
        each_r2("wait_send", part, bufs2, 1)
    for i in range(7, 22):
        ar_copy(1, i).wait_send()


def on_device(right_side, screening, owners):
    vm = lambda *s: pltpu.VMEM(s, F32)
    bm = lambda *s: pltpu.VMEM(s, BF16)
    padded = 8 + 2 * ROWS * PITCH + 8
    scratch = [
        vm(512, 128), vm(512, 128), pltpu.SMEM(owners.shape, jnp.int32),
        pltpu.SemaphoreType.DMA((3,)),
        vm(2, 2 * PLANE, 128), vm(1, 2 * PLANE, 128), vm(2 * PLANE, 128),
        vm(padded, 128), vm(padded, 128), vm(padded, 128), vm(2 * PLANE, 128),
        vm(2, 2, 64, 128), vm(2, 1, 64, 128), vm(3, 2, 2, 64, 128), vm(3, 2, 1, 64, 128),
        vm(2, 2, HALO * 16, 128), vm(2, 1, HALO * 16, 128), vm(2, 2, HALO * 16, 128), vm(2, 1, HALO * 16, 128),
        vm(24 * 16, 128), vm(20 * 16, 128), vm(4, 512, 128),
        vm(R1 * 8, 128), vm(R1 * 8, 128), vm(R1 * 8, 128), vm(R1 * 8, 128),
        vm(R1 * 16 + 16, 128), vm(R1 * 16 + 16, 128), vm(128, 128),
        vm(3, 3, 8, 128), vm(3, 1, 8, 128), vm(2, 5, 8, 128), vm(2, 5, 8, 128), vm(2, 2, 8, 128), vm(2, 2, 8, 128),
        vm(5, 3, 3, 8, 128), vm(5, 3, 1, 8, 128), vm(2, 5, 8, 128), vm(2, 5, 8, 128),
        vm(3, 2, 2, 8, 128), vm(3, 2, 2, 8, 128),
        vm(160, 128), vm(160, 128), vm(160, 128), vm(4 * 56, 128), vm(4 * 56, 128),
        vm(80, 128), vm(64, 128), vm(32, 128), vm(2, 2, 8, 128),
        bm(128, 256), bm(256, 128), bm(512, 128), bm(128, 128), bm(128, 128), bm(128, 128),
        vm(2, 2, 1, 128), vm(2, 7, 1, 128), vm(2, 15, 1, 128),
        pltpu.SemaphoreType.DMA((2, 8)), pltpu.SemaphoreType.DMA((2, 8)),
        pltpu.SemaphoreType.DMA((2, 22)), pltpu.SemaphoreType.DMA((2, 22)),
        pltpu.SemaphoreType.DMA((2, 22)), pltpu.SemaphoreType.DMA((2, 22)),
    ]
    field = pltpu.VMEM((512, 128), F32)
    vmem = pl.BlockSpec(memory_space=pltpu.VMEM)
    hbm = lambda x: pltpu.with_memory_space_constraint(x, pltpu.HBM)
    out = pl.pallas_call(
        kernel,
        out_shape=(field, field),
        in_specs=[pl.BlockSpec(memory_space=pltpu.HBM)] * 3,
        out_specs=(vmem, vmem),
        scratch_shapes=scratch,
        compiler_params=pltpu.CompilerParams(
            collective_id=0, has_side_effects=True, vmem_limit_bytes=40 * 2**20
        ),
    )(hbm(right_side.reshape(512, 128)), hbm(screening.reshape(512, 128)), hbm(owners))
    return tuple(x.reshape(right_side.shape) for x in out)


def solution(mesh):
    spec = P(None, "tx", "ty")
    return jax.shard_map(
        on_device, mesh=mesh, in_specs=(spec, spec, P("tx", None)), out_specs=(spec, spec),
        check_vma=False,
    )
```

```python
import functools

import jax
import jax.numpy as jnp
from jax import lax
from jax.experimental import pallas as pl
from jax.experimental.pallas import tpu as pltpu
from jax.sharding import PartitionSpec as P

MESH = pl.DeviceIdType.MESH
F32 = jnp.float32
BF16 = jnp.bfloat16

NTX, NTY = 8, 16
HALO = 11
ROWS = 56
TOP = 12
PLANE = ROWS * 16
PITCH = 24
R1 = 32
DIRS8 = [(-1, -1), (1, -1), (-1, 1), (1, 1), (0, -1), (0, 1), (-1, 0), (1, 0)]
DIRS14 = [(-2, -1), (2, -1), (-2, 1), (2, 1)] + DIRS8[:6] + [(-2, 0), (2, 0), (-1, 0), (1, 0)]


def iota(shape, axis):
    return lax.broadcasted_iota(jnp.int32, shape, axis)


def dot_split(x, table):
    high = x.astype(BF16).astype(F32)
    parts = jnp.concatenate([high, x - high], axis=0).astype(BF16)
    out = jnp.dot(parts, table, preferred_element_type=F32)
    return out[: x.shape[0]] + out[x.shape[0] :]


def dot_exact(x, table):
    high = x.astype(BF16).astype(F32)
    middle = (x - high).astype(BF16).astype(F32)
    parts = jnp.concatenate([high, middle, x - high - middle], axis=0).astype(BF16)
    out = jnp.dot(parts, table, preferred_element_type=F32)
    n = x.shape[0]
    return out[:n] + (out[n : 2 * n] + out[2 * n :])


def kernel(
    rhs_hbm, scr_hbm, own_hbm, out_ref,
    rhs_ref, scr_ref, own_ref, s_in,
    bs1, b2, gain, va, vb, vc, q1, pk1, pk2, rp1, rp2, sl1, sl2, rs1, rs2, natural,
    l1s, l1g, l1b, l1x, l1v, l1w, l1e,
    tb1, tb2, sd1, sd2, st1, st2, rt1, rt2, rd1, rd2, rx1, rx2,
    l2b, l2s, l2g, l2v, l2w, l2e, l2x, l3g, l3m,
    split, merge, t12, t23, p32, p21,
    arbuf, arr1, arr2,
    s_r1, r_r1, s_r2, r_r2, s_ar, r_ar,
):
    tx = lax.axis_index("tx")
    ty = lax.axis_index("ty")
    zero = lax.div(tx, 64)
    barrier = pltpu.get_barrier_semaphore()
    loads = [
        pltpu.make_async_copy(rhs_hbm, rhs_ref, s_in.at[0]),
        pltpu.make_async_copy(scr_hbm, scr_ref, s_in.at[1]),
        pltpu.make_async_copy(own_hbm, own_ref, s_in.at[2]),
    ]
    for load in loads:
        load.start()

    def inside(dx, dy):
        a, b = tx + dx, ty + dy
        return (a >= 0) & (a < NTX) & (b >= 0) & (b < NTY)

    def at(dx, dy):
        return {"tx": tx + dx, "ty": ty + dy}

    def ring(dx, dy):
        return {"tx": lax.rem(tx + dx, NTX), "ty": lax.rem(ty + dy, NTY)}

    ring_dirs = [(0, k) for k in range(1, NTY)] + [(k, 0) for k in range(1, NTX)]
    extra = [d for d in DIRS14 if d[0] != 0 and d[1] != 0]
    expected = jnp.int32(len(ring_dirs))
    for d in ring_dirs:
        pl.semaphore_signal(barrier, inc=1, device_id=ring(*d), device_id_type=MESH)
    for d in extra:
        ok = inside(*d)
        expected = expected + ok.astype(jnp.int32)

        @pl.when(ok)
        def _():
            pl.semaphore_signal(barrier, inc=1, device_id=at(*d), device_id_type=MESH)

    lane16 = iota((16, 128), 1)
    lane8 = iota((8, 128), 1)
    sub8 = iota((8, 128), 0)
    grp8 = lane8 >> 4
    quarter = lane8 >> 5
    half16 = lane16 >> 3
    own16 = (lane16 >= 32) & (lane16 < 96)
    own8 = (lane8 >= 32) & (lane8 < 96)
    side16 = ((lane16 >= 24) & (lane16 < 32)) | ((lane16 >= 96) & (lane16 < 104))
    side8 = ((lane8 >= 16) & (lane8 < 32)) | ((lane8 >= 96) & (lane8 < 112))
    z16 = jnp.zeros((16, 128), F32)
    z8 = jnp.zeros((8, 128), F32)

    def vrow(t, r):
        return pl.multiple_of(8 + (t * ROWS + r) * PITCH, 8)

    def brow(t, r):
        return pl.multiple_of((t * ROWS + r) * 16, 16)

    def stage(name, fn):
        fn()

    def take_inputs():
        for a, ref in enumerate((rhs_ref, scr_ref)):
            for i in range(2):
                x = [ref[pl.ds(16 * i + k + z, 8, stride=64), :] for k in range(16) for z in (32, 0)]
                x = dot_exact(jnp.concatenate(x, axis=0), split[...])
                for t in (0, 1):
                    at_row = (t * ROWS + TOP + 16 * i) * 16
                    bs1[a, pl.ds(at_row, 256), :] = x[:, 128 * t : 128 * t + 128]

    def pack0(src, count, pk, sl):
        for j in range(4):
            span = pl.ds(pl.multiple_of(j * 16, 16), 16)
            for a in range(count):
                left, right = z16, z16
                for g in range(8):
                    even = src[a, pl.ds(brow(0, TOP + j * 8 + g), 16), :]
                    odd = src[a, pl.ds(brow(1, TOP + j * 8 + g), 16), :]
                    even = pltpu.roll(even, (16 * g - 88) % 128, 1)
                    odd = pltpu.roll(odd, (16 * g - 80) % 128, 1)
                    right = jnp.where(half16 == 2 * g, even, jnp.where(half16 == 2 * g + 1, odd, right))
                    left = jnp.where(
                        half16 == (2 * g - 7) % 16, even,
                        jnp.where(half16 == (2 * g - 6) % 16, odd, left),
                    )
                pk[0, a, span, :] = left
                pk[1, a, span, :] = right
        for a in range(count):
            for m, first in ((0, TOP), (1, TOP + 32 - HALO)):
                for k in range(HALO):
                    even = src[a, pl.ds(brow(0, first + k), 16), :]
                    odd = src[a, pl.ds(brow(1, first + k), 16), :]
                    sl[m, a, pl.ds(16 * k, 16), :] = jnp.where(own16, even, pltpu.roll(odd, 64, 1))

    def unpack0(dst, count, rp, rs, x):
        def row(dxi, j, g):
            r = TOP + (dxi - 1) * 32 + j * 8 + g
            span = pl.ds(pl.multiple_of(j * 16, 16), 16)
            out = []
            for a in range(count):
                fl, fr = rp[dxi, 0, a, span, :], rp[dxi, 1, a, span, :]
                if dxi == 1:
                    even, odd = dst[a, pl.ds(brow(0, r), 16), :], dst[a, pl.ds(brow(1, r), 16), :]
                else:
                    k = j * 8 + g - (32 - HALO if dxi == 0 else 0)
                    both = rs[dxi // 2, a, pl.ds(16 * k, 16), :]
                    even, odd = jnp.where(own16, both, 0.0), jnp.where(own16, pltpu.roll(both, 64, 1), 0.0)
                ve = pltpu.roll(jnp.where(half16 == 2 * g, fl, fr), (24 - 16 * g) % 128, 1)
                vo = pltpu.roll(jnp.where(half16 == 2 * g + 1, fl, fr), (16 - 16 * g) % 128, 1)
                even, odd = jnp.where(side16, ve, even), jnp.where(side16, vo, odd)
                dst[a, pl.ds(brow(0, r), 16), :] = even
                dst[a, pl.ds(brow(1, r), 16), :] = odd
                out.append((even, odd))
            for t in (0, 1):
                at_row = pl.ds(brow(t, r), 16)
                if count == 2:
                    s = out[1][t]
                    gv = jnp.where(s > 0.0, 0.8 / (s + 6.0), 0.0)
                    gain[at_row, :] = gv
                else:
                    gv = gain[at_row, :]
                x[pl.ds(vrow(t, r), 16), :] = gv * out[0][t]

        for j in range(4):
            for g in range(8):
                row(1, j, g)
        for j, groups in ((2, range(5, 8)), (3, range(8))):
            for g in groups:
                row(0, j, g)
        for j, groups in ((0, range(8)), (1, range(3))):
            for g in groups:
                row(2, j, g)

    def r1_copy(i, d, pk, rp, sl, rs, cyc):
        dx, dy = d
        if dy == 0:
            s, t = sl.at[0 if dx == -1 else 1], rs.at[1 if dx == -1 else 0]
        else:
            side = 0 if dy == -1 else 1
            if dx == 0:
                s, t = pk.at[side], rp.at[1, 1 - side]
            elif dx == -1:
                s, t = pk.at[side, :, pl.ds(0, 32)], rp.at[2, 1 - side, :, pl.ds(0, 32)]
            else:
                s, t = pk.at[side, :, pl.ds(32, 32)], rp.at[0, 1 - side, :, pl.ds(32, 32)]
        return pltpu.make_async_remote_copy(
            src_ref=s, dst_ref=t, send_sem=s_r1.at[cyc, i], recv_sem=r_r1.at[cyc, i],
            device_id=at(*d), device_id_type=MESH,
        )

    def start_r1(pk, rp, sl, rs, cyc):
        for i, d in enumerate(DIRS8):
            @pl.when(inside(*d))
            def _():
                r1_copy(i, d, pk, rp, sl, rs, cyc).start()

    def wait_r1(pk, rp, sl, rs, cyc):
        for i, d in enumerate(DIRS8):
            @pl.when(inside(-d[0], -d[1]))
            def _():
                r1_copy(i, d, pk, rp, sl, rs, cyc).wait_recv()

    def sent_r1(pk, rp, sl, rs, cyc):
        for i, d in enumerate(DIRS8):
            @pl.when(inside(*d))
            def _():
                r1_copy(i, d, pk, rp, sl, rs, cyc).wait_send()

    def clear_r1(src, count, rp, rs):
        for a in range(count):
            for t in (0, 1):
                for r in (0, ROWS - 1):
                    src[a, pl.ds(brow(t, r), 16), :] = z16
        for i, dx in ((0, -1), (1, 1)):
            @pl.when(jnp.logical_not(inside(dx, 0)))
            def _():
                rs[i] = jnp.zeros((count, HALO * 16, 128), F32)
        for dxi in range(3):
            for sidei, dy in ((0, -1), (1, 1)):
                @pl.when(jnp.logical_not(inside(dxi - 1, dy)))
                def _():
                    rp[dxi, sidei] = jnp.zeros((count, 64, 128), F32)

    def r2_copy(i, d, bufs, cyc):
        tb, sd, st, rt, rd, rx = bufs
        dx, dy = d
        if i < 14:
            s, t = tb.at[1 + dy], rt.at[2 - dx, 1 - dy]
        elif dy == 0:
            s, t = sd.at[0 if dx < 0 else 1], rd.at[1 if dx < 0 else 0]
        else:
            side = 0 if dy < 0 else 1
            s, t = st.at[side], rx.at[1 - dx, 1 - side]
        return pltpu.make_async_remote_copy(
            src_ref=s, dst_ref=t, send_sem=s_r2.at[cyc, i], recv_sem=r_r2.at[cyc, i],
            device_id=at(*d), device_id_type=MESH,
        )

    def each_r2(op, part, bufs, cyc):
        for i, d in enumerate(DIRS14) if part == 0 else enumerate(DIRS8, 14):
            @pl.when(inside(-d[0], -d[1]) if op == "wait_recv" else inside(*d))
            def _():
                getattr(r2_copy(i, d, bufs, cyc), op)()

    def clear_r2(rt, rd, rx):
        for dx, dy in DIRS14:
            @pl.when(jnp.logical_not(inside(dx, dy)))
            def _():
                rt[2 + dx, 1 + dy] = jnp.zeros(rt.shape[2:], F32)
                if abs(dx) <= 1:
                    if dy == 0:
                        rd[(dx + 1) // 2] = jnp.zeros(rd.shape[1:], F32)
                    else:
                        rx[1 + dx, (dy + 1) // 2] = jnp.zeros(rx.shape[2:], F32)

    def ar_copy(cyc, i):
        if i < 7:
            d, s, t = ring(i + 1, 0), arbuf.at[cyc, 0], arr1.at[cyc, i]
        else:
            d, s, t = ring(0, i - 6), arbuf.at[cyc, 1], arr2.at[cyc, i - 7]
        return pltpu.make_async_remote_copy(
            src_ref=s, dst_ref=t, send_sem=s_ar.at[cyc, i], recv_sem=r_ar.at[cyc, i],
            device_id=d, device_id_type=MESH,
        )

    def ar_begin(cyc, rows):
        out = jnp.zeros((1, 128), F32)
        for k, acc in enumerate(rows):
            acc = jnp.sum(jnp.where(own8, acc, 0.0), axis=0, keepdims=True)
            out = jnp.where(lane8[:1] == k, jnp.sum(acc, axis=1, keepdims=True), out)
        arbuf[cyc, 0] = out
        for i in range(7):
            ar_copy(cyc, i).start()

    def ar_middle(cyc):
        total = arbuf[cyc, 0]
        for i in range(7):
            ar_copy(cyc, i).wait_recv()
        for i in range(7):
            total = total + arr1[cyc, i]
        arbuf[cyc, 1] = total
        for i in range(7, 22):
            ar_copy(cyc, i).start()
        if cyc == 1:
            for i in range(7):
                ar_copy(cyc, i).wait_send()

    def ar_end(cyc, count):
        total = arbuf[cyc, 1]
        for i in range(7, 22):
            ar_copy(cyc, i).wait_recv()
        for i in range(15):
            total = total + arr2[cyc, i]
        return [jnp.broadcast_to(total[:, k : k + 1], (8, 128)) for k in range(count)]

    def stencil0(src, r, count, put):
        rows = [
            [src[pl.ds(vrow(t, r + k - 1), 16), :] for k in range(count + 2)] for t in (0, 1)
        ]
        for k in range(count):
            even, odd = rows[0][k + 1], rows[1][k + 1]
            beside = (odd + pltpu.roll(odd, 1, 1), even + pltpu.roll(even, 127, 1))
            for t in (0, 1):
                at_row = vrow(t, r + k)
                c = rows[t][k + 1]
                depth = [
                    c[8:] + src[pl.ds(at_row + 9, 8), :],
                    c[:8] + src[pl.ds(at_row - 1, 8), :],
                ]
                n = rows[t][k] + rows[t][k + 2]
                n = n + jnp.concatenate(depth, axis=0)
                put(k, t, c, n + beside[t])

    def sweep0(src, dst, bref, r0, count, per):
        def body(i, carry):
            r = r0 + per * i

            def put(k, t, c, n):
                row = pl.ds(brow(t, r + k), 16)
                dst[pl.ds(vrow(t, r + k), 16), :] = 0.2 * c + gain[row, :] * (bref[0, row, :] + n)

            stencil0(src, r, per, put)
            return carry

        lax.fori_loop(0, count // per, body, 0)

    def folded(x):
        return 0.125 * (x[:8] + x[8:])

    def wrow(r):
        return pl.multiple_of(8 + r * 16, 8)

    def stencil1(src, r, count, put):
        rows = [src[pl.ds(wrow(r + k - 1), 8), :] for k in range(count + 2)]
        for k in range(count):
            c = rows[k + 1]
            n = rows[k] + rows[k + 2]
            n = n + (src[pl.ds(wrow(r + k) - 1, 8), :] + src[pl.ds(wrow(r + k) + 1, 8), :])
            n = n + (pltpu.roll(c, 1, 1) + pltpu.roll(c, 127, 1))
            put(k, c, n)

    def sweep1(src, dst):
        def put(k, c, n):
            row = pl.ds((4 + k) * 8, 8)
            dst[pl.ds(wrow(4 + k + zero), 8), :] = 0.2 * c + l1g[row, :] * (l1b[row, :] + 0.5 * n)

        stencil1(src, 4 + zero, 24, put)

    def restrict1():
        parts = []
        for z in range(4):
            x = l1e[pl.ds(2 * z, 8, stride=16), :] + l1e[pl.ds(2 * z + 1, 8, stride=16), :]
            x = x + l1e[pl.ds(2 * z + 8, 8, stride=16), :] + l1e[pl.ds(2 * z + 9, 8, stride=16), :]
            parts.append(x)
        return dot_split(jnp.concatenate(parts, axis=1), t12[...])

    def base2(z, k):
        return z * 56 + 8 + 8 * k + zero

    def stencil2(src, z, k):
        c = src[pl.ds(base2(z, k), 8), :]
        n = src[pl.ds(base2(z, k) - 1, 8), :] + src[pl.ds(base2(z, k) + 1, 8), :]
        if z > 0:
            n = n + src[pl.ds(base2(z - 1, k), 8), :]
        if z < 3:
            n = n + src[pl.ds(base2(z + 1, k), 8), :]
        return c, n + (pltpu.roll(c, 1, 1) + pltpu.roll(c, 127, 1))

    def sweep2(src, dst, tiles):
        for z in range(4):
            for k in tiles:
                c, n = stencil2(src, z, k)
                row = pl.ds(z * 40 + 8 * k, 8)
                dst[pl.ds(base2(z, k), 8), :] = 0.2 * c + l2g[row, :] * (l2b[row, :] + 0.25 * n)

    def table(ref, rows, cols, value, f):
        ref[...] = jnp.where(f(iota((rows, cols), 0), iota((rows, cols), 1)), value, 0.0).astype(BF16)

    def prepare():
        tables()
        zeros()

    def tables():
        table(merge, 256, 128, 1.0, lambda i, o: ((i & 127) - 32 == o >> 1) & ((i >> 7) == (o & 1)))
        table(t12, 512, 128, 0.125, lambda i, o: (((i & 127) - 32) >> 1 == (o & 31)) & ((i >> 7) == (o >> 5)))
        table(t23, 128, 128, 0.125, lambda i, o: ((i - 48) >> 1) == o - 56)
        table(p32, 128, 128, 1.0, lambda i, o: ((o - 48) >> 1) == i - 56)
        table(p21, 128, 128, 1.0, lambda i, o: ((o - 32) >> 1) == i - 48)

    def zeros():
        def clear_pads(i, c):
            for ref in (va, vb, vc):
                ref[pl.ds(pl.multiple_of(i * PITCH, 8), 8), :] = z8
            return c

        lax.fori_loop(0, 2 * ROWS + 1, clear_pads, 0)
        for ref in (vb, vc):
            for t in (0, 1):
                for r in (0, 1, ROWS - 2, ROWS - 1):
                    ref[pl.ds(vrow(t, r), 16), :] = z16
        for ref in (l1v, l1w):
            ref[...] = jnp.zeros(ref.shape, F32)
        for ref in (l1s, l1g, l1b):
            ref[...] = jnp.zeros(ref.shape, F32)
        for ref in (l2v, l2w):
            ref[...] = jnp.zeros(ref.shape, F32)
        clear_r1(bs1, 2, rp1, rs1)
        clear_r1(b2, 1, rp2, rs2)
        clear_r2(rt1, rd1, rx1)
        clear_r2(rt2, rd2, rx2)

    table(split, 128, 256, 1.0, lambda i, o: ((o & 127) - 32 == i >> 1) & ((o >> 7) == (i & 1)))
    for load in loads:
        load.wait()
    stage("take_inputs", take_inputs)
    here = own_ref[0, ty]
    link_l = jnp.where(own_ref[0, jnp.maximum(ty - 1, 0)] == here, 1.0, 0.0)
    link_r = jnp.where(own_ref[0, jnp.minimum(ty + 1, NTY - 1)] == here, 1.0, 0.0)
    link = jnp.where(lane8 == 56, link_l, jnp.where(lane8 == 72, link_r, 1.0))

    bufs1 = (tb1, sd1, st1, rt1, rd1, rx1)
    bufs2 = (tb2, sd2, st2, rt2, rd2, rx2)

    def screen_sums(first, count, out, base):
        for i in range(first, first + count):
            even = bs1[1, pl.ds(brow(0, 4 + 2 * i), 32), :]
            odd = bs1[1, pl.ds(brow(1, 4 + 2 * i), 32), :]
            x = even + odd
            out[pl.ds((base + i) * 8, 8), :] = folded(x[:16] + x[16:])

    def put_tile(tb, a, x):
        tb[0, a] = pltpu.roll(x, 32, 1)
        tb[1, a] = x
        tb[2, a] = pltpu.roll(x, 96, 1)

    def own_screens():
        screen_sums(4, 16, l1e, -4)
        s2_own = restrict1()
        put_tile(tb1, 1, s2_own)
        for m in range(3):
            tb1[m, 2] = link
        rt1[2, 1, 1] = s2_own

    def vcycle(cyc, src, pk, rp, sl, rs, bufs, x, y):
        ns = 2 - cyc
        tb, sd, st, rt, rd, rx = bufs

        def screens1():
            screen_sums(0, 24, l1s, 4)
            s = l1s[...]
            l1g[...] = jnp.where(s > 0.0, 0.8 / (s + 3.0), 0.0)

        def defect0():
            per = 48

            def body(i, c):
                r = 4 + per * i
                held = []

                def put(k, t, centre, n):
                    row = pl.ds(brow(t, r + k), 16)
                    held.append(src[0, row, :] - (bs1[1, row, :] + 6.0) * centre + n)
                    if len(held) == 4:
                        at_row = pl.multiple_of((4 + i * (per // 2) + k // 2) * 8, 8)
                        l1b[pl.ds(at_row, 8), :] = folded((held[0] + held[1]) + (held[2] + held[3]))
                        held.clear()

                stencil0(x, r, per, put)
                return c

            lax.fori_loop(0, 48 // per, body, 0)

        def start1():
            for r in range(4, 28):
                row = pl.ds(r * 8, 8)
                l1v[pl.ds(wrow(r), 8), :] = l1g[row, :] * l1b[row, :]

        def defect1():
            def put(k, centre, n):
                row = pl.ds((8 + k) * 8, 8)
                l1e[pl.ds(k * 8, 8), :] = l1b[row, :] - (l1s[row, :] + 3.0) * centre + 0.5 * n

            stencil1(l1v, 8 + zero, 16, put)

        def pack1():
            for m in (0, 1):
                for k in range(5):
                    sd[m, k] = l1v[pl.ds(wrow(8 + k + 11 * m), 8), :]
            for j in (0, 1):
                left, right = z8, z8
                for g in range(8):
                    v = pltpu.roll(l1v[pl.ds(wrow(8 + 8 * j + g), 8), :], (16 * g - 80) % 128, 1)
                    right = jnp.where(grp8 == g, v, right)
                    left = jnp.where(grp8 == (g + 5) % 8, v, left)
                st[0, j] = left
                st[1, j] = right

        def down1():
            b2_own = restrict1()
            put_tile(tb, 0, b2_own)
            rt[2, 1, 0] = b2_own

        def unpack2():
            for a in range(ns):
                for z in range(4):
                    for k in range(5):
                        x = jnp.where(quarter == (z + 3) % 4, rt[k, 0, a], rt[k, 1, a])
                        x = jnp.where(quarter == (z + 1) % 4, rt[k, 2, a], x)
                        x = pltpu.roll(x, (48 - 32 * z) % 128, 1)
                        row = pl.ds(z * 40 + 8 * k, 8)
                        if a == 0:
                            l2b[row, :] = x
                        else:
                            l2s[row, :] = jnp.where((lane8 >= 16) & (lane8 < 112), x, 0.0)

        def screens3():
            s = l2s[...]
            l2g[...] = jnp.where(s > 0.0, 0.8 / (s + 1.5), 0.0)
            for z in range(2):
                l2e[pl.ds(z * 40, 40), :] = (
                    l2s[pl.ds(2 * z * 40, 40), :] + l2s[pl.ds((2 * z + 1) * 40, 40), :]
                )
            s = restrict2()
            l3g[...] = jnp.where(s > 0.0, 0.8 / (s + 0.75), 0.0)
            up, down = rt[1, 1, 2], rt[3, 1, 2]
            for k, m in enumerate((jnp.where(sub8 < 4, up, link), down)):
                l3m[0, k] = 0.125 * m
                l3m[1, k] = pltpu.roll(0.125 * m, 127, 1)

        def down2():
            for z in range(4):
                for k in range(5):
                    row = pl.ds(z * 40 + 8 * k, 8)
                    l2v[pl.ds(base2(z, k), 8), :] = l2g[row, :] * l2b[row, :]
            sweep2(l2v, l2w, range(5))
            sweep2(l2w, l2v, range(5))
            for k in range(5):
                d = []
                for z in range(4):
                    c, n = stencil2(l2v, z, k)
                    row = pl.ds(z * 40 + 8 * k, 8)
                    d.append(l2b[row, :] - (l2s[row, :] + 1.5) * c + 0.25 * n)
                l2e[pl.ds(8 * k, 8), :] = d[0] + d[1]
                l2e[pl.ds(40 + 8 * k, 8), :] = d[2] + d[3]

        def up2():
            for z in range(4):
                for k in (1, 2, 3):
                    row = pl.ds(base2(z, k), 8)
                    l2v[row, :] = l2v[row, :] + l2x[pl.ds((z // 2) * 32 + 8 * (k - 1), 8), :]
            sweep2(l2v, l2w, (1, 2, 3))
            sweep2(l2w, l2v, (1, 2, 3))
            sweep2(l2v, l2w, (1, 2, 3))
            e2 = jnp.concatenate([l2w[pl.ds(z * 56 + 20 + zero, 16), :] for z in range(4)], axis=0)
            e2 = dot_split(e2, p21[...])
            for z in range(4):
                for a in (0, 8):
                    for b in (0, 1):
                        l1x[pl.ds(a + 2 * z + b, 16, stride=16), :] = e2[16 * z : 16 * z + 16]

        def correct1():
            for r in range(3, 29):
                tile, inner = (r - 8) // 16, (r - 8) % 16
                j, g = inner // 8, inner % 8
                v = jnp.where(grp8 == g, rx[1 + tile, 0, j], rx[1 + tile, 1, j])
                v = pltpu.roll(v, (16 - 16 * g) % 128, 1)
                if tile == 0:
                    base = l1v[pl.ds(wrow(r), 8), :]
                elif tile < 0:
                    base = rd[0, inner - 11]
                else:
                    base = rd[1, inner]
                l1v[pl.ds(wrow(r), 8), :] = jnp.where(side8, v, base) + l1x[pl.ds(r * 8, 8), :]

        def correct0():
            def body(i, c):
                e = l1w[pl.ds(wrow(6 + i), 8), :]
                e = jnp.concatenate([e, e], axis=0)
                for t in (0, 1):
                    for k in (0, 1):
                        row = pl.ds(vrow(t, 8 + 2 * i + k), 16)
                        x[row, :] = x[row, :] + e
                return c

            lax.fori_loop(0, 20, body, 0, unroll=20)

        wait_r1(pk, rp, sl, rs, cyc)
        stage("unpack0", lambda: unpack0(src, ns, rp, rs, x))
        if cyc == 0:
            stage("screens1", screens1)
        stage("sweep0pre", lambda: sweep0(x, y, src, 2, 52, 52))
        sweep0(y, x, src, 3, 50, 50)
        stage("defect0", defect0)
        stage("start1", start1)
        stage("sweep1", lambda: sweep1(l1v, l1w))
        sweep1(l1w, l1v)
        stage("defect1", defect1)
        stage("down1", down1)
        each_r2("start", 0, bufs, cyc)
        stage("pack1", pack1)
        each_r2("start", 1, bufs, cyc)
        sent_r1(pk, rp, sl, rs, cyc)
        if cyc == 1:
            merged(0, vb, vrow)
            merged(1, b2.at[0], brow)
            for part in (0, 1):
                each_r2("wait_send", part, bufs1, 0)
            for i in range(22):
                ar_copy(0, i).wait_send()
        each_r2("wait_recv", 0, bufs, cyc)
        stage("unpack2", unpack2)
        if cyc == 0:
            stage("screens3", screens3)
        stage("down2", down2)
        stage("solve3", lambda: solve3(restrict2()))
        stage("up2", up2)
        each_r2("wait_recv", 1, bufs, cyc)
        stage("correct1", correct1)
        sweep1(l1v, l1w)
        sweep1(l1w, l1v)
        sweep1(l1v, l1w)
        stage("correct0", correct0)
        stage("sweep0post", lambda: sweep0(x, y, src, 9, 38, 38))
        sweep0(y, x, src, 10, 36, 36)
        sweep0(x, y, src, 11, 34, 34)

    def restrict2():
        parts = [
            l2e[pl.ds(z * 40 + 8, 16, stride=2), :] + l2e[pl.ds(z * 40 + 9, 16, stride=2), :]
            for z in range(2)
        ]
        return dot_split(jnp.concatenate(parts, axis=0), t23[...])

    def solve3(b3):
        up_ok = jnp.where((sub8 & 3) != 0, 0.125, 0.0)
        down_ok = jnp.where((sub8 & 3) != 3, 0.125, 0.0)
        g = [[l3g[pl.ds(16 * z + 8 * k, 8), :] for k in (0, 1)] for z in (0, 1)]
        b = [[b3[16 * z + 8 * k : 16 * z + 8 * k + 8] for k in (0, 1)] for z in (0, 1)]
        ml, mr = [l3m[0, 0], l3m[0, 1]], [l3m[1, 0], l3m[1, 1]]
        v = [[g[z][k] * b[z][k] for k in (0, 1)] for z in (0, 1)]
        for counter in range(7):
            new = [[None, None], [None, None]]
            for z in (0, 1):
                for k in (0, 1):
                    c = v[z][k]
                    n = 0.125 * v[1 - z][k]
                    n = n + pltpu.roll(c, 1, 0) * up_ok + pltpu.roll(c, 7, 0) * down_ok
                    n = n + pltpu.roll(c, 1, 1) * ml[k] + pltpu.roll(c, 127, 1) * mr[k]
                    new[z][k] = 0.2 * c + g[z][k] * (b[z][k] + n)
            v = new
        e3 = jnp.concatenate([v[0][0], v[0][1], v[1][0], v[1][1]], axis=0)
        e3 = dot_split(e3, p32[...])
        for z in (0, 1):
            for a in (0, 1):
                l2x[pl.ds(z * 32 + a, 16, stride=2), :] = e3[16 * z : 16 * z + 16]

    stage("pack0x2", lambda: pack0(bs1, 2, pk1, sl1))
    pl.semaphore_wait(barrier, expected)
    start_r1(pk1, rp1, sl1, rs1, 0)
    stage("prepare", prepare)
    stage("own_screens", own_screens)

    def merged(i, planes, start):
        def body(j, c):
            rows = []
            for k in range(16):
                r = TOP + 16 * j + k
                rows.append(jnp.concatenate([planes[pl.ds(start(t, r), 16), :] for t in (0, 1)], axis=1))
            x = dot_exact(jnp.concatenate(rows, axis=0), merge[...])
            for k in range(16):
                r = 16 * j + k
                natural[i, pl.ds(r + 32, 8, stride=64), :] = x[16 * k : 16 * k + 8]
                natural[i, pl.ds(r, 8, stride=64), :] = x[16 * k + 8 : 16 * k + 16]
            return c

        lax.fori_loop(0, 2, body, 0)

    vcycle(0, bs1, pk1, rp1, sl1, rs1, bufs1, va, vb)

    def halves(a):
        return a[0:8] + a[8:16]

    def apply_first(i, acc):
        r = TOP + 32 * i
        acc = list(acc)

        def put(k, t, c, n):
            row = pl.ds(brow(t, r + k), 16)
            q = (bs1[1, row, :] + 6.0) * c - n
            b2[0, row, :] = q
            acc[0] = acc[0] + halves(bs1[0, row, :] * c)
            acc[1] = acc[1] + halves(c * q)

        stencil0(vb, r, 32, put)
        return tuple(acc)

    sums = lax.fori_loop(0, 1, apply_first, (z8, z8))
    stage("pack0x1", lambda: pack0(b2, 1, pk2, sl2))
    start_r1(pk2, rp2, sl2, rs2, 1)
    ar_begin(0, sums)
    ar_middle(0)

    vcycle(1, b2, pk2, rp2, sl2, rs2, bufs2, va, vc)
    rho0, curv0 = ar_end(0, 2)
    step0 = rho0 / curv0
    step0_16 = jnp.concatenate([step0, step0], axis=0)

    def next_z(i, c):
        for k in (0, 1):
            for t in (0, 1):
                row = pl.ds(vrow(t, TOP - 2 + 2 * i + k), 16)
                vc[row, :] = vb[row, :] - step0_16 * vc[row, :]
        return c

    lax.fori_loop(0, 18, next_z, 0, unroll=18)

    def apply_second(i, acc):
        r = TOP + 32 * i
        acc = list(acc)

        def put(k, t, c, n):
            row = pl.ds(brow(t, r + k), 16)
            q = (bs1[1, row, :] + 6.0) * c - n
            q1[row, :] = q
            q0 = b2[0, row, :]
            z0 = vb[pl.ds(vrow(t, r + k), 16), :]
            acc[0] = acc[0] + halves((bs1[0, row, :] - step0_16 * q0) * c)
            acc[1] = acc[1] + halves(c * q)
            acc[2] = acc[2] + halves(c * q0 + z0 * q)

        stencil0(vc, r, 32, put)
        return tuple(acc)

    sums = lax.fori_loop(0, 1, apply_second, (z8, z8, z8))
    ar_begin(1, sums)
    merged(2, vc, vrow)
    merged(3, q1, brow)
    ar_middle(1)
    rho1, zz, cross = ar_end(1, 3)
    beta = rho1 / rho0
    curv1 = zz + beta * (cross + beta * curv0)
    step1 = rho1 / curv1
    mixed = step0 + step1 * beta

    for k in range(0, 512, 8):
        row = pl.ds(k, 8)
        out_ref[0, row, :] = mixed * natural[0, row, :] + step1 * natural[2, row, :]
        out_ref[1, row, :] = rhs_ref[row, :] - mixed * natural[1, row, :] - step1 * natural[3, row, :]

    for part in (0, 1):
        each_r2("wait_send", part, bufs2, 1)
    for i in range(7, 22):
        ar_copy(1, i).wait_send()


def on_device(right_side, screening, owners):
    vm = lambda *s: pltpu.VMEM(s, F32)
    bm = lambda *s: pltpu.VMEM(s, BF16)
    padded = 8 + 2 * ROWS * PITCH + 8
    scratch = [
        vm(512, 128), vm(512, 128), pltpu.SMEM(owners.shape, jnp.int32),
        pltpu.SemaphoreType.DMA((3,)),
        vm(2, 2 * PLANE, 128), vm(1, 2 * PLANE, 128), vm(2 * PLANE, 128),
        vm(padded, 128), vm(padded, 128), vm(padded, 128), vm(2 * PLANE, 128),
        vm(2, 2, 64, 128), vm(2, 1, 64, 128), vm(3, 2, 2, 64, 128), vm(3, 2, 1, 64, 128),
        vm(2, 2, HALO * 16, 128), vm(2, 1, HALO * 16, 128), vm(2, 2, HALO * 16, 128), vm(2, 1, HALO * 16, 128),
        vm(4, 512, 128),
        vm(R1 * 8, 128), vm(R1 * 8, 128), vm(R1 * 8, 128), vm(R1 * 8, 128),
        vm(R1 * 16 + 16, 128), vm(R1 * 16 + 16, 128), vm(128, 128),
        vm(3, 3, 8, 128), vm(3, 1, 8, 128), vm(2, 5, 8, 128), vm(2, 5, 8, 128), vm(2, 2, 8, 128), vm(2, 2, 8, 128),
        vm(5, 3, 3, 8, 128), vm(5, 3, 1, 8, 128), vm(2, 5, 8, 128), vm(2, 5, 8, 128),
        vm(3, 2, 2, 8, 128), vm(3, 2, 2, 8, 128),
        vm(160, 128), vm(160, 128), vm(160, 128), vm(4 * 56, 128), vm(4 * 56, 128),
        vm(80, 128), vm(64, 128), vm(32, 128), vm(2, 2, 8, 128),
        bm(128, 256), bm(256, 128), bm(512, 128), bm(128, 128), bm(128, 128), bm(128, 128),
        vm(2, 2, 1, 128), vm(2, 7, 1, 128), vm(2, 15, 1, 128),
        pltpu.SemaphoreType.DMA((2, 8)), pltpu.SemaphoreType.DMA((2, 8)),
        pltpu.SemaphoreType.DMA((2, 22)), pltpu.SemaphoreType.DMA((2, 22)),
        pltpu.SemaphoreType.DMA((2, 22)), pltpu.SemaphoreType.DMA((2, 22)),
    ]
    vmem = pl.BlockSpec(memory_space=pltpu.VMEM)
    hbm = lambda x: pltpu.with_memory_space_constraint(x, pltpu.HBM)
    out = pl.pallas_call(
        kernel,
        out_shape=pltpu.VMEM((2, 512, 128), F32),
        in_specs=[pl.BlockSpec(memory_space=pltpu.HBM)] * 3,
        out_specs=vmem,
        scratch_shapes=scratch,
        compiler_params=pltpu.CompilerParams(
            collective_id=0, has_side_effects=True, vmem_limit_bytes=40 * 2**20
        ),
    )(hbm(right_side.reshape(512, 128)), hbm(screening.reshape(512, 128)), hbm(owners))
    return out[0].reshape(right_side.shape), out[1].reshape(right_side.shape)


def solution(mesh):
    spec = P(None, "tx", "ty")
    return jax.shard_map(
        on_device, mesh=mesh, in_specs=(spec, spec, P("tx", None)), out_specs=(spec, spec),
        check_vma=False,
    )
```

```python
import functools

import jax
import jax.numpy as jnp
from jax import lax
from jax.experimental import pallas as pl
from jax.experimental.pallas import tpu as pltpu
from jax.sharding import PartitionSpec as P

MESH = pl.DeviceIdType.MESH
F32 = jnp.float32
BF16 = jnp.bfloat16

NTX, NTY = 8, 16
HALO = 11
ROWS = 56
TOP = 12
PLANE = ROWS * 16
PITCH = 24
R1 = 32
DIRS8 = [(-1, -1), (1, -1), (-1, 1), (1, 1), (0, -1), (0, 1), (-1, 0), (1, 0)]
DIRS14 = [(-2, -1), (2, -1), (-2, 1), (2, 1)] + DIRS8[:6] + [(-2, 0), (2, 0), (-1, 0), (1, 0)]


def iota(shape, axis):
    return lax.broadcasted_iota(jnp.int32, shape, axis)


def dot_split(x, table):
    high = x.astype(BF16).astype(F32)
    parts = jnp.concatenate([high, x - high], axis=0).astype(BF16)
    out = jnp.dot(parts, table, preferred_element_type=F32)
    return out[: x.shape[0]] + out[x.shape[0] :]


def dot_exact(x, table):
    high = x.astype(BF16).astype(F32)
    middle = (x - high).astype(BF16).astype(F32)
    parts = jnp.concatenate([high, middle, x - high - middle], axis=0).astype(BF16)
    out = jnp.dot(parts, table, preferred_element_type=F32)
    n = x.shape[0]
    return out[:n] + (out[n : 2 * n] + out[2 * n :])


def kernel(
    rhs_hbm, scr_hbm, own_hbm, out_ref,
    rhs_ref, scr_ref, own_ref, s_in,
    bs1, b2, gain, va, vb, vc, q1, pk1, pk2, rp1, rp2, sl1, sl2, rs1, rs2, natural,
    l1s, l1g, l1b, l1x, l1v, l1w, l1e,
    tb1, tb2, sd1, sd2, st1, st2, rt1, rt2, rd1, rd2, rx1, rx2,
    l2b, l2s, l2g, l2v, l2w, l2e, l2x, l3g, l3m,
    split, merge, t12, t23, p32, p21,
    arbuf, arr1, arr2,
    s_r1, r_r1, s_r2, r_r2, s_ar, r_ar,
):
    tx = lax.axis_index("tx")
    ty = lax.axis_index("ty")
    zero = lax.div(tx, 64)
    barrier = pltpu.get_barrier_semaphore()
    loads = [
        pltpu.make_async_copy(rhs_hbm, rhs_ref, s_in.at[0]),
        pltpu.make_async_copy(scr_hbm, scr_ref, s_in.at[1]),
        pltpu.make_async_copy(own_hbm, own_ref, s_in.at[2]),
    ]
    for load in loads:
        load.start()

    def inside(dx, dy):
        a, b = tx + dx, ty + dy
        return (a >= 0) & (a < NTX) & (b >= 0) & (b < NTY)

    def at(dx, dy):
        return {"tx": tx + dx, "ty": ty + dy}

    def ring(dx, dy):
        return {"tx": lax.rem(tx + dx, NTX), "ty": lax.rem(ty + dy, NTY)}

    ring_dirs = [(0, k) for k in range(1, NTY)] + [(k, 0) for k in range(1, NTX)]
    extra = [d for d in DIRS14 if d[0] != 0 and d[1] != 0]
    expected = jnp.int32(len(ring_dirs))
    for d in ring_dirs:
        pl.semaphore_signal(barrier, inc=1, device_id=ring(*d), device_id_type=MESH)
    for d in extra:
        ok = inside(*d)
        expected = expected + ok.astype(jnp.int32)

        @pl.when(ok)
        def _():
            pl.semaphore_signal(barrier, inc=1, device_id=at(*d), device_id_type=MESH)

    lane16 = iota((16, 128), 1)
    lane8 = iota((8, 128), 1)
    sub8 = iota((8, 128), 0)
    grp8 = lane8 >> 4
    quarter = lane8 >> 5
    own16 = (lane16 >= 32) & (lane16 < 96)
    own8 = (lane8 >= 32) & (lane8 < 96)

    def span16(first, count):
        return ((lane16 - first) & 127) < count

    side_even = span16(27, 5) | span16(96, 6)
    side_odd = span16(26, 6) | span16(96, 5)
    packed_rows = ((0, 11), (11, 10), (21, 11))
    side8 = ((lane8 >= 16) & (lane8 < 32)) | ((lane8 >= 96) & (lane8 < 112))
    z16 = jnp.zeros((16, 128), F32)
    z8 = jnp.zeros((8, 128), F32)

    def vrow(t, r):
        return pl.multiple_of(8 + (t * ROWS + r) * PITCH, 8)

    def brow(t, r):
        return pl.multiple_of((t * ROWS + r) * 16, 16)

    def stage(name, fn):
        fn()

    def take_inputs():
        for a, ref in enumerate((rhs_ref, scr_ref)):
            for i in range(2):
                x = [ref[pl.ds(16 * i + k + z, 8, stride=64), :] for k in range(16) for z in (32, 0)]
                x = dot_exact(jnp.concatenate(x, axis=0), split[...])
                for t in (0, 1):
                    at_row = (t * ROWS + TOP + 16 * i) * 16
                    bs1[a, pl.ds(at_row, 256), :] = x[:, 128 * t : 128 * t + 128]

    def pack0(src, count, pk):
        for j, (r0, rows) in enumerate(packed_rows):
            span = pl.ds(j * 16, 16)
            for a in range(count):
                left, right = z16, z16
                for g in range(rows):
                    even = src[a, pl.ds(brow(0, TOP + r0 + g), 16), :]
                    odd = src[a, pl.ds(brow(1, TOP + r0 + g), 16), :]
                    even = pltpu.roll(even, (11 * g - 91) % 128, 1)
                    odd = pltpu.roll(odd, (11 * g - 85) % 128, 1)
                    right = jnp.where(span16(11 * g, 5), even, jnp.where(span16(11 * g + 5, 6), odd, right))
                    left = jnp.where(span16(11 * g + 69, 6), even, jnp.where(span16(11 * g + 75, 5), odd, left))
                pk[0, a, span, :] = left
                pk[1, a, span, :] = right
    def pack_slabs(src, count, sl):
        for a in range(count):
            for m, first in ((0, TOP), (1, TOP + 32 - HALO)):
                for k in range(HALO):
                    even = src[a, pl.ds(brow(0, first + k), 16), :]
                    odd = src[a, pl.ds(brow(1, first + k), 16), :]
                    sl[m, a, pl.ds(16 * k, 16), :] = jnp.where(own16, even, pltpu.roll(odd, 64, 1))

    def unpack0(dst, count, rp, rs, x):
        def row(dxi, j, g):
            r = TOP + (dxi - 1) * 32 + packed_rows[j][0] + g
            span = pl.ds(j * 16, 16)
            out = []
            for a in range(count):
                fl, fr = rp[dxi, 0, a, span, :], rp[dxi, 1, a, span, :]
                if dxi == 1:
                    even, odd = dst[a, pl.ds(brow(0, r), 16), :], dst[a, pl.ds(brow(1, r), 16), :]
                else:
                    both = rs[dxi // 2, a, pl.ds(16 * g, 16), :]
                    even, odd = jnp.where(own16, both, 0.0), jnp.where(own16, pltpu.roll(both, 64, 1), 0.0)
                ve = pltpu.roll(jnp.where(span16(11 * g, 5), fl, fr), (27 - 11 * g) % 128, 1)
                vo = pltpu.roll(jnp.where(span16(11 * g + 5, 6), fl, fr), (21 - 11 * g) % 128, 1)
                even, odd = jnp.where(side_even, ve, even), jnp.where(side_odd, vo, odd)
                dst[a, pl.ds(brow(0, r), 16), :] = even
                dst[a, pl.ds(brow(1, r), 16), :] = odd
                out.append((even, odd))
            for t in (0, 1):
                at_row = pl.ds(brow(t, r), 16)
                if count == 2:
                    s = out[1][t]
                    gv = jnp.where(s > 0.0, 0.8 / (s + 6.0), 0.0)
                    gain[at_row, :] = gv
                else:
                    gv = gain[at_row, :]
                x[pl.ds(vrow(t, r), 16), :] = gv * out[0][t]

        for dxi, js in ((1, (0, 1, 2)), (0, (2,)), (2, (0,))):
            for j in js:
                for g in range(packed_rows[j][1]):
                    row(dxi, j, g)

    def r1_copy(i, d, pk, rp, sl, rs, cyc):
        dx, dy = d
        if dy == 0:
            s, t = sl.at[0 if dx == -1 else 1], rs.at[1 if dx == -1 else 0]
        else:
            side = 0 if dy == -1 else 1
            if dx == 0:
                s, t = pk.at[side], rp.at[1, 1 - side]
            elif dx == -1:
                s, t = pk.at[side, :, pl.ds(0, 16)], rp.at[2, 1 - side, :, pl.ds(0, 16)]
            else:
                s, t = pk.at[side, :, pl.ds(32, 16)], rp.at[0, 1 - side, :, pl.ds(32, 16)]
        return pltpu.make_async_remote_copy(
            src_ref=s, dst_ref=t, send_sem=s_r1.at[cyc, i], recv_sem=r_r1.at[cyc, i],
            device_id=at(*d), device_id_type=MESH,
        )

    def start_r1(pk, rp, sl, rs, cyc, slabs):
        for i, d in enumerate(DIRS8):
            if (d[1] == 0) != slabs:
                continue

            @pl.when(inside(*d))
            def _():
                r1_copy(i, d, pk, rp, sl, rs, cyc).start()

    def wait_r1(pk, rp, sl, rs, cyc):
        for i, d in enumerate(DIRS8):
            @pl.when(inside(-d[0], -d[1]))
            def _():
                r1_copy(i, d, pk, rp, sl, rs, cyc).wait_recv()

    def sent_r1(pk, rp, sl, rs, cyc):
        for i, d in enumerate(DIRS8):
            @pl.when(inside(*d))
            def _():
                r1_copy(i, d, pk, rp, sl, rs, cyc).wait_send()

    def clear_r1(src, count, rp, rs):
        for a in range(count):
            for t in (0, 1):
                for r in (0, ROWS - 1):
                    src[a, pl.ds(brow(t, r), 16), :] = z16
        for i, dx in ((0, -1), (1, 1)):
            @pl.when(jnp.logical_not(inside(dx, 0)))
            def _():
                rs[i] = jnp.zeros((count, HALO * 16, 128), F32)
        for dxi in range(3):
            for sidei, dy in ((0, -1), (1, 1)):
                @pl.when(jnp.logical_not(inside(dxi - 1, dy)))
                def _():
                    rp[dxi, sidei] = jnp.zeros((count, 48, 128), F32)

    def r2_copy(i, d, bufs, cyc):
        tb, sd, st, rt, rd, rx = bufs
        dx, dy = d
        if i < 14:
            n = 3 if cyc == 0 and abs(dx) == 1 and dy == 0 else 2 - cyc
            s, t = tb.at[1 + dy, pl.ds(0, n)], rt.at[2 - dx, 1 - dy, pl.ds(0, n)]
        elif dy == 0:
            s, t = sd.at[0 if dx < 0 else 1], rd.at[1 if dx < 0 else 0]
        else:
            side = 0 if dy < 0 else 1
            s, t = st.at[side], rx.at[1 - dx, 1 - side]
        return pltpu.make_async_remote_copy(
            src_ref=s, dst_ref=t, send_sem=s_r2.at[cyc, i], recv_sem=r_r2.at[cyc, i],
            device_id=at(*d), device_id_type=MESH,
        )

    def each_r2(op, part, bufs, cyc):
        for i, d in enumerate(DIRS14) if part == 0 else enumerate(DIRS8, 14):
            @pl.when(inside(-d[0], -d[1]) if op == "wait_recv" else inside(*d))
            def _():
                getattr(r2_copy(i, d, bufs, cyc), op)()

    def clear_r2(rt, rd, rx):
        for dx, dy in DIRS14:
            @pl.when(jnp.logical_not(inside(dx, dy)))
            def _():
                rt[2 + dx, 1 + dy] = jnp.zeros(rt.shape[2:], F32)
                if abs(dx) <= 1:
                    if dy == 0:
                        rd[(dx + 1) // 2] = jnp.zeros(rd.shape[1:], F32)
                    else:
                        rx[1 + dx, (dy + 1) // 2] = jnp.zeros(rx.shape[2:], F32)

    def ar_copy(cyc, i):
        if i < 7:
            d, s, t = ring(i + 1, 0), arbuf.at[cyc, 0], arr1.at[cyc, i]
        else:
            d, s, t = ring(0, i - 6), arbuf.at[cyc, 1], arr2.at[cyc, i - 7]
        return pltpu.make_async_remote_copy(
            src_ref=s, dst_ref=t, send_sem=s_ar.at[cyc, i], recv_sem=r_ar.at[cyc, i],
            device_id=d, device_id_type=MESH,
        )

    def ar_begin(cyc, rows):
        out = jnp.zeros((1, 128), F32)
        for k, acc in enumerate(rows):
            acc = jnp.sum(jnp.where(own8, acc, 0.0), axis=0, keepdims=True)
            out = jnp.where(lane8[:1] == k, jnp.sum(acc, axis=1, keepdims=True), out)
        arbuf[cyc, 0] = out
        for i in (3, 2, 4, 1, 5, 6, 0):
            ar_copy(cyc, i).start()

    def ar_middle(cyc):
        total = arbuf[cyc, 0]
        for i in range(7):
            ar_copy(cyc, i).wait_recv()
        for i in range(7):
            total = total + arr1[cyc, i]
        arbuf[cyc, 1] = total
        for k in (10, 6, 9, 11, 5, 7, 14, 2, 8, 13, 3, 12, 4, 15, 1):
            ar_copy(cyc, 6 + k).start()
        if cyc == 1:
            for i in range(7):
                ar_copy(cyc, i).wait_send()

    def ar_end(cyc, count):
        total = arbuf[cyc, 1]
        for i in range(7, 22):
            ar_copy(cyc, i).wait_recv()
        for i in range(15):
            total = total + arr2[cyc, i]
        return [jnp.broadcast_to(total[:, k : k + 1], (8, 128)) for k in range(count)]

    def stencil0(src, r, count, put):
        rows = [
            [src[pl.ds(vrow(t, r + k - 1), 16), :] for k in range(count + 2)] for t in (0, 1)
        ]
        for k in range(count):
            even, odd = rows[0][k + 1], rows[1][k + 1]
            beside = (odd + pltpu.roll(odd, 1, 1), even + pltpu.roll(even, 127, 1))
            for t in (0, 1):
                at_row = vrow(t, r + k)
                c = rows[t][k + 1]
                depth = [
                    c[8:] + src[pl.ds(at_row + 9, 8), :],
                    c[:8] + src[pl.ds(at_row - 1, 8), :],
                ]
                n = rows[t][k] + rows[t][k + 2]
                n = n + jnp.concatenate(depth, axis=0)
                put(k, t, c, n + beside[t])

    def sweep0(src, dst, bref, r0, count, per):
        def body(i, carry):
            r = r0 + per * i

            def put(k, t, c, n):
                row = pl.ds(brow(t, r + k), 16)
                dst[pl.ds(vrow(t, r + k), 16), :] = 0.2 * c + gain[row, :] * (bref[0, row, :] + n)

            stencil0(src, r, per, put)
            return carry

        lax.fori_loop(0, count // per, body, 0)

    def folded(x):
        return 0.125 * (x[:8] + x[8:])

    def wrow(r):
        return pl.multiple_of(8 + r * 16, 8)

    def stencil1(src, r, count, put):
        rows = [src[pl.ds(wrow(r + k - 1), 8), :] for k in range(count + 2)]
        for k in range(count):
            c = rows[k + 1]
            n = rows[k] + rows[k + 2]
            n = n + (src[pl.ds(wrow(r + k) - 1, 8), :] + src[pl.ds(wrow(r + k) + 1, 8), :])
            n = n + (pltpu.roll(c, 1, 1) + pltpu.roll(c, 127, 1))
            put(k, c, n)

    def sweep1(src, dst):
        def put(k, c, n):
            row = pl.ds((4 + k) * 8, 8)
            dst[pl.ds(wrow(4 + k + zero), 8), :] = 0.2 * c + l1g[row, :] * (l1b[row, :] + 0.5 * n)

        stencil1(src, 4 + zero, 24, put)

    def restrict1():
        parts = []
        for z in range(4):
            x = l1e[pl.ds(2 * z, 8, stride=16), :] + l1e[pl.ds(2 * z + 1, 8, stride=16), :]
            x = x + l1e[pl.ds(2 * z + 8, 8, stride=16), :] + l1e[pl.ds(2 * z + 9, 8, stride=16), :]
            parts.append(x)
        return dot_split(jnp.concatenate(parts, axis=1), t12[...])

    def base2(z, k):
        return z * 56 + 8 + 8 * k + zero

    def stencil2(src, z, k):
        c = src[pl.ds(base2(z, k), 8), :]
        n = src[pl.ds(base2(z, k) - 1, 8), :] + src[pl.ds(base2(z, k) + 1, 8), :]
        if z > 0:
            n = n + src[pl.ds(base2(z - 1, k), 8), :]
        if z < 3:
            n = n + src[pl.ds(base2(z + 1, k), 8), :]
        return c, n + (pltpu.roll(c, 1, 1) + pltpu.roll(c, 127, 1))

    def sweep2(src, dst, tiles):
        for z in range(4):
            for k in tiles:
                c, n = stencil2(src, z, k)
                row = pl.ds(z * 40 + 8 * k, 8)
                dst[pl.ds(base2(z, k), 8), :] = 0.2 * c + l2g[row, :] * (l2b[row, :] + 0.25 * n)

    def table(ref, rows, cols, value, f):
        ref[...] = jnp.where(f(iota((rows, cols), 0), iota((rows, cols), 1)), value, 0.0).astype(BF16)

    def prepare():
        tables()
        zeros()

    def tables():
        table(merge, 256, 128, 1.0, lambda i, o: ((i & 127) - 32 == o >> 1) & ((i >> 7) == (o & 1)))
        table(t12, 512, 128, 0.125, lambda i, o: (((i & 127) - 32) >> 1 == (o & 31)) & ((i >> 7) == (o >> 5)))
        table(t23, 128, 128, 0.125, lambda i, o: ((i - 48) >> 1) == o - 56)
        table(p32, 128, 128, 1.0, lambda i, o: ((o - 48) >> 1) == i - 56)
        table(p21, 128, 128, 1.0, lambda i, o: ((o - 32) >> 1) == i - 48)

    def zeros():
        def clear_pads(i, c):
            for ref in (va, vb, vc):
                ref[pl.ds(pl.multiple_of(i * PITCH, 8), 8), :] = z8
            return c

        lax.fori_loop(0, 2 * ROWS + 1, clear_pads, 0)
        for ref in (vb, vc):
            for t in (0, 1):
                for r in (0, 1, ROWS - 2, ROWS - 1):
                    ref[pl.ds(vrow(t, r), 16), :] = z16
        for ref in (l1v, l1w):
            ref[...] = jnp.zeros(ref.shape, F32)
        for ref in (l1s, l1g, l1b):
            ref[...] = jnp.zeros(ref.shape, F32)
        for ref in (l2v, l2w):
            ref[...] = jnp.zeros(ref.shape, F32)
        clear_r1(bs1, 2, rp1, rs1)
        clear_r1(b2, 1, rp2, rs2)
        clear_r2(rt1, rd1, rx1)
        clear_r2(rt2, rd2, rx2)

    table(split, 128, 256, 1.0, lambda i, o: ((o & 127) - 32 == i >> 1) & ((o >> 7) == (i & 1)))
    for load in loads:
        load.wait()
    stage("take_inputs", take_inputs)
    here = own_ref[0, ty]
    link_l = jnp.where(own_ref[0, jnp.maximum(ty - 1, 0)] == here, 1.0, 0.0)
    link_r = jnp.where(own_ref[0, jnp.minimum(ty + 1, NTY - 1)] == here, 1.0, 0.0)
    link = jnp.where(lane8 == 56, link_l, jnp.where(lane8 == 72, link_r, 1.0))

    bufs1 = (tb1, sd1, st1, rt1, rd1, rx1)
    bufs2 = (tb2, sd2, st2, rt2, rd2, rx2)

    def screen_sums(first, count, out, base):
        for i in range(first, first + count):
            even = bs1[1, pl.ds(brow(0, 4 + 2 * i), 32), :]
            odd = bs1[1, pl.ds(brow(1, 4 + 2 * i), 32), :]
            x = even + odd
            out[pl.ds((base + i) * 8, 8), :] = folded(x[:16] + x[16:])

    def put_tile(tb, a, x):
        tb[0, a] = pltpu.roll(x, 32, 1)
        tb[1, a] = x
        tb[2, a] = pltpu.roll(x, 96, 1)

    def own_screens():
        screen_sums(4, 16, l1e, -4)
        s2_own = restrict1()
        put_tile(tb1, 1, s2_own)
        tb1[1, 2] = link
        rt1[2, 1, 1] = s2_own

    def vcycle(cyc, src, pk, rp, sl, rs, bufs, x, y):
        ns = 2 - cyc
        tb, sd, st, rt, rd, rx = bufs

        def screens1():
            screen_sums(0, 24, l1s, 4)
            s = l1s[...]
            l1g[...] = jnp.where(s > 0.0, 0.8 / (s + 3.0), 0.0)

        def defect0():
            per = 48

            def body(i, c):
                r = 4 + per * i
                held = []

                def put(k, t, centre, n):
                    row = pl.ds(brow(t, r + k), 16)
                    held.append(src[0, row, :] - (bs1[1, row, :] + 6.0) * centre + n)
                    if len(held) == 4:
                        at_row = pl.multiple_of((4 + i * (per // 2) + k // 2) * 8, 8)
                        l1b[pl.ds(at_row, 8), :] = folded((held[0] + held[1]) + (held[2] + held[3]))
                        held.clear()

                stencil0(x, r, per, put)
                return c

            lax.fori_loop(0, 48 // per, body, 0)

        def start1():
            for r in range(4, 28):
                row = pl.ds(r * 8, 8)
                l1v[pl.ds(wrow(r), 8), :] = l1g[row, :] * l1b[row, :]

        def defect1():
            def put(k, centre, n):
                row = pl.ds((8 + k) * 8, 8)
                l1e[pl.ds(k * 8, 8), :] = l1b[row, :] - (l1s[row, :] + 3.0) * centre + 0.5 * n

            stencil1(l1v, 8 + zero, 16, put)

        def pack1():
            for m in (0, 1):
                for k in range(5):
                    sd[m, k] = l1v[pl.ds(wrow(8 + k + 11 * m), 8), :]
            for j in (0, 1):
                left, right = z8, z8
                for g in range(8):
                    v = pltpu.roll(l1v[pl.ds(wrow(8 + 8 * j + g), 8), :], (16 * g - 80) % 128, 1)
                    right = jnp.where(grp8 == g, v, right)
                    left = jnp.where(grp8 == (g + 5) % 8, v, left)
                st[0, j] = left
                st[1, j] = right

        def down1():
            b2_own = restrict1()
            put_tile(tb, 0, b2_own)
            rt[2, 1, 0] = b2_own

        def unpack2():
            for a in range(ns):
                for z in range(4):
                    for k in range(5):
                        x = jnp.where(quarter == (z + 3) % 4, rt[k, 0, a], rt[k, 1, a])
                        x = jnp.where(quarter == (z + 1) % 4, rt[k, 2, a], x)
                        x = pltpu.roll(x, (48 - 32 * z) % 128, 1)
                        row = pl.ds(z * 40 + 8 * k, 8)
                        if a == 0:
                            l2b[row, :] = x
                        else:
                            l2s[row, :] = jnp.where((lane8 >= 16) & (lane8 < 112), x, 0.0)

        def screens3():
            s = l2s[...]
            l2g[...] = jnp.where(s > 0.0, 0.8 / (s + 1.5), 0.0)
            for z in range(2):
                l2e[pl.ds(z * 40, 40), :] = (
                    l2s[pl.ds(2 * z * 40, 40), :] + l2s[pl.ds((2 * z + 1) * 40, 40), :]
                )
            s = restrict2()
            l3g[...] = jnp.where(s > 0.0, 0.8 / (s + 0.75), 0.0)
            up, down = rt[1, 1, 2], rt[3, 1, 2]
            for k, m in enumerate((jnp.where(sub8 < 4, up, link), down)):
                l3m[0, k] = 0.125 * m
                l3m[1, k] = pltpu.roll(0.125 * m, 127, 1)

        def down2():
            for z in range(4):
                for k in range(5):
                    row = pl.ds(z * 40 + 8 * k, 8)
                    l2v[pl.ds(base2(z, k), 8), :] = l2g[row, :] * l2b[row, :]
            sweep2(l2v, l2w, range(5))
            sweep2(l2w, l2v, range(5))
            for k in range(5):
                d = []
                for z in range(4):
                    c, n = stencil2(l2v, z, k)
                    row = pl.ds(z * 40 + 8 * k, 8)
                    d.append(l2b[row, :] - (l2s[row, :] + 1.5) * c + 0.25 * n)
                l2e[pl.ds(8 * k, 8), :] = d[0] + d[1]
                l2e[pl.ds(40 + 8 * k, 8), :] = d[2] + d[3]

        def up2():
            for z in range(4):
                for k in (1, 2, 3):
                    row = pl.ds(base2(z, k), 8)
                    l2v[row, :] = l2v[row, :] + l2x[pl.ds((z // 2) * 32 + 8 * (k - 1), 8), :]
            sweep2(l2v, l2w, (1, 2, 3))
            sweep2(l2w, l2v, (1, 2, 3))
            sweep2(l2v, l2w, (1, 2, 3))
            e2 = jnp.concatenate([l2w[pl.ds(z * 56 + 20 + zero, 16), :] for z in range(4)], axis=0)
            e2 = dot_split(e2, p21[...])
            for z in range(4):
                for a in (0, 8):
                    for b in (0, 1):
                        l1x[pl.ds(a + 2 * z + b, 16, stride=16), :] = e2[16 * z : 16 * z + 16]

        def correct1():
            for r in range(3, 29):
                tile, inner = (r - 8) // 16, (r - 8) % 16
                j, g = inner // 8, inner % 8
                v = jnp.where(grp8 == g, rx[1 + tile, 0, j], rx[1 + tile, 1, j])
                v = pltpu.roll(v, (16 - 16 * g) % 128, 1)
                if tile == 0:
                    base = l1v[pl.ds(wrow(r), 8), :]
                elif tile < 0:
                    base = rd[0, inner - 11]
                else:
                    base = rd[1, inner]
                l1v[pl.ds(wrow(r), 8), :] = jnp.where(side8, v, base) + l1x[pl.ds(r * 8, 8), :]

        def correct0():
            def body(i, c):
                e = l1w[pl.ds(wrow(6 + i), 8), :]
                e = jnp.concatenate([e, e], axis=0)
                for t in (0, 1):
                    for k in (0, 1):
                        row = pl.ds(vrow(t, 8 + 2 * i + k), 16)
                        x[row, :] = x[row, :] + e
                return c

            lax.fori_loop(0, 20, body, 0, unroll=20)

        wait_r1(pk, rp, sl, rs, cyc)
        stage("unpack0", lambda: unpack0(src, ns, rp, rs, x))
        if cyc == 0:
            stage("screens1", screens1)
        stage("sweep0pre", lambda: sweep0(x, y, src, 2, 52, 52))
        sweep0(y, x, src, 3, 50, 50)
        stage("defect0", defect0)
        stage("start1", start1)
        stage("sweep1", lambda: sweep1(l1v, l1w))
        sweep1(l1w, l1v)
        stage("defect1", defect1)
        stage("down1", down1)
        each_r2("start", 0, bufs, cyc)
        stage("pack1", pack1)
        each_r2("start", 1, bufs, cyc)
        sent_r1(pk, rp, sl, rs, cyc)
        if cyc == 1:
            merged(0, vb, vrow)
            merged(1, b2.at[0], brow)
            for part in (0, 1):
                each_r2("wait_send", part, bufs1, 0)
            for i in range(22):
                ar_copy(0, i).wait_send()
        each_r2("wait_recv", 0, bufs, cyc)
        stage("unpack2", unpack2)
        if cyc == 0:
            stage("screens3", screens3)
        stage("down2", down2)
        stage("solve3", lambda: solve3(restrict2()))
        stage("up2", up2)
        each_r2("wait_recv", 1, bufs, cyc)
        stage("correct1", correct1)
        sweep1(l1v, l1w)
        sweep1(l1w, l1v)
        sweep1(l1v, l1w)
        stage("correct0", correct0)
        stage("sweep0post", lambda: sweep0(x, y, src, 9, 38, 38))
        sweep0(y, x, src, 10, 36, 36)
        sweep0(x, y, src, 11, 34, 34)

    def restrict2():
        parts = [
            l2e[pl.ds(z * 40 + 8, 16, stride=2), :] + l2e[pl.ds(z * 40 + 9, 16, stride=2), :]
            for z in range(2)
        ]
        return dot_split(jnp.concatenate(parts, axis=0), t23[...])

    def solve3(b3):
        up_ok = jnp.where((sub8 & 3) != 0, 0.125, 0.0)
        down_ok = jnp.where((sub8 & 3) != 3, 0.125, 0.0)
        g = [[l3g[pl.ds(16 * z + 8 * k, 8), :] for k in (0, 1)] for z in (0, 1)]
        b = [[b3[16 * z + 8 * k : 16 * z + 8 * k + 8] for k in (0, 1)] for z in (0, 1)]
        ml, mr = [l3m[0, 0], l3m[0, 1]], [l3m[1, 0], l3m[1, 1]]
        v = [[g[z][k] * b[z][k] for k in (0, 1)] for z in (0, 1)]
        for counter in range(7):
            new = [[None, None], [None, None]]
            for z in (0, 1):
                for k in (0, 1):
                    c = v[z][k]
                    n = 0.125 * v[1 - z][k]
                    n = n + pltpu.roll(c, 1, 0) * up_ok + pltpu.roll(c, 7, 0) * down_ok
                    n = n + pltpu.roll(c, 1, 1) * ml[k] + pltpu.roll(c, 127, 1) * mr[k]
                    new[z][k] = 0.2 * c + g[z][k] * (b[z][k] + n)
            v = new
        e3 = jnp.concatenate([v[0][0], v[0][1], v[1][0], v[1][1]], axis=0)
        e3 = dot_split(e3, p32[...])
        for z in (0, 1):
            for a in (0, 1):
                l2x[pl.ds(z * 32 + a, 16, stride=2), :] = e3[16 * z : 16 * z + 16]

    pack0(bs1, 2, pk1)
    pack_slabs(bs1, 2, sl1)
    pl.semaphore_wait(barrier, expected)
    start_r1(pk1, rp1, sl1, rs1, 0, False)
    start_r1(pk1, rp1, sl1, rs1, 0, True)
    stage("prepare", prepare)
    stage("own_screens", own_screens)

    def merged(i, planes, start):
        def body(j, c):
            rows = []
            for k in range(16):
                r = TOP + 16 * j + k
                rows.append(jnp.concatenate([planes[pl.ds(start(t, r), 16), :] for t in (0, 1)], axis=1))
            x = dot_exact(jnp.concatenate(rows, axis=0), merge[...])
            for k in range(16):
                r = 16 * j + k
                natural[i, pl.ds(r + 32, 8, stride=64), :] = x[16 * k : 16 * k + 8]
                natural[i, pl.ds(r, 8, stride=64), :] = x[16 * k + 8 : 16 * k + 16]
            return c

        lax.fori_loop(0, 2, body, 0)

    vcycle(0, bs1, pk1, rp1, sl1, rs1, bufs1, va, vb)

    def halves(a):
        return a[0:8] + a[8:16]

    def apply_first(i, acc):
        r = TOP + 32 * i
        acc = list(acc)

        def put(k, t, c, n):
            row = pl.ds(brow(t, r + k), 16)
            q = (bs1[1, row, :] + 6.0) * c - n
            b2[0, row, :] = q
            acc[0] = acc[0] + halves(bs1[0, row, :] * c)
            acc[1] = acc[1] + halves(c * q)

        stencil0(vb, r, 32, put)
        return tuple(acc)

    sums = lax.fori_loop(0, 1, apply_first, (z8, z8))
    pack0(b2, 1, pk2)
    start_r1(pk2, rp2, sl2, rs2, 1, False)
    pack_slabs(b2, 1, sl2)
    start_r1(pk2, rp2, sl2, rs2, 1, True)
    ar_begin(0, sums)
    ar_middle(0)

    vcycle(1, b2, pk2, rp2, sl2, rs2, bufs2, va, vc)
    rho0, curv0 = ar_end(0, 2)
    step0 = rho0 / curv0
    step0_16 = jnp.concatenate([step0, step0], axis=0)

    def next_z(i, c):
        for k in (0, 1):
            for t in (0, 1):
                row = pl.ds(vrow(t, TOP - 2 + 2 * i + k), 16)
                vc[row, :] = vb[row, :] - step0_16 * vc[row, :]
        return c

    lax.fori_loop(0, 18, next_z, 0, unroll=18)

    def apply_second(i, acc):
        r = TOP + 32 * i
        acc = list(acc)

        def put(k, t, c, n):
            row = pl.ds(brow(t, r + k), 16)
            q = (bs1[1, row, :] + 6.0) * c - n
            q1[row, :] = q
            q0 = b2[0, row, :]
            z0 = vb[pl.ds(vrow(t, r + k), 16), :]
            acc[0] = acc[0] + halves((bs1[0, row, :] - step0_16 * q0) * c)
            acc[1] = acc[1] + halves(c * q)
            acc[2] = acc[2] + halves(c * q0 + z0 * q)

        stencil0(vc, r, 32, put)
        return tuple(acc)

    sums = lax.fori_loop(0, 1, apply_second, (z8, z8, z8))
    ar_begin(1, sums)
    merged(2, vc, vrow)
    merged(3, q1, brow)
    ar_middle(1)
    rho1, zz, cross = ar_end(1, 3)
    beta = rho1 / rho0
    curv1 = zz + beta * (cross + beta * curv0)
    step1 = rho1 / curv1
    mixed = step0 + step1 * beta

    for k in range(0, 512, 8):
        row = pl.ds(k, 8)
        out_ref[0, row, :] = mixed * natural[0, row, :] + step1 * natural[2, row, :]
        out_ref[1, row, :] = rhs_ref[row, :] - mixed * natural[1, row, :] - step1 * natural[3, row, :]

    for part in (0, 1):
        each_r2("wait_send", part, bufs2, 1)
    for i in range(7, 22):
        ar_copy(1, i).wait_send()


def on_device(right_side, screening, owners):
    vm = lambda *s: pltpu.VMEM(s, F32)
    bm = lambda *s: pltpu.VMEM(s, BF16)
    padded = 8 + 2 * ROWS * PITCH + 8
    scratch = [
        vm(512, 128), vm(512, 128), pltpu.SMEM(owners.shape, jnp.int32),
        pltpu.SemaphoreType.DMA((3,)),
        vm(2, 2 * PLANE, 128), vm(1, 2 * PLANE, 128), vm(2 * PLANE, 128),
        vm(padded, 128), vm(padded, 128), vm(padded, 128), vm(2 * PLANE, 128),
        vm(2, 2, 48, 128), vm(2, 1, 48, 128), vm(3, 2, 2, 48, 128), vm(3, 2, 1, 48, 128),
        vm(2, 2, HALO * 16, 128), vm(2, 1, HALO * 16, 128), vm(2, 2, HALO * 16, 128), vm(2, 1, HALO * 16, 128),
        vm(4, 512, 128),
        vm(R1 * 8, 128), vm(R1 * 8, 128), vm(R1 * 8, 128), vm(R1 * 8, 128),
        vm(R1 * 16 + 16, 128), vm(R1 * 16 + 16, 128), vm(128, 128),
        vm(3, 3, 8, 128), vm(3, 1, 8, 128), vm(2, 5, 8, 128), vm(2, 5, 8, 128), vm(2, 2, 8, 128), vm(2, 2, 8, 128),
        vm(5, 3, 3, 8, 128), vm(5, 3, 1, 8, 128), vm(2, 5, 8, 128), vm(2, 5, 8, 128),
        vm(3, 2, 2, 8, 128), vm(3, 2, 2, 8, 128),
        vm(160, 128), vm(160, 128), vm(160, 128), vm(4 * 56, 128), vm(4 * 56, 128),
        vm(80, 128), vm(64, 128), vm(32, 128), vm(2, 2, 8, 128),
        bm(128, 256), bm(256, 128), bm(512, 128), bm(128, 128), bm(128, 128), bm(128, 128),
        vm(2, 2, 1, 128), vm(2, 7, 1, 128), vm(2, 15, 1, 128),
        pltpu.SemaphoreType.DMA((2, 8)), pltpu.SemaphoreType.DMA((2, 8)),
        pltpu.SemaphoreType.DMA((2, 22)), pltpu.SemaphoreType.DMA((2, 22)),
        pltpu.SemaphoreType.DMA((2, 22)), pltpu.SemaphoreType.DMA((2, 22)),
    ]
    vmem = pl.BlockSpec(memory_space=pltpu.VMEM)
    hbm = lambda x: pltpu.with_memory_space_constraint(x, pltpu.HBM)
    out = pl.pallas_call(
        kernel,
        out_shape=pltpu.VMEM((2, 512, 128), F32),
        in_specs=[pl.BlockSpec(memory_space=pltpu.HBM)] * 3,
        out_specs=vmem,
        scratch_shapes=scratch,
        compiler_params=pltpu.CompilerParams(
            collective_id=0, has_side_effects=True, vmem_limit_bytes=40 * 2**20
        ),
    )(hbm(right_side.reshape(512, 128)), hbm(screening.reshape(512, 128)), hbm(owners))
    return out[0].reshape(right_side.shape), out[1].reshape(right_side.shape)


def solution(mesh):
    spec = P(None, "tx", "ty")
    return jax.shard_map(
        on_device, mesh=mesh, in_specs=(spec, spec, P("tx", None)), out_specs=(spec, spec),
        check_vma=False,
    )
```

```python
import functools

import jax
import jax.numpy as jnp
from jax import lax
from jax.experimental import pallas as pl
from jax.experimental.pallas import tpu as pltpu
from jax.sharding import PartitionSpec as P

MESH = pl.DeviceIdType.MESH
F32 = jnp.float32
BF16 = jnp.bfloat16

NTX, NTY = 8, 16
HALO = 11
ROWS = 56
TOP = 12
PLANE = ROWS * 16
PITCH = 24
R1 = 32
DIRS8 = [(-1, -1), (1, -1), (-1, 1), (1, 1), (0, -1), (0, 1), (-1, 0), (1, 0)]
DIRS14 = [(-2, -1), (2, -1), (-2, 1), (2, 1)] + DIRS8[:6] + [(-2, 0), (2, 0), (-1, 0), (1, 0)]


def iota(shape, axis):
    return lax.broadcasted_iota(jnp.int32, shape, axis)


def dot_split(x, table):
    high = x.astype(BF16).astype(F32)
    parts = jnp.concatenate([high, x - high], axis=0).astype(BF16)
    out = jnp.dot(parts, table, preferred_element_type=F32)
    return out[: x.shape[0]] + out[x.shape[0] :]


def dot_exact(x, table):
    high = x.astype(BF16).astype(F32)
    middle = (x - high).astype(BF16).astype(F32)
    parts = jnp.concatenate([high, middle, x - high - middle], axis=0).astype(BF16)
    out = jnp.dot(parts, table, preferred_element_type=F32)
    n = x.shape[0]
    return out[:n] + (out[n : 2 * n] + out[2 * n :])


def kernel(
    rhs_hbm, scr_hbm, own_hbm, out_ref,
    rhs_ref, scr_ref, own_ref, s_in,
    bs1, b2, gain, va, vb, vc, q1, pk1, pk2, rp1, rp2, sl1, sl2, rs1, rs2, natural,
    l1s, l1g, l1b, l1x, l1v, l1w, l1e,
    tb1, tb2, sd1, sd2, st1, st2, rt1, rt2, rd1, rd2, rx1, rx2,
    l2b, l2s, l2g, l2v, l2w, l2e, l2x, l3g, l3m,
    split, merge, t12, t23, p32, p21,
    arbuf, arr1, arr2,
    s_r1, r_r1, s_r2, r_r2, s_ar, r_ar,
):
    tx = lax.axis_index("tx")
    ty = lax.axis_index("ty")
    zero = lax.div(tx, 64)
    barrier = pltpu.get_barrier_semaphore()
    loads = [
        pltpu.make_async_copy(rhs_hbm, rhs_ref, s_in.at[0]),
        pltpu.make_async_copy(scr_hbm, scr_ref, s_in.at[1]),
        pltpu.make_async_copy(own_hbm, own_ref, s_in.at[2]),
    ]
    for load in loads:
        load.start()

    def inside(dx, dy):
        a, b = tx + dx, ty + dy
        return (a >= 0) & (a < NTX) & (b >= 0) & (b < NTY)

    def at(dx, dy):
        return {"tx": tx + dx, "ty": ty + dy}

    def ring(dx, dy):
        return {"tx": lax.rem(tx + dx, NTX), "ty": lax.rem(ty + dy, NTY)}

    ring_dirs = [(0, k) for k in range(1, NTY)] + [(k, 0) for k in range(1, NTX)]
    extra = [d for d in DIRS14 if d[0] != 0 and d[1] != 0]
    expected = jnp.int32(len(ring_dirs))
    for d in ring_dirs:
        pl.semaphore_signal(barrier, inc=1, device_id=ring(*d), device_id_type=MESH)
    for d in extra:
        ok = inside(*d)
        expected = expected + ok.astype(jnp.int32)

        @pl.when(ok)
        def _():
            pl.semaphore_signal(barrier, inc=1, device_id=at(*d), device_id_type=MESH)

    lane16 = iota((16, 128), 1)
    lane8 = iota((8, 128), 1)
    sub8 = iota((8, 128), 0)
    grp8 = lane8 >> 4
    quarter = lane8 >> 5
    own16 = (lane16 >= 32) & (lane16 < 96)
    own8 = (lane8 >= 32) & (lane8 < 96)

    def span16(first, count):
        return ((lane16 - first) & 127) < count

    side_even = span16(27, 5) | span16(96, 6)
    side_odd = span16(26, 6) | span16(96, 5)
    packed_rows = ((0, 11), (11, 10), (21, 11))
    side8 = ((lane8 >= 16) & (lane8 < 32)) | ((lane8 >= 96) & (lane8 < 112))
    z16 = jnp.zeros((16, 128), F32)
    z8 = jnp.zeros((8, 128), F32)

    def vrow(t, r):
        return pl.multiple_of(8 + (t * ROWS + r) * PITCH, 8)

    def brow(t, r):
        return pl.multiple_of((t * ROWS + r) * 16, 16)

    def stage(name, fn):
        fn()

    def take_inputs():
        for a, ref in enumerate((rhs_ref, scr_ref)):
            for i in range(2):
                x = [ref[pl.ds(16 * i + k + z, 8, stride=64), :] for k in range(16) for z in (32, 0)]
                x = dot_exact(jnp.concatenate(x, axis=0), split[...])
                for t in (0, 1):
                    at_row = (t * ROWS + TOP + 16 * i) * 16
                    bs1[a, pl.ds(at_row, 256), :] = x[:, 128 * t : 128 * t + 128]

    def pack0(src, count, pk):
        for j, (r0, rows) in enumerate(packed_rows):
            span = pl.ds(j * 16, 16)
            for a in range(count):
                left, right = z16, z16
                for g in range(rows):
                    even = src[a, pl.ds(brow(0, TOP + r0 + g), 16), :]
                    odd = src[a, pl.ds(brow(1, TOP + r0 + g), 16), :]
                    even = pltpu.roll(even, (11 * g - 91) % 128, 1)
                    odd = pltpu.roll(odd, (11 * g - 85) % 128, 1)
                    right = jnp.where(span16(11 * g, 5), even, jnp.where(span16(11 * g + 5, 6), odd, right))
                    left = jnp.where(span16(11 * g + 69, 6), even, jnp.where(span16(11 * g + 75, 5), odd, left))
                pk[0, a, span, :] = left
                pk[1, a, span, :] = right
    def pack_slabs(src, count, sl):
        for a in range(count):
            for m, first in ((0, TOP), (1, TOP + 32 - HALO)):
                for k in range(HALO):
                    even = src[a, pl.ds(brow(0, first + k), 16), :]
                    odd = src[a, pl.ds(brow(1, first + k), 16), :]
                    sl[m, a, pl.ds(16 * k, 16), :] = jnp.where(own16, even, pltpu.roll(odd, 64, 1))

    def unpack0(dst, count, rp, rs, x):
        def row(dxi, j, g):
            r = TOP + (dxi - 1) * 32 + packed_rows[j][0] + g
            span = pl.ds(j * 16, 16)
            out = []
            for a in range(count):
                fl, fr = rp[dxi, 0, a, span, :], rp[dxi, 1, a, span, :]
                if dxi == 1:
                    even, odd = dst[a, pl.ds(brow(0, r), 16), :], dst[a, pl.ds(brow(1, r), 16), :]
                else:
                    both = rs[dxi // 2, a, pl.ds(16 * g, 16), :]
                    even, odd = jnp.where(own16, both, 0.0), jnp.where(own16, pltpu.roll(both, 64, 1), 0.0)
                ve = pltpu.roll(jnp.where(span16(11 * g, 5), fl, fr), (27 - 11 * g) % 128, 1)
                vo = pltpu.roll(jnp.where(span16(11 * g + 5, 6), fl, fr), (21 - 11 * g) % 128, 1)
                even, odd = jnp.where(side_even, ve, even), jnp.where(side_odd, vo, odd)
                dst[a, pl.ds(brow(0, r), 16), :] = even
                dst[a, pl.ds(brow(1, r), 16), :] = odd
                out.append((even, odd))
            for t in (0, 1):
                at_row = pl.ds(brow(t, r), 16)
                if count == 2:
                    s = out[1][t]
                    gv = jnp.where(s > 0.0, 0.8 / (s + 6.0), 0.0)
                    gain[at_row, :] = gv
                else:
                    gv = gain[at_row, :]
                x[pl.ds(vrow(t, r), 16), :] = gv * out[0][t]

        for dxi, js in ((1, (0, 1, 2)), (0, (2,)), (2, (0,))):
            for j in js:
                for g in range(packed_rows[j][1]):
                    row(dxi, j, g)

    def r1_copy(i, d, pk, rp, sl, rs, cyc):
        dx, dy = d
        if dy == 0:
            s, t = sl.at[0 if dx == -1 else 1], rs.at[1 if dx == -1 else 0]
        else:
            side = 0 if dy == -1 else 1
            if dx == 0:
                s, t = pk.at[side], rp.at[1, 1 - side]
            elif dx == -1:
                s, t = pk.at[side, :, pl.ds(0, 16)], rp.at[2, 1 - side, :, pl.ds(0, 16)]
            else:
                s, t = pk.at[side, :, pl.ds(32, 16)], rp.at[0, 1 - side, :, pl.ds(32, 16)]
        return pltpu.make_async_remote_copy(
            src_ref=s, dst_ref=t, send_sem=s_r1.at[cyc, i], recv_sem=r_r1.at[cyc, i],
            device_id=at(*d), device_id_type=MESH,
        )

    def start_r1(pk, rp, sl, rs, cyc, slabs):
        for i, d in enumerate(DIRS8):
            if (d[1] == 0) != slabs:
                continue

            @pl.when(inside(*d))
            def _():
                r1_copy(i, d, pk, rp, sl, rs, cyc).start()

    def wait_r1(pk, rp, sl, rs, cyc):
        for i, d in enumerate(DIRS8):
            @pl.when(inside(-d[0], -d[1]))
            def _():
                r1_copy(i, d, pk, rp, sl, rs, cyc).wait_recv()

    def sent_r1(pk, rp, sl, rs, cyc):
        for i, d in enumerate(DIRS8):
            @pl.when(inside(*d))
            def _():
                r1_copy(i, d, pk, rp, sl, rs, cyc).wait_send()

    def clear_r1(src, count, rp, rs):
        for a in range(count):
            for t in (0, 1):
                for r in (0, ROWS - 1):
                    src[a, pl.ds(brow(t, r), 16), :] = z16
        for i, dx in ((0, -1), (1, 1)):
            @pl.when(jnp.logical_not(inside(dx, 0)))
            def _():
                rs[i] = jnp.zeros((count, HALO * 16, 128), F32)
        for dxi in range(3):
            for sidei, dy in ((0, -1), (1, 1)):
                @pl.when(jnp.logical_not(inside(dxi - 1, dy)))
                def _():
                    rp[dxi, sidei] = jnp.zeros((count, 48, 128), F32)

    def r2_copy(i, d, bufs, cyc):
        tb, sd, st, rt, rd, rx = bufs
        dx, dy = d
        if i < 14:
            n = 3 if cyc == 0 and abs(dx) == 1 and dy == 0 else 2 - cyc
            s, t = tb.at[1 + dy, pl.ds(0, n)], rt.at[2 - dx, 1 - dy, pl.ds(0, n)]
        elif dy == 0:
            s, t = sd.at[0 if dx < 0 else 1], rd.at[1 if dx < 0 else 0]
        else:
            side = 0 if dy < 0 else 1
            s, t = st.at[side], rx.at[1 - dx, 1 - side]
        return pltpu.make_async_remote_copy(
            src_ref=s, dst_ref=t, send_sem=s_r2.at[cyc, i], recv_sem=r_r2.at[cyc, i],
            device_id=at(*d), device_id_type=MESH,
        )

    def each_r2(op, part, bufs, cyc):
        for i, d in enumerate(DIRS14) if part == 0 else enumerate(DIRS8, 14):
            @pl.when(inside(-d[0], -d[1]) if op == "wait_recv" else inside(*d))
            def _():
                getattr(r2_copy(i, d, bufs, cyc), op)()

    def clear_r2(rt, rd, rx):
        for dx, dy in DIRS14:
            @pl.when(jnp.logical_not(inside(dx, dy)))
            def _():
                rt[2 + dx, 1 + dy] = jnp.zeros(rt.shape[2:], F32)
                if abs(dx) <= 1:
                    if dy == 0:
                        rd[(dx + 1) // 2] = jnp.zeros(rd.shape[1:], F32)
                    else:
                        rx[1 + dx, (dy + 1) // 2] = jnp.zeros(rx.shape[2:], F32)

    def ar_copy(cyc, i):
        if i < 7:
            d, s, t = ring(i + 1, 0), arbuf.at[cyc, 0], arr1.at[cyc, i]
        else:
            d, s, t = ring(0, i - 6), arbuf.at[cyc, 1], arr2.at[cyc, i - 7]
        return pltpu.make_async_remote_copy(
            src_ref=s, dst_ref=t, send_sem=s_ar.at[cyc, i], recv_sem=r_ar.at[cyc, i],
            device_id=d, device_id_type=MESH,
        )

    def ar_begin(cyc, rows):
        out = jnp.zeros((1, 128), F32)
        for k, acc in enumerate(rows):
            acc = jnp.sum(jnp.where(own8, acc, 0.0), axis=0, keepdims=True)
            out = jnp.where(lane8[:1] == k, jnp.sum(acc, axis=1, keepdims=True), out)
        arbuf[cyc, 0] = out
        for i in (3, 2, 4, 1, 5, 6, 0):
            ar_copy(cyc, i).start()

    def ar_middle(cyc):
        total = arbuf[cyc, 0]
        for i in range(7):
            ar_copy(cyc, i).wait_recv()
        for i in range(7):
            total = total + arr1[cyc, i]
        arbuf[cyc, 1] = total
        for k in (10, 6, 9, 11, 5, 7, 14, 2, 8, 13, 3, 12, 4, 15, 1):
            ar_copy(cyc, 6 + k).start()
        if cyc == 1:
            for i in range(7):
                ar_copy(cyc, i).wait_send()

    def ar_end(cyc, count):
        total = arbuf[cyc, 1]
        for i in range(7, 22):
            ar_copy(cyc, i).wait_recv()
        for i in range(15):
            total = total + arr2[cyc, i]
        return [jnp.broadcast_to(total[:, k : k + 1], (8, 128)) for k in range(count)]

    def stencil0(src, r, count, put):
        rows = [
            [src[pl.ds(vrow(t, r + k - 1), 16), :] for k in range(count + 2)] for t in (0, 1)
        ]
        for k in range(count):
            even, odd = rows[0][k + 1], rows[1][k + 1]
            beside = (odd + pltpu.roll(odd, 1, 1), even + pltpu.roll(even, 127, 1))
            for t in (0, 1):
                at_row = vrow(t, r + k)
                c = rows[t][k + 1]
                depth = [
                    c[8:] + src[pl.ds(at_row + 9, 8), :],
                    c[:8] + src[pl.ds(at_row - 1, 8), :],
                ]
                n = rows[t][k] + rows[t][k + 2]
                n = n + jnp.concatenate(depth, axis=0)
                put(k, t, c, n + beside[t])

    def sweep0(src, dst, bref, r0, count, per):
        def body(i, carry):
            r = r0 + per * i

            def put(k, t, c, n):
                row = pl.ds(brow(t, r + k), 16)
                dst[pl.ds(vrow(t, r + k), 16), :] = 0.2 * c + gain[row, :] * (bref[0, row, :] + n)

            stencil0(src, r, per, put)
            return carry

        lax.fori_loop(0, count // per, body, 0)

    def folded(x):
        return 0.125 * (x[:8] + x[8:])

    def wrow(r):
        return pl.multiple_of(8 + r * 16, 8)

    def stencil1(src, r, count, put):
        rows = [src[pl.ds(wrow(r + k - 1), 8), :] for k in range(count + 2)]
        for k in range(count):
            c = rows[k + 1]
            n = rows[k] + rows[k + 2]
            n = n + (src[pl.ds(wrow(r + k) - 1, 8), :] + src[pl.ds(wrow(r + k) + 1, 8), :])
            n = n + (pltpu.roll(c, 1, 1) + pltpu.roll(c, 127, 1))
            put(k, c, n)

    def sweep1(src, dst, first, count):
        def put(k, c, n):
            row = pl.ds((first + k) * 8, 8)
            dst[pl.ds(wrow(first + k + zero), 8), :] = 0.2 * c + l1g[row, :] * (l1b[row, :] + 0.5 * n)

        stencil1(src, first + zero, count, put)

    def restrict1():
        parts = []
        for z in range(4):
            x = l1e[pl.ds(2 * z, 8, stride=16), :] + l1e[pl.ds(2 * z + 1, 8, stride=16), :]
            x = x + l1e[pl.ds(2 * z + 8, 8, stride=16), :] + l1e[pl.ds(2 * z + 9, 8, stride=16), :]
            parts.append(x)
        return dot_split(jnp.concatenate(parts, axis=1), t12[...])

    def base2(z, k):
        return z * 56 + 8 + 8 * k + zero

    def stencil2(src, z, k):
        c = src[pl.ds(base2(z, k), 8), :]
        n = src[pl.ds(base2(z, k) - 1, 8), :] + src[pl.ds(base2(z, k) + 1, 8), :]
        if z > 0:
            n = n + src[pl.ds(base2(z - 1, k), 8), :]
        if z < 3:
            n = n + src[pl.ds(base2(z + 1, k), 8), :]
        return c, n + (pltpu.roll(c, 1, 1) + pltpu.roll(c, 127, 1))

    def sweep2(src, dst, tiles):
        for z in range(4):
            for k in tiles:
                c, n = stencil2(src, z, k)
                row = pl.ds(z * 40 + 8 * k, 8)
                dst[pl.ds(base2(z, k), 8), :] = 0.2 * c + l2g[row, :] * (l2b[row, :] + 0.25 * n)

    def table(ref, rows, cols, value, f):
        ref[...] = jnp.where(f(iota((rows, cols), 0), iota((rows, cols), 1)), value, 0.0).astype(BF16)

    def prepare():
        tables()
        zeros()

    def tables():
        table(merge, 256, 128, 1.0, lambda i, o: ((i & 127) - 32 == o >> 1) & ((i >> 7) == (o & 1)))
        table(t12, 512, 128, 0.125, lambda i, o: (((i & 127) - 32) >> 1 == (o & 31)) & ((i >> 7) == (o >> 5)))
        table(t23, 128, 128, 0.125, lambda i, o: ((i - 48) >> 1) == o - 56)
        table(p32, 128, 128, 1.0, lambda i, o: ((o - 48) >> 1) == i - 56)
        table(p21, 128, 128, 1.0, lambda i, o: ((o - 32) >> 1) == i - 48)

    def zeros():
        def clear_pads(i, c):
            for ref in (va, vb, vc):
                ref[pl.ds(pl.multiple_of(i * PITCH, 8), 8), :] = z8
            return c

        lax.fori_loop(0, 2 * ROWS + 1, clear_pads, 0)
        for ref in (vb, vc):
            for t in (0, 1):
                for r in (0, 1, ROWS - 2, ROWS - 1):
                    ref[pl.ds(vrow(t, r), 16), :] = z16
        for ref in (l1v, l1w):
            ref[...] = jnp.zeros(ref.shape, F32)
        for ref in (l1s, l1g, l1b):
            ref[...] = jnp.zeros(ref.shape, F32)
        for ref in (l2v, l2w):
            ref[...] = jnp.zeros(ref.shape, F32)
        clear_r1(bs1, 2, rp1, rs1)
        clear_r1(b2, 1, rp2, rs2)
        clear_r2(rt1, rd1, rx1)
        clear_r2(rt2, rd2, rx2)

    table(split, 128, 256, 1.0, lambda i, o: ((o & 127) - 32 == i >> 1) & ((o >> 7) == (i & 1)))
    for load in loads:
        load.wait()
    stage("take_inputs", take_inputs)
    here = own_ref[0, ty]
    link_l = jnp.where(own_ref[0, jnp.maximum(ty - 1, 0)] == here, 1.0, 0.0)
    link_r = jnp.where(own_ref[0, jnp.minimum(ty + 1, NTY - 1)] == here, 1.0, 0.0)
    link = jnp.where(lane8 == 56, link_l, jnp.where(lane8 == 72, link_r, 1.0))

    bufs1 = (tb1, sd1, st1, rt1, rd1, rx1)
    bufs2 = (tb2, sd2, st2, rt2, rd2, rx2)

    def screen_sums(first, count, out, base):
        for i in range(first, first + count):
            even = bs1[1, pl.ds(brow(0, 4 + 2 * i), 32), :]
            odd = bs1[1, pl.ds(brow(1, 4 + 2 * i), 32), :]
            x = even + odd
            out[pl.ds((base + i) * 8, 8), :] = folded(x[:16] + x[16:])

    def put_tile(tb, a, x):
        tb[0, a] = pltpu.roll(x, 32, 1)
        tb[1, a] = x
        tb[2, a] = pltpu.roll(x, 96, 1)

    def own_screens():
        screen_sums(4, 16, l1e, -4)
        s2_own = restrict1()
        put_tile(tb1, 1, s2_own)
        tb1[1, 2] = link
        rt1[2, 1, 1] = s2_own

    def vcycle(cyc, src, pk, rp, sl, rs, bufs, x, y):
        ns = 2 - cyc
        tb, sd, st, rt, rd, rx = bufs

        def screens1():
            screen_sums(0, 24, l1s, 4)
            s = l1s[...]
            l1g[...] = jnp.where(s > 0.0, 0.8 / (s + 3.0), 0.0)

        def defect0():
            per = 48

            def body(i, c):
                r = 4 + per * i
                held = []

                def put(k, t, centre, n):
                    row = pl.ds(brow(t, r + k), 16)
                    held.append(src[0, row, :] - (bs1[1, row, :] + 6.0) * centre + n)
                    if len(held) == 4:
                        at_row = pl.multiple_of((4 + i * (per // 2) + k // 2) * 8, 8)
                        l1b[pl.ds(at_row, 8), :] = folded((held[0] + held[1]) + (held[2] + held[3]))
                        held.clear()

                stencil0(x, r, per, put)
                return c

            lax.fori_loop(0, 48 // per, body, 0)

        def start1():
            for r in range(5, 27):
                row = pl.ds(r * 8, 8)
                l1v[pl.ds(wrow(r), 8), :] = l1g[row, :] * l1b[row, :]

        def defect1():
            def put(k, centre, n):
                row = pl.ds((8 + k) * 8, 8)
                l1e[pl.ds(k * 8, 8), :] = l1b[row, :] - (l1s[row, :] + 3.0) * centre + 0.5 * n

            stencil1(l1v, 8 + zero, 16, put)

        def pack1():
            for m in (0, 1):
                for k in range(5):
                    sd[m, k] = l1v[pl.ds(wrow(8 + k + 11 * m), 8), :]
            for j in (0, 1):
                left, right = z8, z8
                for g in range(8):
                    v = pltpu.roll(l1v[pl.ds(wrow(8 + 8 * j + g), 8), :], (16 * g - 80) % 128, 1)
                    right = jnp.where(grp8 == g, v, right)
                    left = jnp.where(grp8 == (g + 5) % 8, v, left)
                st[0, j] = left
                st[1, j] = right

        def down1():
            b2_own = restrict1()
            put_tile(tb, 0, b2_own)
            rt[2, 1, 0] = b2_own

        def unpack2():
            for a in range(ns):
                for z in range(4):
                    for k in range(5):
                        x = jnp.where(quarter == (z + 3) % 4, rt[k, 0, a], rt[k, 1, a])
                        x = jnp.where(quarter == (z + 1) % 4, rt[k, 2, a], x)
                        x = pltpu.roll(x, (48 - 32 * z) % 128, 1)
                        row = pl.ds(z * 40 + 8 * k, 8)
                        if a == 0:
                            l2b[row, :] = x
                        else:
                            l2s[row, :] = jnp.where((lane8 >= 16) & (lane8 < 112), x, 0.0)

        def screens3():
            s = l2s[...]
            l2g[...] = jnp.where(s > 0.0, 0.8 / (s + 1.5), 0.0)
            for z in range(2):
                l2e[pl.ds(z * 40, 40), :] = (
                    l2s[pl.ds(2 * z * 40, 40), :] + l2s[pl.ds((2 * z + 1) * 40, 40), :]
                )
            s = restrict2()
            l3g[...] = jnp.where(s > 0.0, 0.8 / (s + 0.75), 0.0)
            up, down = rt[1, 1, 2], rt[3, 1, 2]
            for k, m in enumerate((jnp.where(sub8 < 4, up, link), down)):
                l3m[0, k] = 0.125 * m
                l3m[1, k] = pltpu.roll(0.125 * m, 127, 1)

        def down2():
            for z in range(4):
                for k in range(5):
                    row = pl.ds(z * 40 + 8 * k, 8)
                    l2v[pl.ds(base2(z, k), 8), :] = l2g[row, :] * l2b[row, :]
            sweep2(l2v, l2w, range(5))
            sweep2(l2w, l2v, range(5))
            for k in range(5):
                d = []
                for z in range(4):
                    c, n = stencil2(l2v, z, k)
                    row = pl.ds(z * 40 + 8 * k, 8)
                    d.append(l2b[row, :] - (l2s[row, :] + 1.5) * c + 0.25 * n)
                l2e[pl.ds(8 * k, 8), :] = d[0] + d[1]
                l2e[pl.ds(40 + 8 * k, 8), :] = d[2] + d[3]

        def up2():
            for z in range(4):
                for k in (1, 2, 3):
                    row = pl.ds(base2(z, k), 8)
                    l2v[row, :] = l2v[row, :] + l2x[pl.ds((z // 2) * 32 + 8 * (k - 1), 8), :]
            sweep2(l2v, l2w, (1, 2, 3))
            sweep2(l2w, l2v, (1, 2, 3))
            sweep2(l2v, l2w, (1, 2, 3))
            e2 = jnp.concatenate([l2w[pl.ds(z * 56 + 20 + zero, 16), :] for z in range(4)], axis=0)
            e2 = dot_split(e2, p21[...])
            for z in range(4):
                for a in (0, 8):
                    for b in (0, 1):
                        l1x[pl.ds(a + 2 * z + b, 16, stride=16), :] = e2[16 * z : 16 * z + 16]

        def correct1():
            for r in range(3, 29):
                tile, inner = (r - 8) // 16, (r - 8) % 16
                j, g = inner // 8, inner % 8
                v = jnp.where(grp8 == g, rx[1 + tile, 0, j], rx[1 + tile, 1, j])
                v = pltpu.roll(v, (16 - 16 * g) % 128, 1)
                if tile == 0:
                    base = l1v[pl.ds(wrow(r), 8), :]
                elif tile < 0:
                    base = rd[0, inner - 11]
                else:
                    base = rd[1, inner]
                l1v[pl.ds(wrow(r), 8), :] = jnp.where(side8, v, base) + l1x[pl.ds(r * 8, 8), :]

        def correct0():
            def body(i, c):
                e = l1w[pl.ds(wrow(6 + i), 8), :]
                e = jnp.concatenate([e, e], axis=0)
                for t in (0, 1):
                    for k in (0, 1):
                        row = pl.ds(vrow(t, 8 + 2 * i + k), 16)
                        x[row, :] = x[row, :] + e
                return c

            lax.fori_loop(0, 20, body, 0, unroll=20)

        wait_r1(pk, rp, sl, rs, cyc)
        stage("unpack0", lambda: unpack0(src, ns, rp, rs, x))
        if cyc == 0:
            stage("screens1", screens1)
        stage("sweep0pre", lambda: sweep0(x, y, src, 2, 52, 52))
        sweep0(y, x, src, 3, 50, 50)
        stage("defect0", defect0)
        stage("start1", start1)
        sweep1(l1v, l1w, 6, 20)
        sweep1(l1w, l1v, 7, 18)
        stage("defect1", defect1)
        stage("down1", down1)
        each_r2("start", 0, bufs, cyc)
        stage("pack1", pack1)
        each_r2("start", 1, bufs, cyc)
        sent_r1(pk, rp, sl, rs, cyc)
        if cyc == 1:
            merged(0, vb, vrow)
            merged(1, b2.at[0], brow)
            for part in (0, 1):
                each_r2("wait_send", part, bufs1, 0)
            for i in range(22):
                ar_copy(0, i).wait_send()
        each_r2("wait_recv", 0, bufs, cyc)
        stage("unpack2", unpack2)
        if cyc == 0:
            stage("screens3", screens3)
        stage("down2", down2)
        stage("solve3", lambda: solve3(restrict2()))
        stage("up2", up2)
        each_r2("wait_recv", 1, bufs, cyc)
        stage("correct1", correct1)
        sweep1(l1v, l1w, 4, 24)
        sweep1(l1w, l1v, 5, 22)
        sweep1(l1v, l1w, 6, 20)
        stage("correct0", correct0)
        stage("sweep0post", lambda: sweep0(x, y, src, 9, 38, 38))
        sweep0(y, x, src, 10, 36, 36)
        sweep0(x, y, src, 11, 34, 34)

    def restrict2():
        parts = [
            l2e[pl.ds(z * 40 + 8, 16, stride=2), :] + l2e[pl.ds(z * 40 + 9, 16, stride=2), :]
            for z in range(2)
        ]
        return dot_split(jnp.concatenate(parts, axis=0), t23[...])

    def solve3(b3):
        up_ok = jnp.where((sub8 & 3) != 0, 0.125, 0.0)
        down_ok = jnp.where((sub8 & 3) != 3, 0.125, 0.0)
        g = [[l3g[pl.ds(16 * z + 8 * k, 8), :] for k in (0, 1)] for z in (0, 1)]
        b = [[b3[16 * z + 8 * k : 16 * z + 8 * k + 8] for k in (0, 1)] for z in (0, 1)]
        ml, mr = [l3m[0, 0], l3m[0, 1]], [l3m[1, 0], l3m[1, 1]]
        v = [[g[z][k] * b[z][k] for k in (0, 1)] for z in (0, 1)]
        for counter in range(7):
            new = [[None, None], [None, None]]
            for z in (0, 1):
                for k in (0, 1):
                    c = v[z][k]
                    n = 0.125 * v[1 - z][k]
                    n = n + pltpu.roll(c, 1, 0) * up_ok + pltpu.roll(c, 7, 0) * down_ok
                    n = n + pltpu.roll(c, 1, 1) * ml[k] + pltpu.roll(c, 127, 1) * mr[k]
                    new[z][k] = 0.2 * c + g[z][k] * (b[z][k] + n)
            v = new
        e3 = jnp.concatenate([v[0][0], v[0][1], v[1][0], v[1][1]], axis=0)
        e3 = dot_split(e3, p32[...])
        for z in (0, 1):
            for a in (0, 1):
                l2x[pl.ds(z * 32 + a, 16, stride=2), :] = e3[16 * z : 16 * z + 16]

    pack0(bs1, 2, pk1)
    pack_slabs(bs1, 2, sl1)
    pl.semaphore_wait(barrier, expected)
    start_r1(pk1, rp1, sl1, rs1, 0, False)
    start_r1(pk1, rp1, sl1, rs1, 0, True)
    stage("prepare", prepare)
    stage("own_screens", own_screens)

    def merged(i, planes, start):
        def body(j, c):
            rows = []
            for k in range(16):
                r = TOP + 16 * j + k
                rows.append(jnp.concatenate([planes[pl.ds(start(t, r), 16), :] for t in (0, 1)], axis=1))
            x = dot_exact(jnp.concatenate(rows, axis=0), merge[...])
            for k in range(16):
                r = 16 * j + k
                natural[i, pl.ds(r + 32, 8, stride=64), :] = x[16 * k : 16 * k + 8]
                natural[i, pl.ds(r, 8, stride=64), :] = x[16 * k + 8 : 16 * k + 16]
            return c

        lax.fori_loop(0, 2, body, 0)

    vcycle(0, bs1, pk1, rp1, sl1, rs1, bufs1, va, vb)

    def halves(a):
        return a[0:8] + a[8:16]

    def apply_first(i, acc):
        r = TOP + 32 * i
        acc = list(acc)

        def put(k, t, c, n):
            row = pl.ds(brow(t, r + k), 16)
            q = (bs1[1, row, :] + 6.0) * c - n
            b2[0, row, :] = q
            acc[0] = acc[0] + halves(bs1[0, row, :] * c)
            acc[1] = acc[1] + halves(c * q)

        stencil0(vb, r, 32, put)
        return tuple(acc)

    sums = lax.fori_loop(0, 1, apply_first, (z8, z8))
    pack0(b2, 1, pk2)
    start_r1(pk2, rp2, sl2, rs2, 1, False)
    pack_slabs(b2, 1, sl2)
    start_r1(pk2, rp2, sl2, rs2, 1, True)
    ar_begin(0, sums)
    ar_middle(0)

    vcycle(1, b2, pk2, rp2, sl2, rs2, bufs2, va, vc)
    rho0, curv0 = ar_end(0, 2)
    step0 = rho0 / curv0
    step0_16 = jnp.concatenate([step0, step0], axis=0)

    def next_z(i, c):
        for k in (0, 1):
            for t in (0, 1):
                row = pl.ds(vrow(t, TOP - 1 + 2 * i + k), 16)
                vc[row, :] = vb[row, :] - step0_16 * vc[row, :]
        return c

    lax.fori_loop(0, 17, next_z, 0, unroll=17)

    def apply_second(i, acc):
        r = TOP + 32 * i
        acc = list(acc)

        def put(k, t, c, n):
            row = pl.ds(brow(t, r + k), 16)
            q = (bs1[1, row, :] + 6.0) * c - n
            q1[row, :] = q
            q0 = b2[0, row, :]
            z0 = vb[pl.ds(vrow(t, r + k), 16), :]
            acc[0] = acc[0] + halves((bs1[0, row, :] - step0_16 * q0) * c)
            acc[1] = acc[1] + halves(c * q)
            acc[2] = acc[2] + halves(c * q0 + z0 * q)

        stencil0(vc, r, 32, put)
        return tuple(acc)

    sums = lax.fori_loop(0, 1, apply_second, (z8, z8, z8))
    ar_begin(1, sums)
    merged(2, vc, vrow)
    merged(3, q1, brow)
    ar_middle(1)
    rho1, zz, cross = ar_end(1, 3)
    beta = rho1 / rho0
    curv1 = zz + beta * (cross + beta * curv0)
    step1 = rho1 / curv1
    mixed = step0 + step1 * beta

    for k in range(0, 512, 8):
        row = pl.ds(k, 8)
        out_ref[0, row, :] = mixed * natural[0, row, :] + step1 * natural[2, row, :]
        out_ref[1, row, :] = rhs_ref[row, :] - mixed * natural[1, row, :] - step1 * natural[3, row, :]

    for part in (0, 1):
        each_r2("wait_send", part, bufs2, 1)
    for i in range(7, 22):
        ar_copy(1, i).wait_send()


def on_device(right_side, screening, owners):
    vm = lambda *s: pltpu.VMEM(s, F32)
    bm = lambda *s: pltpu.VMEM(s, BF16)
    padded = 8 + 2 * ROWS * PITCH + 8
    scratch = [
        vm(512, 128), vm(512, 128), pltpu.SMEM(owners.shape, jnp.int32),
        pltpu.SemaphoreType.DMA((3,)),
        vm(2, 2 * PLANE, 128), vm(1, 2 * PLANE, 128), vm(2 * PLANE, 128),
        vm(padded, 128), vm(padded, 128), vm(padded, 128), vm(2 * PLANE, 128),
        vm(2, 2, 48, 128), vm(2, 1, 48, 128), vm(3, 2, 2, 48, 128), vm(3, 2, 1, 48, 128),
        vm(2, 2, HALO * 16, 128), vm(2, 1, HALO * 16, 128), vm(2, 2, HALO * 16, 128), vm(2, 1, HALO * 16, 128),
        vm(4, 512, 128),
        vm(R1 * 8, 128), vm(R1 * 8, 128), vm(R1 * 8, 128), vm(R1 * 8, 128),
        vm(R1 * 16 + 16, 128), vm(R1 * 16 + 16, 128), vm(128, 128),
        vm(3, 3, 8, 128), vm(3, 1, 8, 128), vm(2, 5, 8, 128), vm(2, 5, 8, 128), vm(2, 2, 8, 128), vm(2, 2, 8, 128),
        vm(5, 3, 3, 8, 128), vm(5, 3, 1, 8, 128), vm(2, 5, 8, 128), vm(2, 5, 8, 128),
        vm(3, 2, 2, 8, 128), vm(3, 2, 2, 8, 128),
        vm(160, 128), vm(160, 128), vm(160, 128), vm(4 * 56, 128), vm(4 * 56, 128),
        vm(80, 128), vm(64, 128), vm(32, 128), vm(2, 2, 8, 128),
        bm(128, 256), bm(256, 128), bm(512, 128), bm(128, 128), bm(128, 128), bm(128, 128),
        vm(2, 2, 1, 128), vm(2, 7, 1, 128), vm(2, 15, 1, 128),
        pltpu.SemaphoreType.DMA((2, 8)), pltpu.SemaphoreType.DMA((2, 8)),
        pltpu.SemaphoreType.DMA((2, 22)), pltpu.SemaphoreType.DMA((2, 22)),
        pltpu.SemaphoreType.DMA((2, 22)), pltpu.SemaphoreType.DMA((2, 22)),
    ]
    vmem = pl.BlockSpec(memory_space=pltpu.VMEM)
    hbm = lambda x: pltpu.with_memory_space_constraint(x, pltpu.HBM)
    out = pl.pallas_call(
        kernel,
        out_shape=pltpu.VMEM((2, 512, 128), F32),
        in_specs=[pl.BlockSpec(memory_space=pltpu.HBM)] * 3,
        out_specs=vmem,
        scratch_shapes=scratch,
        compiler_params=pltpu.CompilerParams(
            collective_id=0, has_side_effects=True, vmem_limit_bytes=40 * 2**20
        ),
    )(hbm(right_side.reshape(512, 128)), hbm(screening.reshape(512, 128)), hbm(owners))
    return out[0].reshape(right_side.shape), out[1].reshape(right_side.shape)


def solution(mesh):
    spec = P(None, "tx", "ty")
    return jax.shard_map(
        on_device, mesh=mesh, in_specs=(spec, spec, P("tx", None)), out_specs=(spec, spec),
        check_vma=False,
    )
```
